32 devices in a mesh: ctx: 16 (over z, x, core), tp: 2 (over y).
Axes of the slice: x: 2, y: 2, z: 4, core: 2. Of those that a mesh axis runs over, the one named last changes fastest.
Arguments:
- stored: bfloat16 [2048, 4096], P('ctx', 'tp'), may hold values from -6 to 6
- source_owner: int32 [2048], P('ctx'), may hold values from 0 to 15, as said below
- doc_ids: int32 [2048], P('ctx'), may hold values from 0 to 12, as said below
- doc_starts: int32 [13], replicated, may hold values from 0 to 2040, as said below
- wq: bfloat16 [4096, 4096], P('ctx', 'tp'), may hold values from -1 to 1
- wk: bfloat16 [4096, 1024], P('ctx', 'tp'), may hold values from -1 to 1
- wv: bfloat16 [4096, 1024], P('ctx', 'tp'), may hold values from -0.09375 to 0.09375
Outputs:
- context: bfloat16 [2048, 4096], P('ctx', 'tp')
The draws below stay inside these ranges and needn't reach their ends.
Inputs may be any that keep to these rules, and one draw needn't show every extreme that they name: `source_owner`: every owner stores exactly 128 rows, taken in packed order; each packed shard of 128 rows takes at most 16 rows from any one owner, and exactly 16 from some owner. `doc_ids`: Nondecreasing; document k occupies positions doc_starts[k] up to the next document's start; one document has exactly 1280 tokens. Increasing, doc_starts[0] = 0, consistent with doc_ids.
All inputs are finite; a program needn't handle non-finite values.
Results may differ from the reference program's by a relative error of at most 0.0035.
The reference program's roundings to bfloat16 on the way (of `packed` and `queries`) count: a program that leaves them out, or rounds other values in their place, can miss the bound.
Values may be sent and summed in bfloat16 or wider, within the bound.
No kernel may reach another device: no remote copies, remote signals or barrier semaphores. Data moves between devices by JAX's collectives and lax.ppermute only.
A program may use at most 64 MiB of HBM per device.

```python
import math
import jax
import jax.numpy as jnp
from jax import lax

MODEL_WIDTH = 4096
QUERY_HEADS = 32
KEY_VALUE_HEADS = 8
HEAD_SIZE = 128
DOC_MEAN = 64
TOK_DEV = 128
WINDOW_TOKENS = 2048
MOST = 1280
NDOC = 13
N_CTX = 16


def draw_source_owner(key, part):
    mean = TOK_DEV // N_CTX
    key_spread, key_order, key_owner = jax.random.split(jax.random.fold_in(key, 11), 3)
    spread = jax.random.randint(key_spread, (N_CTX // 2,), 0, mean + 1).astype(jnp.int32)
    spread = spread.at[0].set(mean)
    amounts = jnp.concatenate([mean + spread, mean - spread]).astype(jnp.int32)
    shifts = jnp.repeat(jnp.arange(N_CTX, dtype=jnp.int32), amounts, total_repeat_length=TOK_DEV)
    block_keys = jax.random.split(key_order, N_CTX)

    def shuffle(block_key):
        return jax.random.permutation(block_key, shifts)
    shuffled = jax.vmap(shuffle)(block_keys)
    relabel = jax.random.permutation(key_owner, N_CTX).astype(jnp.int32)
    blocks = jnp.arange(N_CTX, dtype=jnp.int32)[:, None]
    return relabel[(blocks + shuffled) % N_CTX].reshape(WINDOW_TOKENS).astype(jnp.int32)


def document_plan(key):
    shorts = NDOC - 1
    key_spread, key_order = jax.random.split(jax.random.fold_in(key, 23))
    spread = jax.random.randint(key_spread, (shorts // 2,), 0, DOC_MEAN - 7).astype(jnp.int32)
    lengths = jnp.concatenate([jnp.full((1,), MOST, jnp.int32), DOC_MEAN + spread, DOC_MEAN - spread])
    lengths = lengths[jax.random.permutation(key_order, NDOC)]
    return (jnp.cumsum(lengths) - lengths).astype(jnp.int32)


def draw_doc_starts(key, part):
    return document_plan(key)


def draw_doc_ids(key, part):
    starts = document_plan(key)
    places = jnp.arange(WINDOW_TOKENS, dtype=jnp.int32)
    inside = (starts[None, :] <= places[:, None]).astype(jnp.int32)
    return (jnp.sum(inside, axis=1) - 1).astype(jnp.int32)


def projection_pair(key):
    key_query, key_from_keys = jax.random.split(jax.random.fold_in(key, 31))
    key_matrix = jax.random.normal(key_from_keys, (MODEL_WIDTH, KEY_VALUE_HEADS * HEAD_SIZE), jnp.float32) / math.sqrt(MODEL_WIDTH)
    noise = jax.random.normal(key_query, (MODEL_WIDTH, QUERY_HEADS * HEAD_SIZE), jnp.float32) / math.sqrt(MODEL_WIDTH)
    query_w = 3.0 * noise
    return (jnp.clip(query_w, -1.0, 1.0), jnp.clip(key_matrix, -1.0, 1.0))


def draw_wq(key, part):
    return projection_pair(key)[0].astype(jnp.bfloat16)


def draw_wk(key, part):
    return projection_pair(key)[1].astype(jnp.bfloat16)


def levels(own_key, extent, cuts, least, largest):
    gain, own = 1.0, jax.random.fold_in(own_key, 6)
    for axis_at, parts in cuts:
        steps = jnp.exp(jax.random.uniform(jax.random.fold_in(own, axis_at), (parts,), jnp.float32, least / len(cuts), largest / len(cuts)))
        gain = gain * jnp.repeat(steps, extent[axis_at] // parts).reshape([-1 if axis == axis_at else 1 for axis in range(len(extent))])
    return gain


def centred(own_key, dims, scale, bound, cuts=(), held_as=jnp.bfloat16):
    entries = scale * jax.random.normal(own_key, dims, jnp.float32)
    if cuts:
        entries = entries * levels(own_key, dims, cuts, -0.22, 0.18)
    return jnp.clip(entries, -bound, bound).astype(held_as)


def setup_inputs(seed: int = 0) -> dict:
    keys = jax.random.split(jax.random.key(seed), 8)
    stored = centred(keys[0], (WINDOW_TOKENS, MODEL_WIDTH), 1.0, 6.0, ((0, 16), (1, 2)))
    source_owner = draw_source_owner(jax.random.fold_in(keys[7], 71), 0)
    doc_ids = draw_doc_ids(jax.random.fold_in(keys[7], 71), 0)
    doc_starts = draw_doc_starts(jax.random.fold_in(keys[7], 71), 0)
    wq = draw_wq(jax.random.fold_in(keys[7], 71), 0)
    wk = draw_wk(jax.random.fold_in(keys[7], 71), 0)
    wv = centred(keys[6], (MODEL_WIDTH, KEY_VALUE_HEADS * HEAD_SIZE), MODEL_WIDTH ** -0.5, 0.09375, ((0, 16), (1, 2)))
    return {"stored": stored, "source_owner": source_owner, "doc_ids": doc_ids, "doc_starts": doc_starts, "wq": wq, "wk": wk, "wv": wv}


rope_base = 500000.0


def apply_rotary(value_rows, token_positions, heads):
    rows = value_rows.shape[0]
    size = value_rows.shape[1] // heads
    half = size // 2
    freqs = rope_base ** (-jnp.arange(half, dtype=jnp.float32) * 2.0 / size)
    angles = token_positions.astype(jnp.float32)[:, None] * freqs[None, :]
    cosine = jnp.cos(angles)[:, None, :]
    sine = jnp.sin(angles)[:, None, :]
    shaped = value_rows.reshape(rows, heads, size)
    first = shaped[..., :half]
    second = shaped[..., half:]
    joined = jnp.concatenate([first * cosine - second * sine, second * cosine + first * sine], axis=-1)
    return joined.reshape(rows, heads * size)


def reference(stored, source_owner, doc_ids, doc_starts, wq, wk, wv):
    owners_hot = (source_owner[:, None] == jnp.arange(N_CTX, dtype=jnp.int32)[None, :]).astype(jnp.int32)
    earlier = jnp.cumsum(owners_hot, axis=0).astype(jnp.int32) - owners_hot
    rank = jnp.sum(earlier * owners_hot, axis=1).astype(jnp.int32)
    packed = stored[(source_owner * TOK_DEV + rank).astype(jnp.int32)]
    queries_raw = jnp.dot(packed, wq, preferred_element_type=jnp.float32)
    unrotated_keys = jnp.dot(packed, wk, preferred_element_type=jnp.float32)
    values_raw = jnp.dot(packed, wv, preferred_element_type=jnp.float32)
    token_positions = (jnp.arange(WINDOW_TOKENS, dtype=jnp.int32) - doc_starts[doc_ids]).astype(jnp.int32)
    queries = apply_rotary(queries_raw, token_positions, QUERY_HEADS).astype(jnp.bfloat16)
    key_rows = apply_rotary(unrotated_keys, token_positions, KEY_VALUE_HEADS).astype(jnp.bfloat16)
    value_rows = values_raw.astype(jnp.bfloat16)
    query_group = QUERY_HEADS // KEY_VALUE_HEADS
    rows_per_block = 128
    scale = 1.0 / (HEAD_SIZE ** 0.5)
    every_key_row = key_rows.astype(jnp.float32).reshape(WINDOW_TOKENS, KEY_VALUE_HEADS, HEAD_SIZE)
    every_value_row = value_rows.astype(jnp.float32).reshape(WINDOW_TOKENS, KEY_VALUE_HEADS, HEAD_SIZE)

    def block(index):
        start = (index * rows_per_block).astype(jnp.int32)
        query_block = lax.dynamic_slice_in_dim(queries, start, rows_per_block, 0).astype(jnp.float32)
        query_block = query_block.reshape(rows_per_block, KEY_VALUE_HEADS, query_group, HEAD_SIZE)
        ids_blk = lax.dynamic_slice_in_dim(doc_ids, start, rows_per_block, 0)
        scores = jnp.einsum("qhgd,khd->hgqk", query_block, every_key_row) * scale
        same = (ids_blk[:, None] == doc_ids[None, :])[None, None]
        top = jnp.max(jnp.where(same, scores, -1e30), axis=-1)
        weights = jnp.where(same, jnp.exp(scores - top[..., None]), 0.0)
        total = jnp.sum(weights, axis=-1)
        rounded = lax.optimization_barrier(weights.astype(jnp.bfloat16)).astype(jnp.float32)
        mixed = jnp.einsum("hgqk,khd->qhgd", rounded, every_value_row)
        result = mixed / jnp.transpose(total, (2, 0, 1))[..., None]
        return result.reshape(rows_per_block, QUERY_HEADS * HEAD_SIZE).astype(jnp.bfloat16)

    blocks = lax.map(block, jnp.arange(WINDOW_TOKENS // rows_per_block, dtype=jnp.int32))
    return blocks.reshape(WINDOW_TOKENS, QUERY_HEADS * HEAD_SIZE)
```

```python
import functools

import jax
import jax.numpy as jnp
from jax import lax
from jax.experimental import pallas as pl
from jax.experimental.pallas import tpu as pltpu
from jax.sharding import PartitionSpec as P

HEAD_SIZE = 128
ROPE_BASE = 500000.0
VMEM_LIMIT = 48 * 1024 * 1024

VMEM_SPEC = pl.BlockSpec(memory_space=pltpu.VMEM)
SMEM_SPEC = pl.BlockSpec(memory_space=pltpu.SMEM)


def rotate(raw, cosine, sine):
    return raw * cosine + pltpu.roll(raw, HEAD_SIZE // 2, 1) * sine


def kv_kernel(layout, *refs):
    row_blocks, col_chunks, weight_parts, col_blocks = layout
    table = refs[0]
    pieces = refs[1 : 1 + row_blocks * col_chunks]
    at = 1 + row_blocks * col_chunks
    weights = refs[at : at + weight_parts]
    cosine, sine, tokens, kv, loose = refs[at + weight_parts :]
    piece_rows, piece_cols = pieces[0].shape
    for row in range(row_blocks):
        for col in range(col_chunks):
            loose[
                row * piece_rows : (row + 1) * piece_rows,
                col * piece_cols : (col + 1) * piece_cols,
            ] = pieces[row * col_chunks + col][...]
    width = loose.shape[1] // col_blocks
    for block in range(col_blocks):
        source = pl.ds(pl.multiple_of(table[block] * width, width), width)
        tokens[:, block * width : (block + 1) * width] = loose[:, source]
    total = project(tokens, weights)
    kv[:, :HEAD_SIZE] = rotate(total[:, :HEAD_SIZE], cosine[...], sine[...]).astype(kv.dtype)
    kv[:, HEAD_SIZE:] = total[:, HEAD_SIZE:].astype(kv.dtype)


def project(tokens, weights):
    total = None
    start = 0
    for weight in weights:
        depth = weight.shape[0]
        part = jnp.dot(
            tokens[:, start : start + depth], weight[...], preferred_element_type=jnp.float32
        )
        total = part if total is None else total + part
        start += depth
    return total


def attention_kernel(layout, *refs):
    weight_parts, kv_parts, block_rows = layout
    tokens = refs[0]
    weights = refs[1 : 1 + weight_parts]
    kvs = refs[1 + weight_parts : 1 + weight_parts + kv_parts]
    cosine, sine, query_start, key_start, slot_row, outgoing = refs[
        1 + weight_parts + kv_parts : 7 + weight_parts + kv_parts
    ]
    queries, scores, context = refs[7 + weight_parts + kv_parts :]
    rows = tokens.shape[0]
    heads = weights[0].shape[1] // HEAD_SIZE
    raw = project(tokens, weights)
    for head in range(heads):
        cols = slice(head * HEAD_SIZE, (head + 1) * HEAD_SIZE)
        queries[:, cols] = rotate(raw[:, cols], cosine[...], sine[...]).astype(queries.dtype)
    factor = 1.4426950408889634 / HEAD_SIZE**0.5
    for block in range(rows // block_rows):
        own = slice(block * block_rows, (block + 1) * block_rows)
        for head in range(heads):
            cols = slice(head * HEAD_SIZE, (head + 1) * HEAD_SIZE)
            start = 0
            for kv in kvs:
                count = kv.shape[0]
                part = lax.dot_general(
                    queries[own, cols],
                    kv[:, :HEAD_SIZE],
                    (((1,), (1,)), ((), ())),
                    preferred_element_type=jnp.float32,
                )
                same = query_start[own, :] == key_start[:, start : start + count]
                scores[:, start : start + count] = jnp.where(same, part, -1e30)
                start += count
            top = jnp.max(scores[...], axis=1, keepdims=True)
            total = jnp.zeros((block_rows, 1), jnp.float32)
            mixed = jnp.zeros((block_rows, HEAD_SIZE), jnp.float32)
            start = 0
            for kv in kvs:
                count = kv.shape[0]
                kept = jnp.exp2((scores[:, start : start + count] - top) * factor)
                total = total + jnp.sum(kept, axis=1, keepdims=True)
                mixed = mixed + jnp.dot(
                    kept.astype(jnp.bfloat16),
                    kv[:, HEAD_SIZE:],
                    preferred_element_type=jnp.float32,
                )
                start += count
            context[own, cols] = (mixed / total).astype(context.dtype)
    places = lax.broadcasted_iota(jnp.int32, (slot_row.shape[0], rows), 1)
    hot = jnp.where(places == slot_row[...], 1.0, 0.0).astype(jnp.bfloat16)
    outgoing[...] = jnp.dot(hot, context[...], preferred_element_type=jnp.float32).astype(
        outgoing.dtype
    )


def combine_kernel(groups, *refs):
    columns = refs[0]
    incoming = refs[1:-1]
    out = refs[-1]
    width = incoming[0].shape[1]
    span = incoming[0].shape[0] // groups
    places = lax.broadcasted_iota(jnp.int32, (out.shape[0], span), 1)
    for group in range(groups):
        hot = jnp.where(places == columns[:, group : group + 1], 1.0, 0.0).astype(jnp.bfloat16)
        for part, ref in enumerate(incoming):
            picked = jnp.dot(
                hot,
                ref[group * span : (group + 1) * span, :],
                preferred_element_type=jnp.float32,
            )
            start = (group * len(incoming) + part) * width
            out[:, start : start + width] = picked.astype(out.dtype)


def call(kernel, out_shape, operands, scratch=(), flops=0, smem_first=False):
    specs = [VMEM_SPEC] * len(operands)
    if smem_first:
        specs[0] = SMEM_SPEC
    many = isinstance(out_shape, (list, tuple))
    moved = sum(x.size * x.dtype.itemsize for x in operands)
    return pl.pallas_call(
        kernel,
        out_shape=out_shape,
        in_specs=specs,
        out_specs=[VMEM_SPEC] * len(out_shape) if many else VMEM_SPEC,
        scratch_shapes=list(scratch),
        compiler_params=pltpu.CompilerParams(vmem_limit_bytes=VMEM_LIMIT),
        cost_estimate=pl.CostEstimate(flops=flops, bytes_accessed=moved, transcendentals=0),
    )(*operands)


def swap(value, bits):
    count = lax.axis_size("ctx")
    return lax.ppermute(value, "ctx", [(i, i ^ bits) for i in range(count)])


def flip(value):
    return lax.ppermute(value, "tp", [(0, 1), (1, 0)])


def body(stored, source_owner, doc_ids, doc_starts, wq, wk, wv):
    nctx = lax.axis_size("ctx")
    ntp = lax.axis_size("tp")
    me = lax.axis_index("ctx")
    rows = stored.shape[0]
    cap = 2 * rows // nctx
    size = HEAD_SIZE
    depth = wq.shape[0]
    kvheads = wk.shape[1] // size
    query_group = wq.shape[1] // size // kvheads
    groups = kvheads
    team = nctx // groups
    group, mate = me // team, me % team
    split = groups > 1
    pair = 2 * size
    parts = query_group * size // pair

    owners = lax.all_to_all(
        jnp.broadcast_to(source_owner[None, :], (nctx, rows)), "ctx", 0, 0, tiled=True
    )
    owner_range = jnp.arange(nctx, dtype=jnp.int32)
    hot = (owners[:, :, None] == owner_range).astype(jnp.bfloat16)
    lower = (
        jnp.arange(rows)[:, None] > jnp.arange(rows)[None, :]
    ).astype(jnp.bfloat16)
    within = jnp.einsum("pq,sqo->spo", lower, hot, preferred_element_type=jnp.float32)
    counts = jnp.sum(hot.astype(jnp.float32), axis=1)
    before = jnp.cumsum(counts, axis=0) - counts
    rank = jnp.sum(hot.astype(jnp.float32) * (within + before[:, None, :]), axis=2)
    rank_hot = (rank[:, :, None] == jnp.arange(rows, dtype=jnp.float32)).astype(jnp.bfloat16)
    shard_no = jnp.arange(nctx, dtype=jnp.bfloat16)[:, None, None]
    place_no = jnp.arange(rows, dtype=jnp.bfloat16)[None, :, None]
    coded = jnp.concatenate([hot * shard_no, hot * place_no], axis=2)
    found = jnp.einsum("spo,spr->or", coded, rank_hot, preferred_element_type=jnp.float32)
    packed_at = (found[:nctx] * rows + found[nctx:]).astype(jnp.int32)
    start_of = jnp.max(
        jnp.where(doc_starts <= packed_at[:, :, None], doc_starts, 0), axis=2
    )
    before = before.astype(jnp.int32)

    if split:
        rel = jnp.arange(groups, dtype=jnp.int32)
        turns = jnp.array([0, 2, 1, 3], dtype=jnp.int32)
        order = ((group ^ rel)[None, :] * team + (mate ^ turns)[:, None]).reshape(-1)
        mine = (group ^ rel) * team + mate
        half = nctx // ntp
        table = order % half + jnp.where(order // half == lax.axis_index("tp"), 0, half)
        col_blocks = nctx
    else:
        order = owner_range
        mine = me[None]
        table = jnp.zeros((1,), jnp.int32)
        col_blocks = 1

    my_place = packed_at[mine].reshape(-1)
    my_start = start_of[mine].reshape(-1)
    key_start = start_of[order].reshape(1, -1)
    freqs = ROPE_BASE ** (-jnp.arange(size // 2, dtype=jnp.float32) * 2.0 / size)
    angles = (my_place - my_start).astype(jnp.float32)[:, None] * freqs[None, :]
    cosine = jnp.cos(angles)
    sine = jnp.sin(angles)
    cosine = jnp.concatenate([cosine, cosine], axis=1)
    sine = jnp.concatenate([-sine, sine], axis=1)

    weight_sets = [jnp.stack([wk.reshape(depth, groups, size), wv.reshape(depth, groups, size)], 2)]
    grid = wq.reshape(depth, groups, parts, pair)
    weight_sets += [grid[:, :, part] for part in range(parts)]
    weight_sets = [
        jnp.swapaxes(w.reshape(depth, groups, pair), 0, 1) for w in weight_sets
    ]

    def gather_weights(blocks):
        if not split:
            return [lax.all_gather(blocks[0], "ctx", axis=0, tiled=True)]
        held = [lax.dynamic_index_in_dim(blocks, group, 0, keepdims=False)]
        for step in range(1, groups):
            block = lax.dynamic_index_in_dim(blocks, group ^ step, 0, keepdims=False)
            held.append(swap(block, step * team))
        held = jnp.concatenate(held, axis=0)
        held = jnp.concatenate([held, swap(held, 2)], axis=0)
        return [held, swap(held, 1)]

    if split:
        pieces = [stored] + [swap(stored, step * team) for step in range(1, groups)]
        pieces = [(piece, flip(piece)) for piece in pieces]
    else:
        pieces = [(lax.all_gather(stored, "tp", axis=1, tiled=True),)]
    row_blocks, col_chunks = len(pieces), len(pieces[0])
    flat = [chunk for piece in pieces for chunk in piece]
    total_rows = row_blocks * rows
    width = stored.shape[1] * ntp

    kv_weights = gather_weights(weight_sets[0])
    tokens, kv = call(
        functools.partial(kv_kernel, (row_blocks, col_chunks, len(kv_weights), col_blocks)),
        [
            jax.ShapeDtypeStruct((total_rows, width), jnp.bfloat16),
            jax.ShapeDtypeStruct((total_rows, pair), jnp.bfloat16),
        ],
        [table, *flat, *kv_weights, cosine, sine],
        scratch=[pltpu.VMEM((total_rows, width), jnp.bfloat16)],
        flops=2 * total_rows * width * pair,
        smem_first=True,
    )
    if split:
        kvs = jnp.concatenate([kv, swap(kv, 2)], axis=0)
        kvs = [kvs, swap(kvs, 1)]
    else:
        kvs = [lax.all_gather(kv, "ctx", axis=0, tiled=True)]

    slot = before[:, mine][:, :, None] + jnp.arange(cap, dtype=jnp.int32)
    slot_row = jnp.where(
        slot < rows, slot + jnp.arange(row_blocks, dtype=jnp.int32)[None, :, None] * rows, -1
    ).reshape(-1, 1)
    keys = nctx * rows
    block_rows = min(2 * rows, total_rows)
    incoming = []
    for part in range(parts):
        weights = gather_weights(weight_sets[1 + part])
        outgoing = call(
            functools.partial(attention_kernel, (len(weights), len(kvs), block_rows)),
            jax.ShapeDtypeStruct((slot_row.shape[0], pair), jnp.bfloat16),
            [tokens, *weights, *kvs, cosine, sine, my_start[:, None], key_start, slot_row],
            scratch=[
                pltpu.VMEM((total_rows, pair), jnp.bfloat16),
                pltpu.VMEM((block_rows, keys), jnp.float32),
                pltpu.VMEM((total_rows, pair), jnp.bfloat16),
            ],
            flops=2 * total_rows * pair * (width + 2 * keys + slot_row.shape[0]),
        )
        incoming.append(lax.all_to_all(outgoing, "ctx", 0, 0, tiled=True))

    own_hot = source_owner[:, None] == owner_range
    earlier = jnp.einsum(
        "pq,qo->po", lower, own_hot.astype(jnp.bfloat16), preferred_element_type=jnp.float32
    )
    local_rank = jnp.sum(jnp.where(own_hot, earlier, 0.0), axis=1).astype(jnp.int32)
    owner_group, owner_mate = source_owner // team, source_owner % team
    every = jnp.arange(groups, dtype=jnp.int32)
    columns = (
        (owner_mate * groups)[:, None] + (owner_group[:, None] ^ every[None, :])
    ) * cap + local_rank[:, None]
    return call(
        functools.partial(combine_kernel, groups),
        jax.ShapeDtypeStruct((rows, wq.shape[1]), jnp.bfloat16),
        [columns, *incoming],
        flops=2 * rows * wq.shape[1] * team * groups * cap,
    )


def solution(mesh):
    return jax.shard_map(
        body,
        mesh=mesh,
        in_specs=(
            P("ctx", "tp"),
            P("ctx"),
            P("ctx"),
            P(),
            P("ctx", "tp"),
            P("ctx", "tp"),
            P("ctx", "tp"),
        ),
        out_specs=P("ctx", "tp"),
        check_vma=False,
    )
```

```python
import functools

import jax
import jax.numpy as jnp
import numpy as np
from jax import lax
from jax.experimental import pallas as pl
from jax.experimental.pallas import tpu as pltpu
from jax.sharding import PartitionSpec as P

HEAD_SIZE = 128
LANES = 128
ROPE_BASE = 500000.0
VMEM_LIMIT = 48 * 1024 * 1024
OTHER = -(2.0**100)

VMEM_SPEC = pl.BlockSpec(memory_space=pltpu.VMEM)
SMEM_SPEC = pl.BlockSpec(memory_space=pltpu.SMEM)


def dot(a, b):
    return jnp.dot(a, b, preferred_element_type=jnp.float32)


def dot_rows(a, b):
    return lax.dot_general(
        a, b, (((1,), (1,)), ((), ())), preferred_element_type=jnp.float32
    )


def call(kernel, out_shape, operands, scratch=(), flops=0, smem=()):
    specs = [SMEM_SPEC if at in smem else VMEM_SPEC for at in range(len(operands))]
    many = isinstance(out_shape, (list, tuple))
    outs = out_shape if many else [out_shape]
    moved = sum(x.size * x.dtype.itemsize for x in [*operands, *outs])
    return pl.pallas_call(
        kernel,
        out_shape=out_shape,
        in_specs=specs,
        out_specs=[VMEM_SPEC] * len(out_shape) if many else VMEM_SPEC,
        scratch_shapes=list(scratch),
        compiler_params=pltpu.CompilerParams(vmem_limit_bytes=VMEM_LIMIT),
        cost_estimate=pl.CostEstimate(flops=flops, bytes_accessed=moved, transcendentals=0),
    )(*operands)


def weights_kernel(wq, wk, wv, first, second):
    for group in range(first.shape[0]):
        own = slice(group * HEAD_SIZE, (group + 1) * HEAD_SIZE)
        half = second.shape[2]
        start = group * 2 * half
        first[group, :, :HEAD_SIZE] = wk[:, own]
        first[group, :, HEAD_SIZE : 2 * HEAD_SIZE] = wv[:, own]
        first[group, :, 2 * HEAD_SIZE :] = wq[:, start : start + half]
        second[group] = wq[:, start + half : start + 2 * half]


def places_kernel(cap, mine, order, me, doc_starts, owners, freqs, *refs):
    angles, key_hot, query_bar, slots, columns, coded, starts, local = refs
    shards, rows = owners.shape
    groups = mine.shape[0]
    team = shards // groups
    owner_at = lax.broadcasted_iota(jnp.int32, (shards, rows), 0)
    upper = jnp.where(
        lax.broadcasted_iota(jnp.int32, (rows, rows), 0)
        < lax.broadcasted_iota(jnp.int32, (rows, rows), 1),
        1.0,
        0.0,
    ).astype(jnp.bfloat16)
    rank_at = lax.broadcasted_iota(jnp.int32, (rows, rows), 0).astype(jnp.float32)
    lane = lax.broadcasted_iota(jnp.int32, (1, rows), 1).astype(jnp.float32)
    before = jnp.zeros((shards, 1), jnp.float32)
    found = jnp.zeros((3 * shards, rows), jnp.float32)
    for shard in range(shards):
        hot = jnp.where(owners[shard : shard + 1, :] == owner_at, 1.0, 0.0)
        within = dot(hot.astype(jnp.bfloat16), upper)
        local[shard : shard + 1, :] = jnp.sum(hot * within, axis=0, keepdims=True)
        rank = jnp.sum(hot * (within + before), axis=0, keepdims=True)
        before = before + jnp.sum(hot, axis=1, keepdims=True)
        rank_hot = jnp.where(rank_at == rank, 1.0, 0.0).astype(jnp.bfloat16)
        codes = jnp.concatenate([hot * float(shard), hot * lane, hot * within], axis=0)
        found = found + dot_rows(codes.astype(jnp.bfloat16), rank_hot)
    shard_of = found[:shards]
    place = shard_of * rows + found[shards : 2 * shards]
    start = jnp.zeros_like(place)
    docs = doc_starts.shape[0]
    doc_lane = lax.broadcasted_iota(jnp.int32, (1, LANES), 1)
    doc_row = jnp.full((1, LANES), -1.0, jnp.float32)
    for doc in range(docs):
        value = doc_starts[doc].astype(jnp.float32)
        start = jnp.maximum(start, jnp.where(value <= place, value, 0.0))
        doc_row = jnp.where(doc_lane == doc, value, doc_row)
    coded[...] = shard_of * (groups * cap) + found[2 * shards :]
    starts[:shards, :] = start
    starts[shards : 2 * shards, :] = place - start
    flat = jnp.transpose(starts[...])
    which = lax.broadcasted_iota(jnp.int32, flat.shape, 1)
    for group in range(groups):
        own = slice(group * rows, (group + 1) * rows)
        at = mine[group]
        begin = jnp.sum(jnp.where(which == at, flat, 0.0), axis=1, keepdims=True)
        inside = jnp.sum(jnp.where(which == at + shards, flat, 0.0), axis=1, keepdims=True)
        angles[own, :] = inside * freqs[...]
        query_bar[own, :] = jnp.where(begin == doc_row, 0.0, OTHER).astype(jnp.bfloat16)
        slots[:, own] = (coded[pl.ds(at, 1), :] + float(group * cap)).astype(jnp.int32)
    for block in range(shards):
        own = slice(block * rows, (block + 1) * rows)
        begin = jnp.sum(jnp.where(which == order[block], flat, 0.0), axis=1, keepdims=True)
        key_hot[own, :] = jnp.where(begin == doc_row, 1.0, 0.0).astype(jnp.bfloat16)
    owner = owners[pl.ds(me[0], 1), :]
    owner_group = jnp.zeros_like(owner)
    for group in range(1, groups):
        owner_group = jnp.where(owner >= group * team, group, owner_group)
    owner_mate = owner - owner_group * team
    rank = local[pl.ds(me[0], 1), :].astype(jnp.int32)
    columns[...] = (owner_mate * groups + owner_group) * cap + rank


def rotate(raw, cosine, sine):
    return raw * cosine + pltpu.roll(raw, HEAD_SIZE // 2, 1) * sine


def project(tokens, weights, cols):
    total = None
    start = 0
    for weight in weights:
        depth = weight.shape[0]
        part = dot(tokens[:, start : start + depth], weight[:, cols])
        total = part if total is None else total + part
        start += depth
    return total


def kv_kernel(layout, places, table, *refs):
    row_blocks, col_chunks, weight_parts, col_blocks = layout
    pieces = refs[: row_blocks * col_chunks]
    at = row_blocks * col_chunks
    weights = refs[at : at + weight_parts]
    cosine, sine, tokens, kv, loose = refs[at + weight_parts :]
    piece_rows, piece_cols = pieces[0].shape
    for row in range(row_blocks):
        there = pl.ds(pl.multiple_of(places[row] * piece_rows, piece_rows), piece_rows)
        for col in range(col_chunks):
            loose[there, col * piece_cols : (col + 1) * piece_cols] = pieces[
                row * col_chunks + col
            ][...]
    width = loose.shape[1] // col_blocks
    for block in range(col_blocks):
        source = pl.ds(pl.multiple_of(table[block] * width, width), width)
        tokens[:, block * width : (block + 1) * width] = loose[:, source]
    total = project(tokens, weights, slice(0, 2 * HEAD_SIZE))
    kv[:, :HEAD_SIZE] = rotate(total[:, :HEAD_SIZE], cosine[...], sine[...]).astype(kv.dtype)
    kv[:, HEAD_SIZE:] = total[:, HEAD_SIZE:].astype(kv.dtype)


def query_kernel(start, tokens, *refs):
    weights = refs[:-3]
    cosine, sine, queries = refs[-3:]
    count = queries.shape[1]
    raw = project(tokens, weights, slice(start, start + count))
    for head in range(count // HEAD_SIZE):
        cols = slice(head * HEAD_SIZE, (head + 1) * HEAD_SIZE)
        queries[:, cols] = rotate(raw[:, cols], cosine[...], sine[...]).astype(queries.dtype)


def attention_kernel(block_rows, queries, query_bar, key_hot, slots, *refs):
    kvs = refs[:-6]
    outgoing, keys, values, long, scores, context = refs[-6:]
    rows = queries.shape[0]
    heads = queries.shape[1] // HEAD_SIZE
    start = 0
    for kv in kvs:
        own = slice(start, start + kv.shape[0])
        keys[own, :HEAD_SIZE] = kv[:, :HEAD_SIZE]
        values[own, :] = kv[:, HEAD_SIZE:]
        start += kv.shape[0]
    keys[:, HEAD_SIZE:] = key_hot[...]
    for head in range(heads):
        long[head, :, :HEAD_SIZE] = queries[:, head * HEAD_SIZE : (head + 1) * HEAD_SIZE]
        long[head, :, HEAD_SIZE:] = query_bar[...]
    factor = 1.4426950408889634 / HEAD_SIZE**0.5
    steps = [(block, head) for block in range(rows // block_rows) for head in range(heads)]

    def score(step):
        block, head = steps[step]
        own = slice(block * block_rows, (block + 1) * block_rows)
        scores[step % 2] = dot_rows(long[head, own, :], keys[...])

    score(0)
    for step, (block, head) in enumerate(steps):
        if step + 1 < len(steps):
            score(step + 1)
        own = slice(block * block_rows, (block + 1) * block_rows)
        held = scores[step % 2]
        top = jnp.max(held, axis=1, keepdims=True)
        kept = jnp.exp2((held - top) * factor)
        total = jnp.sum(kept, axis=1, keepdims=True)
        mixed = dot(kept.astype(jnp.bfloat16), values[...])
        context[own, head * HEAD_SIZE : (head + 1) * HEAD_SIZE] = (mixed / total).astype(
            context.dtype
        )
    places = lax.broadcasted_iota(jnp.int32, (outgoing.shape[0], rows), 0)
    hot = jnp.where(places == slots[...], 1.0, 0.0).astype(jnp.bfloat16)
    outgoing[...] = dot(hot, context[...]).astype(outgoing.dtype)


def combine_kernel(groups, columns, *refs):
    incoming = refs[:-1]
    out = refs[-1]
    width = incoming[0].shape[1]
    span = incoming[0].shape[0] // groups
    places = lax.broadcasted_iota(jnp.int32, (span, out.shape[0]), 0)
    hot = jnp.where(places == columns[...], 1.0, 0.0).astype(jnp.bfloat16)
    for group in range(groups):
        for part, ref in enumerate(incoming):
            picked = lax.dot_general(
                hot,
                ref[group * span : (group + 1) * span, :],
                (((0,), (0,)), ((), ())),
                preferred_element_type=jnp.float32,
            )
            start = (group * len(incoming) + part) * width
            out[:, start : start + width] = picked.astype(out.dtype)


def swap(value, bits):
    count = lax.axis_size("ctx")
    return lax.ppermute(value, "ctx", [(i, i ^ bits) for i in range(count)])


def step_along(value, team, pairs):
    return lax.ppermute(
        value, "ctx", [(a * team + t, b * team + t) for a, b in pairs for t in range(team)]
    )


def flip(value):
    return lax.ppermute(value, "tp", [(0, 1), (1, 0)])


def spread(value):
    across = swap(value, 2)
    return [value, across, swap(value, 1), swap(across, 1)]


def along_line(value, group, team):
    near = swap(value, team)
    over = step_along(value, team, [(1, 2), (2, 1)])
    over_near = step_along(near, team, [(1, 2), (2, 1)])
    end = step_along(over, team, [(1, 0), (2, 3)])
    end_near = step_along(over_near, team, [(1, 0), (2, 3)])
    edge = (group == 0) | (group == 3)
    third = jnp.where(edge, end, over)
    fourth = jnp.where(edge, end_near, over_near)
    places = jnp.stack(
        [group, group ^ 1, group ^ jnp.where(edge, 2, 3), group ^ jnp.where(edge, 3, 2)]
    )
    return [value, near, third, fourth], places


def body(stored, source_owner, doc_ids, doc_starts, wq, wk, wv):
    nctx = lax.axis_size("ctx")
    ntp = lax.axis_size("tp")
    me = lax.axis_index("ctx")
    rows = stored.shape[0]
    cap = 2 * rows // nctx
    size = HEAD_SIZE
    depth = wq.shape[0]
    groups = wk.shape[1] // size
    team = nctx // groups
    group, mate = me // team, me % team
    split = groups > 1
    half = wq.shape[1] // groups // 2

    if split:
        pieces, places = along_line(stored, group, team)
        pieces = [(piece, flip(piece)) for piece in pieces]
    else:
        pieces = [(lax.all_gather(stored, "tp", axis=1, tiled=True),)]
        places = jnp.zeros((1,), jnp.int32)
    row_blocks, col_chunks = len(pieces), len(pieces[0])
    flat = [chunk for piece in pieces for chunk in piece]
    total_rows = row_blocks * rows
    width = stored.shape[1] * ntp

    first, second = call(
        weights_kernel,
        [
            jax.ShapeDtypeStruct((groups, depth, 2 * size + half), jnp.bfloat16),
            jax.ShapeDtypeStruct((groups, depth, half), jnp.bfloat16),
        ],
        [wq, wk, wv],
    )

    def gather_weights(slabs):
        if not split:
            return [lax.all_gather(slabs[0], "ctx", axis=0, tiled=True)]
        lines = [[g * team + t for g in range(groups)] for t in range(team)]
        mine = lax.all_to_all(slabs, "ctx", 0, 0, axis_index_groups=lines, tiled=True)
        return spread(mine.reshape(groups * depth, slabs.shape[2]))

    first = gather_weights(first)
    second = gather_weights(second)

    owner_range = jnp.arange(nctx, dtype=jnp.int32)
    if split:
        rel = jnp.arange(groups, dtype=jnp.int32)
        turns = jnp.array([0, 2, 1, 3], dtype=jnp.int32)
        order = (rel[None, :] * team + (mate ^ turns)[:, None]).reshape(-1)
        mine = rel * team + mate
        share = nctx // ntp
        table = order % share + jnp.where(order // share == lax.axis_index("tp"), 0, share)
        col_blocks = nctx
    else:
        order = owner_range
        mine = me[None]
        table = jnp.zeros((1,), jnp.int32)
        col_blocks = 1

    owners = lax.all_to_all(
        jnp.broadcast_to(source_owner[None, :], (nctx, rows)), "ctx", 0, 0, tiled=True
    )
    freqs = ROPE_BASE ** (-np.arange(size // 2) * 2.0 / size)
    freqs = jnp.asarray(np.concatenate([freqs, freqs])[None, :], jnp.float32)
    sign = jnp.asarray(np.repeat([-1.0, 1.0], size // 2)[None, :], jnp.float32)
    keys = nctx * rows
    angles, key_hot, query_bar, slots, columns = call(
        functools.partial(places_kernel, cap),
        [
            jax.ShapeDtypeStruct((total_rows, size), jnp.float32),
            jax.ShapeDtypeStruct((keys, LANES), jnp.bfloat16),
            jax.ShapeDtypeStruct((total_rows, LANES), jnp.bfloat16),
            jax.ShapeDtypeStruct((1, total_rows), jnp.int32),
            jax.ShapeDtypeStruct((1, rows), jnp.int32),
        ],
        [mine, order, me[None], doc_starts, owners, freqs],
        scratch=[
            pltpu.VMEM((nctx, rows), jnp.float32),
            pltpu.VMEM((max(2 * nctx, LANES), rows), jnp.float32),
            pltpu.VMEM((nctx, rows), jnp.float32),
        ],
        flops=10**9,
        smem=(0, 1, 2, 3),
    )
    cosine = jnp.cos(angles)
    sine = jnp.sin(angles) * sign

    tokens, kv = call(
        functools.partial(kv_kernel, (row_blocks, col_chunks, len(first), col_blocks)),
        [
            jax.ShapeDtypeStruct((total_rows, width), jnp.bfloat16),
            jax.ShapeDtypeStruct((total_rows, 2 * size), jnp.bfloat16),
        ],
        [places, table, *flat, *first, cosine, sine],
        scratch=[pltpu.VMEM((total_rows, width), jnp.bfloat16)],
        flops=4 * total_rows * width * size,
        smem=(0, 1),
    )
    kvs = spread(kv) if split else [lax.all_gather(kv, "ctx", axis=0, tiled=True)]

    block_rows = min(2 * rows, total_rows)
    incoming = []
    for weights, start in ((first, 2 * size), (second, 0)):
        queries = call(
            functools.partial(query_kernel, start),
            jax.ShapeDtypeStruct((total_rows, half), jnp.bfloat16),
            [tokens, *weights, cosine, sine],
            flops=2 * total_rows * width * half,
        )
        outgoing = call(
            functools.partial(attention_kernel, block_rows),
            jax.ShapeDtypeStruct((nctx * groups * cap, half), jnp.bfloat16),
            [queries, query_bar, key_hot, slots, *kvs],
            scratch=[
                pltpu.VMEM((keys, size + LANES), jnp.bfloat16),
                pltpu.VMEM((keys, size), jnp.bfloat16),
                pltpu.VMEM((half // size, total_rows, size + LANES), jnp.bfloat16),
                pltpu.VMEM((2, block_rows, keys), jnp.float32),
                pltpu.VMEM((total_rows, half), jnp.bfloat16),
            ],
            flops=8 * total_rows * half * keys,
        )
        incoming.append(lax.all_to_all(outgoing, "ctx", 0, 0, tiled=True))

    return call(
        functools.partial(combine_kernel, groups),
        jax.ShapeDtypeStruct((rows, wq.shape[1]), jnp.bfloat16),
        [columns, *incoming],
        flops=2 * rows * wq.shape[1] * nctx * cap,
    )


def solution(mesh):
    return jax.shard_map(
        body,
        mesh=mesh,
        in_specs=(
            P("ctx", "tp"),
            P("ctx"),
            P("ctx"),
            P(),
            P("ctx", "tp"),
            P("ctx", "tp"),
            P("ctx", "tp"),
        ),
        out_specs=P("ctx", "tp"),
        check_vma=False,
    )
```

```python
import functools

import jax
import jax.numpy as jnp
import numpy as np
from jax import lax
from jax.experimental import pallas as pl
from jax.experimental.pallas import tpu as pltpu
from jax.sharding import PartitionSpec as P

HEAD_SIZE = 128
LANES = 128
ROPE_BASE = 500000.0
OTHER = -(2.0**100)

VMEM_SPEC = pl.BlockSpec(memory_space=pltpu.VMEM)
SMEM_SPEC = pl.BlockSpec(memory_space=pltpu.SMEM)


def dot(a, b):
    return jnp.dot(a, b, preferred_element_type=jnp.float32)


def dot_rows(a, b):
    return lax.dot_general(
        a, b, (((1,), (1,)), ((), ())), preferred_element_type=jnp.float32
    )


def call(kernel, out_shape, operands, scratch=(), flops=0, smem=(), vmem=24):
    specs = [SMEM_SPEC if at in smem else VMEM_SPEC for at in range(len(operands))]
    many = isinstance(out_shape, (list, tuple))
    outs = out_shape if many else [out_shape]
    moved = sum(x.size * x.dtype.itemsize for x in [*operands, *outs])
    return pl.pallas_call(
        kernel,
        out_shape=out_shape,
        in_specs=specs,
        out_specs=[VMEM_SPEC] * len(out_shape) if many else VMEM_SPEC,
        scratch_shapes=list(scratch),
        compiler_params=pltpu.CompilerParams(vmem_limit_bytes=vmem * 2**20),
        cost_estimate=pl.CostEstimate(flops=flops, bytes_accessed=moved, transcendentals=0),
    )(*operands)


def weights_kernel(far, wq, wk, wv, first, *second):
    half = second[0].shape[1]
    for group in range(first.shape[0]):
        own = slice(group * HEAD_SIZE, (group + 1) * HEAD_SIZE)
        start = group * 2 * half
        first[group, :, :HEAD_SIZE] = wk[:, own]
        first[group, :, HEAD_SIZE : 2 * HEAD_SIZE] = wv[:, own]
        first[group, :, 2 * HEAD_SIZE :] = wq[:, start : start + half]
        start = pl.multiple_of(far[group] * 2 * half + half, half)
        second[group][...] = wq[:, pl.ds(start, half)]


def places_kernel(cap, mine, order, me, doc_starts, owners, freqs, *refs):
    angles, key_hot, query_bar, slots, columns, coded, starts, local = refs
    shards, rows = owners.shape
    groups = mine.shape[0]
    team = shards // groups
    owner_at = lax.broadcasted_iota(jnp.int32, (shards, rows), 0)
    upper = jnp.where(
        lax.broadcasted_iota(jnp.int32, (rows, rows), 0)
        < lax.broadcasted_iota(jnp.int32, (rows, rows), 1),
        1.0,
        0.0,
    ).astype(jnp.bfloat16)
    rank_at = lax.broadcasted_iota(jnp.int32, (rows, rows), 0).astype(jnp.float32)
    lane = lax.broadcasted_iota(jnp.int32, (1, rows), 1).astype(jnp.float32)
    before = jnp.zeros((shards, 1), jnp.float32)
    found = jnp.zeros((3 * shards, rows), jnp.float32)
    for shard in range(shards):
        hot = jnp.where(owners[shard : shard + 1, :] == owner_at, 1.0, 0.0)
        within = dot(hot.astype(jnp.bfloat16), upper)
        local[shard : shard + 1, :] = jnp.sum(hot * within, axis=0, keepdims=True)
        rank = jnp.sum(hot * (within + before), axis=0, keepdims=True)
        before = before + jnp.sum(hot, axis=1, keepdims=True)
        rank_hot = jnp.where(rank_at == rank, 1.0, 0.0).astype(jnp.bfloat16)
        codes = jnp.concatenate([hot * float(shard), hot * lane, hot * within], axis=0)
        found = found + dot_rows(codes.astype(jnp.bfloat16), rank_hot)
    shard_of = found[:shards]
    place = shard_of * rows + found[shards : 2 * shards]
    start = jnp.zeros_like(place)
    docs = doc_starts.shape[0]
    doc_lane = lax.broadcasted_iota(jnp.int32, (1, LANES), 1)
    doc_row = jnp.full((1, LANES), -1.0, jnp.float32)
    for doc in range(docs):
        value = doc_starts[doc].astype(jnp.float32)
        start = jnp.maximum(start, jnp.where(value <= place, value, 0.0))
        doc_row = jnp.where(doc_lane == doc, value, doc_row)
    coded[...] = shard_of * (groups * cap) + found[2 * shards :]
    starts[:shards, :] = start
    starts[shards : 2 * shards, :] = place - start
    flat = jnp.transpose(starts[...])
    which = lax.broadcasted_iota(jnp.int32, flat.shape, 1)
    for group in range(groups):
        own = slice(group * rows, (group + 1) * rows)
        at = mine[group]
        begin = jnp.sum(jnp.where(which == at, flat, 0.0), axis=1, keepdims=True)
        inside = jnp.sum(jnp.where(which == at + shards, flat, 0.0), axis=1, keepdims=True)
        angles[own, :] = inside * freqs[...]
        query_bar[own, :] = jnp.where(begin == doc_row, 0.0, OTHER).astype(jnp.bfloat16)
        slots[:, own] = (coded[pl.ds(at, 1), :] + float(group * cap)).astype(jnp.int32)
    for block in range(shards):
        own = slice(block * rows, (block + 1) * rows)
        begin = jnp.sum(jnp.where(which == order[block], flat, 0.0), axis=1, keepdims=True)
        key_hot[own, :] = jnp.where(begin == doc_row, 1.0, 0.0).astype(jnp.bfloat16)
    owner = owners[pl.ds(me[0], 1), :]
    owner_group = jnp.zeros_like(owner)
    for group in range(1, groups):
        owner_group = jnp.where(owner >= group * team, group, owner_group)
    owner_mate = owner - owner_group * team
    rank = local[pl.ds(me[0], 1), :].astype(jnp.int32)
    columns[...] = (owner_mate * groups + owner_group) * cap + rank


def rotate(raw, cosine, sine):
    return raw * cosine + pltpu.roll(raw, HEAD_SIZE // 2, 1) * sine


def project(tokens, weights, cols):
    total = None
    start = 0
    for weight in weights:
        depth = weight.shape[0]
        part = dot(tokens[:, start : start + depth], weight[:, cols])
        total = part if total is None else total + part
        start += depth
    return total


def kv_kernel(blocks, table, pieces, *refs):
    weights = refs[:-5]
    cosine, sine, tokens, kv, loose = refs[-5:]
    count, rows, width = pieces.shape
    chunks = loose.shape[1] // width
    for piece in range(count):
        row, col = piece // chunks, piece % chunks
        loose[row * rows : (row + 1) * rows, col * width : (col + 1) * width] = pieces[piece]
    width = loose.shape[1] // blocks
    for block in range(blocks):
        source = pl.ds(pl.multiple_of(table[block] * width, width), width)
        tokens[:, block * width : (block + 1) * width] = loose[:, source]
    total = project(tokens, weights, slice(0, 2 * HEAD_SIZE))
    kv[:, :HEAD_SIZE] = rotate(total[:, :HEAD_SIZE], cosine[...], sine[...]).astype(kv.dtype)
    kv[:, HEAD_SIZE:] = total[:, HEAD_SIZE:].astype(kv.dtype)


def query_kernel(parts, tokens, *refs):
    first, second = refs[:parts], refs[parts : 2 * parts]
    cosine, sine, queries = refs[2 * parts :]
    half = queries.shape[1] // 2
    skip = first[0].shape[1] - half
    for at, (weights, start) in enumerate(((first, skip), (second, 0))):
        raw = project(tokens, weights, slice(start, start + half))
        for head in range(half // HEAD_SIZE):
            cols = slice(head * HEAD_SIZE, (head + 1) * HEAD_SIZE)
            turned = rotate(raw[:, cols], cosine[...], sine[...]).astype(queries.dtype)
            queries[:, at * half + cols.start : at * half + cols.stop] = turned


def assemble_kernel(far, *refs):
    out = refs[-1]
    for step, piece in enumerate(refs[:-1]):
        rows = piece.shape[0]
        out[pl.ds(pl.multiple_of(far[step] * rows, rows), rows), :] = piece[...]


def attention_kernel(block_rows, queries, query_bar, key_hot, slots, *refs):
    kvs = refs[:-6]
    outgoing, keys, values, long, scores, context = refs[-6:]
    rows = queries.shape[0]
    heads = queries.shape[1] // HEAD_SIZE
    start = 0
    for kv in kvs:
        own = slice(start, start + kv.shape[0])
        keys[own, :HEAD_SIZE] = kv[:, :HEAD_SIZE]
        values[own, :] = kv[:, HEAD_SIZE:]
        start += kv.shape[0]
    keys[:, HEAD_SIZE:] = key_hot[...]
    for head in range(heads):
        long[head, :, :HEAD_SIZE] = queries[:, head * HEAD_SIZE : (head + 1) * HEAD_SIZE]
        long[head, :, HEAD_SIZE:] = query_bar[...]
    factor = 1.4426950408889634 / HEAD_SIZE**0.5
    steps = [(block, head) for block in range(rows // block_rows) for head in range(heads)]

    def score(step):
        block, head = steps[step]
        own = slice(block * block_rows, (block + 1) * block_rows)
        scores[step % 2] = dot_rows(long[head, own, :], keys[...])

    score(0)
    for step, (block, head) in enumerate(steps):
        if step + 1 < len(steps):
            score(step + 1)
        own = slice(block * block_rows, (block + 1) * block_rows)
        held = scores[step % 2]
        top = jnp.max(held, axis=1, keepdims=True)
        kept = jnp.exp2((held - top) * factor)
        total = jnp.sum(kept, axis=1, keepdims=True)
        mixed = dot(kept.astype(jnp.bfloat16), values[...])
        context[own, head * HEAD_SIZE : (head + 1) * HEAD_SIZE] = (mixed / total).astype(
            context.dtype
        )
    places = lax.broadcasted_iota(jnp.int32, (outgoing.shape[0], rows), 0)
    hot = jnp.where(places == slots[...], 1.0, 0.0).astype(jnp.bfloat16)
    outgoing[...] = dot(hot, context[...]).astype(outgoing.dtype)


def combine_kernel(groups, columns, *refs):
    incoming = refs[:-1]
    out = refs[-1]
    width = incoming[0].shape[1]
    span = incoming[0].shape[0] // groups
    places = lax.broadcasted_iota(jnp.int32, (span, out.shape[0]), 0)
    hot = jnp.where(places == columns[...], 1.0, 0.0).astype(jnp.bfloat16)
    for group in range(groups):
        for part, ref in enumerate(incoming):
            picked = lax.dot_general(
                hot,
                ref[group * span : (group + 1) * span, :],
                (((0,), (0,)), ((), ())),
                preferred_element_type=jnp.float32,
            )
            start = (group * len(incoming) + part) * width
            out[:, start : start + width] = picked.astype(out.dtype)


def turn(value, axis, bits):
    count = lax.axis_size(axis)
    return lax.ppermute(value, axis, [(i, i ^ bits) for i in range(count)])


def spread(value):
    across = turn(value, "team", 2)
    return [value, across, turn(value, "team", 1), turn(across, "team", 1)]


def body(stored, source_owner, doc_ids, doc_starts, wq, wk, wv):
    groups, team = lax.axis_size("line"), lax.axis_size("team")
    nctx, ntp = groups * team, lax.axis_size("tp")
    group, mate = lax.axis_index("line"), lax.axis_index("team")
    me = group * team + mate
    rows = stored.shape[0]
    cap = 2 * rows // nctx
    size = HEAD_SIZE
    depth = wq.shape[0]
    split = groups > 1
    half = wq.shape[1] // groups // 2

    pieces = lax.all_gather(stored, ("line", "tp"), axis=0)
    row_blocks, col_chunks = groups, ntp
    total_rows = row_blocks * rows
    width = stored.shape[1] * ntp

    far = group ^ jnp.arange(groups, dtype=jnp.int32)
    first, *second = call(
        weights_kernel,
        [jax.ShapeDtypeStruct((groups, depth, 2 * size + half), jnp.bfloat16)]
        + [jax.ShapeDtypeStruct((depth, half), jnp.bfloat16)] * groups,
        [far, wq, wk, wv],
        smem=(0,),
    )
    if split:
        first = lax.all_to_all(first, "line", 0, 0, tiled=True)
        first = spread(first.reshape(groups * depth, first.shape[2]))
        moved = [turn(second[step], "line", step) for step in range(1, groups)]
        second = call(
            assemble_kernel,
            jax.ShapeDtypeStruct((groups * depth, half), jnp.bfloat16),
            [far, second[0], *moved],
            smem=(0,),
        )
        second = spread(second)
    else:
        first = [lax.all_gather(first[0], "team", axis=0, tiled=True)]
        second = [lax.all_gather(second[0], "team", axis=0, tiled=True)]

    owner_range = jnp.arange(nctx, dtype=jnp.int32)
    if split:
        rel = jnp.arange(groups, dtype=jnp.int32)
        turns = mate ^ jnp.array([0, 2, 1, 3], dtype=jnp.int32)
        order = (rel[None, :] * team + turns[:, None]).reshape(-1)
        mine = rel * team + mate
    else:
        order = owner_range
        mine = me[None]

    owners = lax.all_to_all(
        jnp.broadcast_to(source_owner[None, :], (nctx, rows)), ("line", "team"), 0, 0, tiled=True
    )
    freqs = ROPE_BASE ** (-np.arange(size // 2) * 2.0 / size)
    freqs = jnp.asarray(np.concatenate([freqs, freqs])[None, :], jnp.float32)
    sign = jnp.asarray(np.repeat([-1.0, 1.0], size // 2)[None, :], jnp.float32)
    keys = nctx * rows
    angles, key_hot, query_bar, slots, columns = call(
        functools.partial(places_kernel, cap),
        [
            jax.ShapeDtypeStruct((total_rows, size), jnp.float32),
            jax.ShapeDtypeStruct((keys, LANES), jnp.bfloat16),
            jax.ShapeDtypeStruct((total_rows, LANES), jnp.bfloat16),
            jax.ShapeDtypeStruct((1, total_rows), jnp.int32),
            jax.ShapeDtypeStruct((1, rows), jnp.int32),
        ],
        [mine, order, me[None], doc_starts, owners, freqs],
        scratch=[
            pltpu.VMEM((nctx, rows), jnp.float32),
            pltpu.VMEM((max(2 * nctx, LANES), rows), jnp.float32),
            pltpu.VMEM((nctx, rows), jnp.float32),
        ],
        flops=10**9,
        smem=(0, 1, 2, 3),
    )
    cosine = jnp.cos(angles)
    sine = jnp.sin(angles) * sign

    blocks = nctx if split else 1
    tokens, kv = call(
        functools.partial(kv_kernel, blocks),
        [
            jax.ShapeDtypeStruct((total_rows, width), jnp.bfloat16),
            jax.ShapeDtypeStruct((total_rows, 2 * size), jnp.bfloat16),
        ],
        [order if split else jnp.zeros((1,), jnp.int32), pieces, *first, cosine, sine],
        scratch=[pltpu.VMEM((total_rows, width), jnp.bfloat16)],
        flops=4 * total_rows * width * size,
        smem=(0,),
        vmem=32,
    )
    kvs = spread(kv) if split else [lax.all_gather(kv, "team", axis=0, tiled=True)]
    queries = call(
        functools.partial(query_kernel, len(first)),
        jax.ShapeDtypeStruct((total_rows, 2 * half), jnp.bfloat16),
        [tokens, *first, *second, cosine, sine],
        flops=4 * total_rows * width * half,
        vmem=32,
    )
    block_rows = min(2 * rows, total_rows)
    outgoing = call(
        functools.partial(attention_kernel, block_rows),
        jax.ShapeDtypeStruct((nctx * groups * cap, 2 * half), jnp.bfloat16),
        [queries, query_bar, key_hot, slots, *kvs],
        scratch=[
            pltpu.VMEM((keys, size + LANES), jnp.bfloat16),
            pltpu.VMEM((keys, size), jnp.bfloat16),
            pltpu.VMEM((2 * half // size, total_rows, size + LANES), jnp.bfloat16),
            pltpu.VMEM((2, block_rows, keys), jnp.float32),
            pltpu.VMEM((total_rows, 2 * half), jnp.bfloat16),
        ],
        flops=8 * total_rows * half * keys,
        vmem=40,
    )
    incoming = lax.all_to_all(outgoing, ("line", "team"), 0, 0, tiled=True)
    return call(
        functools.partial(combine_kernel, groups),
        jax.ShapeDtypeStruct((rows, wq.shape[1]), jnp.bfloat16),
        [columns, incoming],
        flops=2 * rows * wq.shape[1] * nctx * cap,
        vmem=16,
    )


def solution(mesh):
    def program(stored, source_owner, doc_ids, doc_starts, wq, wk, wv):
        ctx, tp = mesh.shape["ctx"], mesh.shape["tp"]
        groups = wk.shape[1] // HEAD_SIZE // tp
        parts = jax.sharding.Mesh(
            mesh.devices.reshape(groups, ctx // groups, tp), ("line", "team", "tp")
        )
        both = ("line", "team")
        return jax.shard_map(
            body,
            mesh=parts,
            in_specs=(
                P(both, "tp"),
                P(both),
                P(both),
                P(),
                P(both, "tp"),
                P(both, "tp"),
                P(both, "tp"),
            ),
            out_specs=P(both, "tp"),
            check_vma=False,
        )(stored, source_owner, doc_ids, doc_starts, wq, wk, wv)

    return program
```

```python
import functools

import jax
import jax.numpy as jnp
import numpy as np
from jax import lax
from jax.experimental import pallas as pl
from jax.experimental.pallas import tpu as pltpu
from jax.sharding import PartitionSpec as P

HEAD_SIZE = 128
LANES = 128
ROPE_BASE = 500000.0
OTHER = -(2.0**100)

VMEM_SPEC = pl.BlockSpec(memory_space=pltpu.VMEM)
SMEM_SPEC = pl.BlockSpec(memory_space=pltpu.SMEM)


def dot(a, b):
    return jnp.dot(a, b, preferred_element_type=jnp.float32)


def dot_rows(a, b):
    return lax.dot_general(
        a, b, (((1,), (1,)), ((), ())), preferred_element_type=jnp.float32
    )


def call(kernel, out_shape, operands, scratch=(), flops=0, smem=(), vmem=24):
    specs = [SMEM_SPEC if at in smem else VMEM_SPEC for at in range(len(operands))]
    many = isinstance(out_shape, (list, tuple))
    outs = out_shape if many else [out_shape]
    moved = sum(x.size * x.dtype.itemsize for x in [*operands, *outs])
    return pl.pallas_call(
        kernel,
        out_shape=out_shape,
        in_specs=specs,
        out_specs=[VMEM_SPEC] * len(out_shape) if many else VMEM_SPEC,
        scratch_shapes=list(scratch),
        compiler_params=pltpu.CompilerParams(vmem_limit_bytes=vmem * 2**20),
        cost_estimate=pl.CostEstimate(flops=flops, bytes_accessed=moved, transcendentals=0),
    )(*operands)


def weights_kernel(far, wq, wk, wv, *outs):
    groups = far.shape[0]
    parts = len(outs) // groups - 1
    width = outs[0].shape[1]
    for step in range(groups):
        start = pl.multiple_of(far[step] * HEAD_SIZE, HEAD_SIZE)
        outs[step][:, :HEAD_SIZE] = wk[:, pl.ds(start, HEAD_SIZE)]
        outs[step][:, HEAD_SIZE:] = wv[:, pl.ds(start, HEAD_SIZE)]
        for part in range(parts):
            start = pl.multiple_of((far[step] * parts + part) * width, width)
            outs[(part + 1) * groups + step][...] = wq[:, pl.ds(start, width)]


def assemble_kernel(far, *refs):
    out = refs[-1]
    for step, piece in enumerate(refs[:-1]):
        rows = piece.shape[0]
        out[pl.ds(pl.multiple_of(far[step] * rows, rows), rows), :] = piece[...]


def places_kernel(cap, mine, order, mate, twist, doc_starts, owners, freqs, *refs):
    angles, key_hot, query_bar, slots, columns, coded, starts, local = refs
    shards, rows = owners.shape
    groups = mine.shape[0]
    team = shards // groups
    span = groups * cap
    owner_at = lax.broadcasted_iota(jnp.int32, (shards, rows), 0)
    upper = jnp.where(
        lax.broadcasted_iota(jnp.int32, (rows, rows), 0)
        < lax.broadcasted_iota(jnp.int32, (rows, rows), 1),
        1.0,
        0.0,
    ).astype(jnp.bfloat16)
    rank_at = lax.broadcasted_iota(jnp.int32, (rows, rows), 0).astype(jnp.float32)
    lane = lax.broadcasted_iota(jnp.int32, (1, rows), 1).astype(jnp.float32)
    before = jnp.zeros((shards, 1), jnp.float32)
    found = jnp.zeros((3 * shards, rows), jnp.float32)
    for shard in range(shards):
        hot = jnp.where(owners[shard : shard + 1, :] == owner_at, 1.0, 0.0)
        within = dot(hot.astype(jnp.bfloat16), upper)
        local[shard : shard + 1, :] = jnp.sum(hot * within, axis=0, keepdims=True)
        rank = jnp.sum(hot * (within + before), axis=0, keepdims=True)
        before = before + jnp.sum(hot, axis=1, keepdims=True)
        rank_hot = jnp.where(rank_at == rank, 1.0, 0.0).astype(jnp.bfloat16)
        codes = jnp.concatenate([hot * float(shard), hot * lane, hot * within], axis=0)
        found = found + dot_rows(codes.astype(jnp.bfloat16), rank_hot)
    shard_of = found[:shards]
    place = shard_of * rows + found[shards : 2 * shards]
    docs = doc_starts.shape[0]
    doc_lane = lax.broadcasted_iota(jnp.int32, (1, LANES), 1)
    doc_row = jnp.full((1, LANES), -1.0, jnp.float32)
    start = jnp.zeros_like(place)
    for doc in range(docs):
        value = doc_starts[doc].astype(jnp.float32)
        start = jnp.maximum(start, jnp.where(value <= place, value, 0.0))
        doc_row = jnp.where(doc_lane == doc, value, doc_row)
    to_shard = shard_of.astype(jnp.int32)
    to_group = jnp.zeros_like(to_shard)
    for group in range(1, groups):
        to_group = jnp.where(to_shard >= group * team, group, to_group)
    to_mate = (to_shard - to_group * team) ^ twist[0]
    inside = found[2 * shards :].astype(jnp.int32)
    coded[...] = (to_mate * groups + to_group) * span + inside
    starts[:shards, :] = start
    starts[shards : 2 * shards, :] = place - start
    flat = jnp.transpose(starts[...])
    which = lax.broadcasted_iota(jnp.int32, flat.shape, 1)
    column = lax.broadcasted_iota(jnp.int32, (rows, 1), 0)
    for group in range(groups):
        own = slice(group * rows, (group + 1) * rows)
        at = mine[group]
        offset = jnp.sum(jnp.where(which == at + shards, flat, 0.0), axis=1, keepdims=True)
        angles[own, :] = offset * freqs[...]
        slots[:, own] = coded[pl.ds(at, 1), :] + group * cap
        shard = group * team + mate[0]
        place = column + shard * rows
        begin = jnp.zeros_like(column)
        for doc in range(docs):
            begin = jnp.where(doc_starts[doc] <= place, doc_starts[doc], begin)
        query_bar[own, :] = jnp.where(begin.astype(jnp.float32) == doc_row, 0.0, OTHER).astype(
            jnp.bfloat16
        )
        owner = owners[pl.ds(shard, 1), :]
        owner_group = jnp.zeros_like(owner)
        for step in range(1, groups):
            owner_group = jnp.where(owner >= step * team, step, owner_group)
        owner_mate = (owner - owner_group * team) ^ twist[0]
        rank = local[pl.ds(shard, 1), :].astype(jnp.int32)
        columns[group : group + 1, :] = owner_mate * span + owner_group * cap + rank
    for block in range(shards):
        own = slice(block * rows, (block + 1) * rows)
        begin = jnp.sum(jnp.where(which == order[block], flat, 0.0), axis=1, keepdims=True)
        key_hot[own, :] = jnp.where(begin == doc_row, 1.0, 0.0).astype(jnp.bfloat16)


def rotate(raw, cosine, sine):
    return raw * cosine + pltpu.roll(raw, HEAD_SIZE // 2, 1) * sine


def project(tokens, weights):
    total = None
    start = 0
    for weight in weights:
        depth = weight.shape[0]
        part = dot(tokens[:, start : start + depth], weight[...])
        total = part if total is None else total + part
        start += depth
    return total


def kv_kernel(layout, places, table, *refs):
    row_blocks, col_chunks, blocks = layout
    count = row_blocks * col_chunks
    pieces, weights = refs[:count], refs[count:-5]
    cosine, sine, tokens, kv, loose = refs[-5:]
    rows, width = pieces[0].shape
    for row in range(row_blocks):
        there = pl.ds(pl.multiple_of(places[row] * rows, rows), rows)
        for col in range(col_chunks):
            loose[there, col * width : (col + 1) * width] = pieces[row * col_chunks + col][...]
    width = loose.shape[1] // blocks
    for block in range(blocks):
        source = pl.ds(pl.multiple_of(table[block] * width, width), width)
        tokens[:, block * width : (block + 1) * width] = loose[:, source]
    total = project(tokens, weights)
    kv[:, :HEAD_SIZE] = rotate(total[:, :HEAD_SIZE], cosine[...], sine[...]).astype(kv.dtype)
    kv[:, HEAD_SIZE:] = total[:, HEAD_SIZE:].astype(kv.dtype)


def query_kernel(parts, tokens, *refs):
    weights = refs[:parts]
    cosine, sine, slots = refs[parts : parts + 3]
    outs, queries = refs[parts + 3 : -1], refs[-1]
    raw = project(tokens, weights)
    for head in range(queries.shape[1] // HEAD_SIZE):
        cols = slice(head * HEAD_SIZE, (head + 1) * HEAD_SIZE)
        queries[:, cols] = rotate(raw[:, cols], cosine[...], sine[...]).astype(queries.dtype)
    count = outs[0].shape[0]
    at = lax.broadcasted_iota(jnp.int32, (count, queries.shape[0]), 0)
    for step, out in enumerate(outs):
        hot = jnp.where(at + step * count == slots[...], 1.0, 0.0).astype(jnp.bfloat16)
        out[...] = dot(hot, queries[...]).astype(out.dtype)


def attention_kernel(layout, far, columns, query_bar, key_hot, *refs):
    query_parts, kv_parts, block_rows = layout
    arrived = refs[:query_parts]
    kvs = refs[query_parts : query_parts + kv_parts]
    outs = refs[query_parts + kv_parts : -5]
    keys, values, long, scores, context = refs[-5:]
    groups, rows = columns.shape
    heads = arrived[0].shape[1] // HEAD_SIZE
    start = 0
    for kv in kvs:
        own = slice(start, start + kv.shape[0])
        keys[own, :HEAD_SIZE] = kv[:, :HEAD_SIZE]
        values[own, :] = kv[:, HEAD_SIZE:]
        start += kv.shape[0]
    keys[:, HEAD_SIZE:] = key_hot[...]
    span = arrived[0].shape[0] // groups
    at = lax.broadcasted_iota(jnp.int32, (span * query_parts, rows), 0)
    for group in range(groups):
        hot = jnp.where(at == columns[group : group + 1, :], 1.0, 0.0).astype(jnp.bfloat16)
        there = slice(group * span, (group + 1) * span)
        slab = jnp.concatenate([part[there, :] for part in arrived], axis=0)
        picked = lax.dot_general(
            hot, slab, (((0,), (0,)), ((), ())), preferred_element_type=jnp.float32
        ).astype(jnp.bfloat16)
        own = slice(group * rows, (group + 1) * rows)
        for head in range(heads):
            long[head, own, :HEAD_SIZE] = picked[:, head * HEAD_SIZE : (head + 1) * HEAD_SIZE]
            long[head, own, HEAD_SIZE:] = query_bar[own, :]
    factor = 1.4426950408889634 / HEAD_SIZE**0.5
    blocks = groups * rows // block_rows
    steps = [(block, head) for block in range(blocks) for head in range(heads)]

    def score(step):
        block, head = steps[step]
        own = slice(block * block_rows, (block + 1) * block_rows)
        scores[step % 2] = dot_rows(long[head, own, :], keys[...])

    score(0)
    for step, (block, head) in enumerate(steps):
        if step + 1 < len(steps):
            score(step + 1)
        own = slice(block * block_rows, (block + 1) * block_rows)
        held = scores[step % 2]
        top = jnp.max(held, axis=1, keepdims=True)
        kept = jnp.exp2((held - top) * factor)
        total = jnp.sum(kept, axis=1, keepdims=True)
        mixed = dot(kept.astype(jnp.bfloat16), values[...])
        context[own, head * HEAD_SIZE : (head + 1) * HEAD_SIZE] = (mixed / total).astype(
            context.dtype
        )
    for step, out in enumerate(outs):
        out[...] = context[pl.ds(pl.multiple_of(far[step] * rows, rows), rows), :]


def finish_kernel(far, *refs):
    out = refs[-1]
    groups = far.shape[0]
    parts = (len(refs) - 1) // groups
    width = refs[0].shape[1]
    for part in range(parts):
        for step in range(groups):
            start = pl.multiple_of((far[step] * parts + part) * width, width)
            out[:, pl.ds(start, width)] = refs[part * groups + step][...]


def turn(value, axis, bits):
    count = lax.axis_size(axis)
    return lax.ppermute(value, axis, [(i, i ^ bits) for i in range(count)])


def spread(value):
    across = turn(value, "team", 2)
    return [value, across, turn(value, "team", 1), turn(across, "team", 1)]


def after(value, *others):
    return lax.optimization_barrier((value, *others))[0]


def body(stored, source_owner, doc_ids, doc_starts, wq, wk, wv):
    groups, team = lax.axis_size("line"), lax.axis_size("team")
    nctx, ntp = groups * team, lax.axis_size("tp")
    group, mate = lax.axis_index("line"), lax.axis_index("team")
    rows = stored.shape[0]
    cap = 2 * rows // nctx
    size = HEAD_SIZE
    depth = wq.shape[0]
    split = groups > 1
    pair = 2 * size
    parts = wq.shape[1] // groups // pair
    total_rows = groups * rows
    width = stored.shape[1] * ntp
    keys = nctx * rows
    far = group ^ jnp.arange(groups, dtype=jnp.int32)

    def flip(value):
        return lax.ppermute(value, "tp", [(0, 1), (1, 0)])

    if split:
        inner, outer = [(1, 2), (2, 1)], [(1, 0), (2, 3)]
        near = turn(stored, "line", 1)
        over = lax.ppermute(stored, "line", inner)
        over_near = lax.ppermute(near, "line", inner)
        end = lax.ppermute(over, "line", outer)
        end_near = lax.ppermute(over_near, "line", outer)
        edge = (group == 0) | (group == groups - 1)
        third = jnp.where(edge, end, over)
        fourth = jnp.where(edge, end_near, over_near)
        places = jnp.stack(
            [group, group ^ 1, group ^ jnp.where(edge, 2, 3), group ^ jnp.where(edge, 3, 2)]
        )
        pieces = [
            chunk for piece in (stored, near, third, fourth) for chunk in (piece, flip(piece))
        ]
        token_steps = [(near, over), (over_near, end), (end_near,)]
        chunks = ntp
    else:
        pieces = [lax.all_gather(stored, "tp", axis=1, tiled=True)]
        places = jnp.zeros((1,), jnp.int32)
        chunks = 1

    slabs = call(
        weights_kernel,
        [jax.ShapeDtypeStruct((depth, pair), jnp.bfloat16)] * (groups * (1 + parts)),
        [far, wq, wk, wv],
        smem=(0,),
    )
    sets = []
    for at in range(1 + parts):
        slab = slabs[at * groups : (at + 1) * groups]
        if split:
            if at:
                slab = [after(value, *token_steps[at - 1]) for value in slab]
            moved = [turn(slab[step], "line", step) for step in range(1, groups)]
            held = call(
                assemble_kernel,
                jax.ShapeDtypeStruct((groups * depth, pair), jnp.bfloat16),
                [far, slab[0], *moved],
                smem=(0,),
            )
            sets.append(spread(held))
        else:
            sets.append([lax.all_gather(slab[0], "team", axis=0, tiled=True)])

    if split:
        rel = jnp.arange(groups, dtype=jnp.int32)
        turns = mate ^ jnp.array([0, 2, 1, 3], dtype=jnp.int32)
        order = (rel[None, :] * team + turns[:, None]).reshape(-1)
        mine = rel * team + mate
        twist = mate[None]
        share = nctx // ntp
        table = order % share + jnp.where(order // share == lax.axis_index("tp"), 0, share)
    else:
        order = jnp.arange(nctx, dtype=jnp.int32)
        mine = mate[None]
        twist = table = jnp.zeros((1,), jnp.int32)

    owners = lax.all_to_all(
        jnp.broadcast_to(source_owner[None, :], (nctx, rows)), ("line", "team"), 0, 0, tiled=True
    )
    freqs = ROPE_BASE ** (-np.arange(size // 2) * 2.0 / size)
    freqs = jnp.asarray(np.concatenate([freqs, freqs])[None, :], jnp.float32)
    sign = jnp.asarray(np.repeat([-1.0, 1.0], size // 2)[None, :], jnp.float32)
    angles, key_hot, query_bar, slots, columns = call(
        functools.partial(places_kernel, cap),
        [
            jax.ShapeDtypeStruct((total_rows, size), jnp.float32),
            jax.ShapeDtypeStruct((keys, LANES), jnp.bfloat16),
            jax.ShapeDtypeStruct((total_rows, LANES), jnp.bfloat16),
            jax.ShapeDtypeStruct((1, total_rows), jnp.int32),
            jax.ShapeDtypeStruct((groups, rows), jnp.int32),
        ],
        [mine, order, mate[None], twist, doc_starts, owners, freqs],
        scratch=[
            pltpu.VMEM((nctx, rows), jnp.int32),
            pltpu.VMEM((max(2 * nctx, LANES), rows), jnp.float32),
            pltpu.VMEM((nctx, rows), jnp.float32),
        ],
        flops=10**9,
        smem=(0, 1, 2, 3, 4),
    )
    cosine = jnp.cos(angles)
    sine = jnp.sin(angles) * sign

    tokens, kv = call(
        functools.partial(kv_kernel, (groups, chunks, nctx if split else 1)),
        [
            jax.ShapeDtypeStruct((total_rows, width), jnp.bfloat16),
            jax.ShapeDtypeStruct((total_rows, pair), jnp.bfloat16),
        ],
        [places, table, *pieces, *sets[0], cosine, sine],
        scratch=[pltpu.VMEM((total_rows, width), jnp.bfloat16)],
        flops=2 * total_rows * width * pair,
        smem=(0, 1),
        vmem=28,
    )
    kvs = spread(kv) if split else [lax.all_gather(kv, "team", axis=0, tiled=True)]

    block_rows = min(2 * rows, total_rows)
    lanes_out = team if split else 1
    slot_count = nctx * groups * cap
    ready = []
    for part in range(parts):
        leaving = call(
            functools.partial(query_kernel, len(sets[1 + part])),
            [jax.ShapeDtypeStruct((slot_count // lanes_out, pair), jnp.bfloat16)] * lanes_out,
            [tokens, *sets[1 + part], cosine, sine, slots],
            scratch=[pltpu.VMEM((total_rows, pair), jnp.bfloat16)],
            flops=2 * total_rows * (width + slot_count) * pair,
        )
        if split:
            arrived = [leaving[0]] + [turn(leaving[e], "team", e) for e in range(1, team)]
        else:
            arrived = [lax.all_to_all(leaving[0], "team", 0, 0, tiled=True)]
        context = call(
            functools.partial(attention_kernel, (len(arrived), len(kvs), block_rows)),
            [jax.ShapeDtypeStruct((rows, pair), jnp.bfloat16)] * groups,
            [far, columns, query_bar, key_hot, *arrived, *kvs],
            scratch=[
                pltpu.VMEM((keys, size + LANES), jnp.bfloat16),
                pltpu.VMEM((keys, size), jnp.bfloat16),
                pltpu.VMEM((pair // size, total_rows, size + LANES), jnp.bfloat16),
                pltpu.VMEM((2, block_rows, keys), jnp.float32),
                pltpu.VMEM((total_rows, pair), jnp.bfloat16),
            ],
            flops=8 * total_rows * pair * keys,
            smem=(0,),
            vmem=40,
        )
        ready += [context[0]] + [turn(context[step], "line", step) for step in range(1, groups)]

    return call(
        finish_kernel,
        jax.ShapeDtypeStruct((rows, wq.shape[1]), jnp.bfloat16),
        [far, *ready],
        smem=(0,),
    )


def solution(mesh):
    def program(stored, source_owner, doc_ids, doc_starts, wq, wk, wv):
        ctx, tp = mesh.shape["ctx"], mesh.shape["tp"]
        groups = wk.shape[1] // HEAD_SIZE // tp
        parts = jax.sharding.Mesh(
            mesh.devices.reshape(groups, ctx // groups, tp), ("line", "team", "tp")
        )
        both = ("line", "team")
        return jax.shard_map(
            body,
            mesh=parts,
            in_specs=(
                P(both, "tp"),
                P(both),
                P(both),
                P(),
                P(both, "tp"),
                P(both, "tp"),
                P(both, "tp"),
            ),
            out_specs=P(both, "tp"),
            check_vma=False,
        )(stored, source_owner, doc_ids, doc_starts, wq, wk, wv)

    return program
```

```python
import functools

import jax
import jax.numpy as jnp
import numpy as np
from jax import lax
from jax.experimental import pallas as pl
from jax.experimental.pallas import tpu as pltpu
from jax.sharding import PartitionSpec as P

HEAD_SIZE = 128
LANES = 128
ROPE_BASE = 500000.0
OTHER = -(2.0**100)

VMEM_SPEC = pl.BlockSpec(memory_space=pltpu.VMEM)
SMEM_SPEC = pl.BlockSpec(memory_space=pltpu.SMEM)


def dot(a, b):
    return jnp.dot(a, b, preferred_element_type=jnp.float32)


def dot_rows(a, b):
    return lax.dot_general(
        a, b, (((1,), (1,)), ((), ())), preferred_element_type=jnp.float32
    )


def call(kernel, out_shape, operands, scratch=(), flops=0, smem=(), vmem=24):
    specs = [SMEM_SPEC if at in smem else VMEM_SPEC for at in range(len(operands))]
    many = isinstance(out_shape, (list, tuple))
    outs = out_shape if many else [out_shape]
    moved = sum(x.size * x.dtype.itemsize for x in [*operands, *outs])
    return pl.pallas_call(
        kernel,
        out_shape=out_shape,
        in_specs=specs,
        out_specs=[VMEM_SPEC] * len(out_shape) if many else VMEM_SPEC,
        scratch_shapes=list(scratch),
        compiler_params=pltpu.CompilerParams(vmem_limit_bytes=vmem * 2**20),
        cost_estimate=pl.CostEstimate(flops=flops, bytes_accessed=moved, transcendentals=0),
    )(*operands)


def weights_kernel(far, wq, wk, wv, *outs):
    groups = far.shape[0]
    parts = len(outs) // groups - 1
    width = outs[0].shape[1]
    for step in range(groups):
        start = pl.multiple_of(far[step] * HEAD_SIZE, HEAD_SIZE)
        outs[step][:, :HEAD_SIZE] = wk[:, pl.ds(start, HEAD_SIZE)]
        outs[step][:, HEAD_SIZE:] = wv[:, pl.ds(start, HEAD_SIZE)]
        for part in range(parts):
            start = pl.multiple_of((far[step] * parts + part) * width, width)
            outs[(part + 1) * groups + step][...] = wq[:, pl.ds(start, width)]


def assemble_kernel(far, *refs):
    out = refs[-1]
    for step, piece in enumerate(refs[:-1]):
        rows = piece.shape[0]
        out[pl.ds(pl.multiple_of(far[step] * rows, rows), rows), :] = piece[...]


def places_kernel(cap, mine, order, mate, twist, doc_starts, owners, freqs, *refs):
    angles, key_hot, query_bar, slots, columns, coded, starts, local = refs
    shards, rows = owners.shape
    groups = mine.shape[0]
    team = shards // groups
    span = groups * cap
    owner_at = lax.broadcasted_iota(jnp.int32, (shards, rows), 0)
    upper = jnp.where(
        lax.broadcasted_iota(jnp.int32, (rows, rows), 0)
        < lax.broadcasted_iota(jnp.int32, (rows, rows), 1),
        1.0,
        0.0,
    ).astype(jnp.bfloat16)
    rank_at = lax.broadcasted_iota(jnp.int32, (rows, rows), 0).astype(jnp.float32)
    lane = lax.broadcasted_iota(jnp.int32, (1, rows), 1).astype(jnp.float32)
    before = jnp.zeros((shards, 1), jnp.float32)
    found = jnp.zeros((3 * shards, rows), jnp.float32)
    for shard in range(shards):
        hot = jnp.where(owners[shard : shard + 1, :] == owner_at, 1.0, 0.0)
        within = dot(hot.astype(jnp.bfloat16), upper)
        local[shard : shard + 1, :] = jnp.sum(hot * within, axis=0, keepdims=True)
        rank = jnp.sum(hot * (within + before), axis=0, keepdims=True)
        before = before + jnp.sum(hot, axis=1, keepdims=True)
        rank_hot = jnp.where(rank_at == rank, 1.0, 0.0).astype(jnp.bfloat16)
        codes = jnp.concatenate([hot * float(shard), hot * lane, hot * within], axis=0)
        found = found + dot_rows(codes.astype(jnp.bfloat16), rank_hot)
    shard_of = found[:shards]
    place = shard_of * rows + found[shards : 2 * shards]
    docs = doc_starts.shape[0]
    doc_lane = lax.broadcasted_iota(jnp.int32, (1, LANES), 1)
    doc_row = jnp.full((1, LANES), -1.0, jnp.float32)
    start = jnp.zeros_like(place)
    for doc in range(docs):
        value = doc_starts[doc].astype(jnp.float32)
        start = jnp.maximum(start, jnp.where(value <= place, value, 0.0))
        doc_row = jnp.where(doc_lane == doc, value, doc_row)
    to_shard = shard_of.astype(jnp.int32)
    to_group = jnp.zeros_like(to_shard)
    for group in range(1, groups):
        to_group = jnp.where(to_shard >= group * team, group, to_group)
    to_mate = (to_shard - to_group * team) ^ twist[0]
    inside = found[2 * shards :].astype(jnp.int32)
    coded[...] = (to_mate * groups + to_group) * span + inside
    starts[:shards, :] = start
    starts[shards : 2 * shards, :] = place - start
    flat = jnp.transpose(starts[...])
    which = lax.broadcasted_iota(jnp.int32, flat.shape, 1)
    column = lax.broadcasted_iota(jnp.int32, (rows, 1), 0)
    for group in range(groups):
        own = slice(group * rows, (group + 1) * rows)
        at = mine[group]
        offset = jnp.sum(jnp.where(which == at + shards, flat, 0.0), axis=1, keepdims=True)
        angles[own, :] = offset * freqs[...]
        slots[:, own] = coded[pl.ds(at, 1), :] + group * cap
        shard = group * team + mate[0]
        place = column + shard * rows
        begin = jnp.zeros_like(column)
        for doc in range(docs):
            begin = jnp.where(doc_starts[doc] <= place, doc_starts[doc], begin)
        query_bar[own, :] = jnp.where(begin.astype(jnp.float32) == doc_row, 0.0, OTHER).astype(
            jnp.bfloat16
        )
        owner = owners[pl.ds(shard, 1), :]
        owner_group = jnp.zeros_like(owner)
        for step in range(1, groups):
            owner_group = jnp.where(owner >= step * team, step, owner_group)
        owner_mate = (owner - owner_group * team) ^ twist[0]
        rank = local[pl.ds(shard, 1), :].astype(jnp.int32)
        columns[group : group + 1, :] = owner_mate * span + owner_group * cap + rank
    for block in range(shards):
        own = slice(block * rows, (block + 1) * rows)
        begin = jnp.sum(jnp.where(which == order[block], flat, 0.0), axis=1, keepdims=True)
        key_hot[own, :] = jnp.where(begin == doc_row, 1.0, 0.0).astype(jnp.bfloat16)


def rotate(raw, cosine, sine):
    return raw * cosine + pltpu.roll(raw, HEAD_SIZE // 2, 1) * sine


def project(tokens, weights):
    total = None
    start = 0
    for weight in weights:
        depth = weight.shape[0]
        part = dot(tokens[:, start : start + depth], weight[...])
        total = part if total is None else total + part
        start += depth
    return total


def kv_kernel(layout, places, table, *refs):
    row_blocks, col_chunks, blocks = layout
    count = row_blocks * col_chunks
    pieces, weights = refs[:count], refs[count:-5]
    cosine, sine, tokens, kv, loose = refs[-5:]
    rows, width = pieces[0].shape
    for row in range(row_blocks):
        there = pl.ds(pl.multiple_of(places[row] * rows, rows), rows)
        for col in range(col_chunks):
            loose[there, col * width : (col + 1) * width] = pieces[row * col_chunks + col][...]
    width = loose.shape[1] // blocks
    for block in range(blocks):
        source = pl.ds(pl.multiple_of(table[block] * width, width), width)
        tokens[:, block * width : (block + 1) * width] = loose[:, source]
    total = project(tokens, weights)
    kv[:, :HEAD_SIZE] = rotate(total[:, :HEAD_SIZE], cosine[...], sine[...]).astype(kv.dtype)
    kv[:, HEAD_SIZE:] = total[:, HEAD_SIZE:].astype(kv.dtype)


def query_kernel(parts, tokens, *refs):
    weights = refs[:parts]
    cosine, sine, slots = refs[parts : parts + 3]
    outs, queries = refs[parts + 3 : -1], refs[-1]
    raw = project(tokens, weights)
    for head in range(queries.shape[1] // HEAD_SIZE):
        cols = slice(head * HEAD_SIZE, (head + 1) * HEAD_SIZE)
        queries[:, cols] = rotate(raw[:, cols], cosine[...], sine[...]).astype(queries.dtype)
    count = outs[0].shape[0]
    at = lax.broadcasted_iota(jnp.int32, (count, queries.shape[0]), 0)
    for step, out in enumerate(outs):
        hot = jnp.where(at + step * count == slots[...], 1.0, 0.0).astype(jnp.bfloat16)
        out[...] = dot(hot, queries[...]).astype(out.dtype)


def attention_kernel(layout, far, columns, query_bar, key_hot, *refs):
    query_parts, kv_parts, block_rows = layout
    arrived = refs[:query_parts]
    kvs = refs[query_parts : query_parts + kv_parts]
    outs = refs[query_parts + kv_parts : -5]
    keys, values, long, scores, context = refs[-5:]
    groups, rows = columns.shape
    heads = arrived[0].shape[1] // HEAD_SIZE
    start = 0
    for kv in kvs:
        own = slice(start, start + kv.shape[0])
        keys[own, :HEAD_SIZE] = kv[:, :HEAD_SIZE]
        values[own, :] = kv[:, HEAD_SIZE:]
        start += kv.shape[0]
    keys[:, HEAD_SIZE:] = key_hot[...]
    span = arrived[0].shape[0] // groups
    at = lax.broadcasted_iota(jnp.int32, (span * query_parts, rows), 0)
    for group in range(groups):
        hot = jnp.where(at == columns[group : group + 1, :], 1.0, 0.0).astype(jnp.bfloat16)
        there = slice(group * span, (group + 1) * span)
        slab = jnp.concatenate([part[there, :] for part in arrived], axis=0)
        picked = lax.dot_general(
            hot, slab, (((0,), (0,)), ((), ())), preferred_element_type=jnp.float32
        ).astype(jnp.bfloat16)
        own = slice(group * rows, (group + 1) * rows)
        for head in range(heads):
            long[head, own, :HEAD_SIZE] = picked[:, head * HEAD_SIZE : (head + 1) * HEAD_SIZE]
            long[head, own, HEAD_SIZE:] = query_bar[own, :]
    factor = 1.4426950408889634 / HEAD_SIZE**0.5
    blocks = groups * rows // block_rows
    steps = [(block, head) for block in range(blocks) for head in range(heads)]

    def score(step):
        block, head = steps[step]
        own = slice(block * block_rows, (block + 1) * block_rows)
        scores[step % 2] = dot_rows(long[head, own, :], keys[...])

    score(0)
    for step, (block, head) in enumerate(steps):
        if step + 1 < len(steps):
            score(step + 1)
        own = slice(block * block_rows, (block + 1) * block_rows)
        held = scores[step % 2]
        top = jnp.max(held, axis=1, keepdims=True)
        kept = jnp.exp2((held - top) * factor)
        total = jnp.sum(kept, axis=1, keepdims=True)
        mixed = dot(kept.astype(jnp.bfloat16), values[...])
        context[own, head * HEAD_SIZE : (head + 1) * HEAD_SIZE] = (mixed / total).astype(
            context.dtype
        )
    for step, out in enumerate(outs):
        out[...] = context[pl.ds(pl.multiple_of(far[step] * rows, rows), rows), :]


def finish_kernel(far, *refs):
    out = refs[-1]
    groups = far.shape[0]
    parts = (len(refs) - 1) // groups
    width = refs[0].shape[1]
    for part in range(parts):
        for step in range(groups):
            start = pl.multiple_of((far[step] * parts + part) * width, width)
            out[:, pl.ds(start, width)] = refs[part * groups + step][...]


def turn(value, axis, bits):
    count = lax.axis_size(axis)
    return lax.ppermute(value, axis, [(i, i ^ bits) for i in range(count)])


def spread(value):
    across = turn(value, "team", 2)
    return [value, across, turn(value, "team", 1), turn(across, "team", 1)]


def after(value, *others):
    return lax.optimization_barrier((value, *others))[0]


def body(stored, source_owner, doc_ids, doc_starts, wq, wk, wv):
    groups, team = lax.axis_size("line"), lax.axis_size("team")
    nctx, ntp = groups * team, lax.axis_size("tp")
    group, mate = lax.axis_index("line"), lax.axis_index("team")
    rows = stored.shape[0]
    cap = 2 * rows // nctx
    size = HEAD_SIZE
    depth = wq.shape[0]
    split = groups > 1
    pair = 2 * size
    parts = wq.shape[1] // groups // pair
    total_rows = groups * rows
    width = stored.shape[1] * ntp
    keys = nctx * rows
    far = group ^ jnp.arange(groups, dtype=jnp.int32)

    def flip(value):
        return lax.ppermute(value, "tp", [(0, 1), (1, 0)])

    slabs = call(
        weights_kernel,
        [jax.ShapeDtypeStruct((depth, pair), jnp.bfloat16)] * (groups * (1 + parts)),
        [far, wq, wk, wv],
        smem=(0,),
    )
    slabs = [slabs[at * groups : (at + 1) * groups] for at in range(1 + parts)]

    if split:
        inner, outer = [(1, 2), (2, 1)], [(1, 0), (2, 3)]
        near = turn(stored, "line", 1)
        over = lax.ppermute(stored, "line", inner)
        flips = [flip(stored)]
        flips.append(flip(after(near, flips[0])))
        over_near = lax.ppermute(after(near, over, flips[0]), "line", inner)
        end = lax.ppermute(after(over, near), "line", outer)
        edge = (group == 0) | (group == groups - 1)
        third = jnp.where(edge, end, over)
        flips.append(flip(after(third, flips[1])))
        end_near = lax.ppermute(after(over_near, flips[1]), "line", outer)
        fourth = jnp.where(edge, end_near, over_near)
        flips.append(flip(after(fourth, flips[2])))
        places = jnp.stack(
            [group, group ^ 1, group ^ jnp.where(edge, 2, 3), group ^ jnp.where(edge, 3, 2)]
        )
        pieces = [
            chunk for both in zip((stored, near, third, fourth), flips) for chunk in both
        ]
        chunks = ntp

        moved = []

        def move(at, step, *others):
            earlier = moved[-2:-1]
            moved.append(turn(after(slabs[at][step], *earlier, *others), "line", step))
            return moved[-1]

        def assemble(at, *steps):
            return call(
                assemble_kernel,
                jax.ShapeDtypeStruct((groups * depth, pair), jnp.bfloat16),
                [far, slabs[at][0], *steps],
                smem=(0,),
            )

        sets = []
        first = move(0, 1)
        second = move(0, 2, near, over, flips[0])
        sets.append(spread(assemble(0, first, second, move(0, 3))))
        first = move(1, 1, over_near, end, flips[1])
        second = move(1, 2)
        held = assemble(1, first, second, move(1, 3, end_near))
        sets.append(spread(after(held, sets[0][1])))
        first = move(2, 1, flips[2])
        second = move(2, 2, sets[0][1])
        last_held = assemble(2, first, second, move(2, 3, flips[3]))
    else:
        pieces = [lax.all_gather(stored, "tp", axis=1, tiled=True)]
        places = jnp.zeros((1,), jnp.int32)
        chunks = 1
        sets = [[lax.all_gather(slab[0], "team", axis=0, tiled=True)] for slab in slabs]

    if split:
        rel = jnp.arange(groups, dtype=jnp.int32)
        turns = mate ^ jnp.array([0, 2, 1, 3], dtype=jnp.int32)
        order = (rel[None, :] * team + turns[:, None]).reshape(-1)
        mine = rel * team + mate
        twist = mate[None]
        share = nctx // ntp
        table = order % share + jnp.where(order // share == lax.axis_index("tp"), 0, share)
    else:
        order = jnp.arange(nctx, dtype=jnp.int32)
        mine = mate[None]
        twist = table = jnp.zeros((1,), jnp.int32)

    owners = lax.all_to_all(
        jnp.broadcast_to(source_owner[None, :], (nctx, rows)), ("line", "team"), 0, 0, tiled=True
    )
    freqs = ROPE_BASE ** (-np.arange(size // 2) * 2.0 / size)
    freqs = jnp.asarray(np.concatenate([freqs, freqs])[None, :], jnp.float32)
    sign = jnp.asarray(np.repeat([-1.0, 1.0], size // 2)[None, :], jnp.float32)
    angles, key_hot, query_bar, slots, columns = call(
        functools.partial(places_kernel, cap),
        [
            jax.ShapeDtypeStruct((total_rows, size), jnp.float32),
            jax.ShapeDtypeStruct((keys, LANES), jnp.bfloat16),
            jax.ShapeDtypeStruct((total_rows, LANES), jnp.bfloat16),
            jax.ShapeDtypeStruct((1, total_rows), jnp.int32),
            jax.ShapeDtypeStruct((groups, rows), jnp.int32),
        ],
        [mine, order, mate[None], twist, doc_starts, owners, freqs],
        scratch=[
            pltpu.VMEM((nctx, rows), jnp.int32),
            pltpu.VMEM((max(2 * nctx, LANES), rows), jnp.float32),
            pltpu.VMEM((nctx, rows), jnp.float32),
        ],
        flops=10**9,
        smem=(0, 1, 2, 3, 4),
    )
    cosine = jnp.cos(angles)
    sine = jnp.sin(angles) * sign

    tokens, kv = call(
        functools.partial(kv_kernel, (groups, chunks, nctx if split else 1)),
        [
            jax.ShapeDtypeStruct((total_rows, width), jnp.bfloat16),
            jax.ShapeDtypeStruct((total_rows, pair), jnp.bfloat16),
        ],
        [places, table, *pieces, *sets[0], cosine, sine],
        scratch=[pltpu.VMEM((total_rows, width), jnp.bfloat16)],
        flops=2 * total_rows * width * pair,
        smem=(0, 1),
        vmem=28,
    )
    block_rows = min(2 * rows, total_rows)
    lanes_out = team if split else 1
    slot_count = nctx * groups * cap

    def project_part(part):
        return call(
            functools.partial(query_kernel, len(sets[1 + part])),
            [jax.ShapeDtypeStruct((slot_count // lanes_out, pair), jnp.bfloat16)] * lanes_out,
            [tokens, *sets[1 + part], cosine, sine, slots],
            scratch=[pltpu.VMEM((total_rows, pair), jnp.bfloat16)],
            flops=2 * total_rows * (width + slot_count) * pair,
        )

    def attend(arrived):
        context = call(
            functools.partial(attention_kernel, (len(arrived), len(kvs), block_rows)),
            [jax.ShapeDtypeStruct((rows, pair), jnp.bfloat16)] * groups,
            [far, columns, query_bar, key_hot, *arrived, *kvs],
            scratch=[
                pltpu.VMEM((keys, size + LANES), jnp.bfloat16),
                pltpu.VMEM((keys, size), jnp.bfloat16),
                pltpu.VMEM((pair // size, total_rows, size + LANES), jnp.bfloat16),
                pltpu.VMEM((2, block_rows, keys), jnp.float32),
                pltpu.VMEM((total_rows, pair), jnp.bfloat16),
            ],
            flops=8 * total_rows * pair * keys,
            smem=(0,),
            vmem=40,
        )
        return [context[0]] + [turn(context[step], "line", step) for step in range(1, groups)]

    def exchange(leaving):
        if split:
            return [leaving[0]] + [turn(leaving[e], "team", e) for e in range(1, team)]
        return [lax.all_to_all(leaving[0], "team", 0, 0, tiled=True)]

    if split:
        sets.append(spread(after(last_held, sets[1][1], kv)))
        leaving = project_part(0)
        across = turn(kv, "team", 2)
        kvs = [kv, across, turn(kv, "team", 1), turn(after(across, leaving[0]), "team", 1)]
    else:
        kvs = [lax.all_gather(kv, "team", axis=0, tiled=True)]
        leaving = project_part(0)
    arrived = [exchange(leaving)] + [exchange(project_part(part)) for part in range(1, parts)]
    ready = [piece for queries in arrived for piece in attend(queries)]

    return call(
        finish_kernel,
        jax.ShapeDtypeStruct((rows, wq.shape[1]), jnp.bfloat16),
        [far, *ready],
        smem=(0,),
    )


def solution(mesh):
    def program(stored, source_owner, doc_ids, doc_starts, wq, wk, wv):
        ctx, tp = mesh.shape["ctx"], mesh.shape["tp"]
        groups = wk.shape[1] // HEAD_SIZE // tp
        parts = jax.sharding.Mesh(
            mesh.devices.reshape(groups, ctx // groups, tp), ("line", "team", "tp")
        )
        both = ("line", "team")
        return jax.shard_map(
            body,
            mesh=parts,
            in_specs=(
                P(both, "tp"),
                P(both),
                P(both),
                P(),
                P(both, "tp"),
                P(both, "tp"),
                P(both, "tp"),
            ),
            out_specs=P(both, "tp"),
            check_vma=False,
        )(stored, source_owner, doc_ids, doc_starts, wq, wk, wv)

    return program
```

```python
import functools

import jax
import jax.numpy as jnp
import numpy as np
from jax import lax
from jax.experimental import pallas as pl
from jax.experimental.pallas import tpu as pltpu
from jax.sharding import PartitionSpec as P

HEAD_SIZE = 128
LANES = 128
ROPE_BASE = 500000.0
OTHER = -(2.0**100)

VMEM_SPEC = pl.BlockSpec(memory_space=pltpu.VMEM)
SMEM_SPEC = pl.BlockSpec(memory_space=pltpu.SMEM)


def dot(a, b):
    return jnp.dot(a, b, preferred_element_type=jnp.float32)


def dot_rows(a, b):
    return lax.dot_general(
        a, b, (((1,), (1,)), ((), ())), preferred_element_type=jnp.float32
    )


def call(kernel, out_shape, operands, scratch=(), flops=0, smem=(), vmem=24):
    specs = [SMEM_SPEC if at in smem else VMEM_SPEC for at in range(len(operands))]
    many = isinstance(out_shape, (list, tuple))
    outs = out_shape if many else [out_shape]
    moved = sum(x.size * x.dtype.itemsize for x in [*operands, *outs])
    return pl.pallas_call(
        kernel,
        out_shape=out_shape,
        in_specs=specs,
        out_specs=[VMEM_SPEC] * len(out_shape) if many else VMEM_SPEC,
        scratch_shapes=list(scratch),
        compiler_params=pltpu.CompilerParams(vmem_limit_bytes=vmem * 2**20),
        cost_estimate=pl.CostEstimate(flops=flops, bytes_accessed=moved, transcendentals=0),
    )(*operands)


def weights_kernel(far, wq, wk, wv, *outs):
    groups = far.shape[0]
    parts = len(outs) // groups - 1
    width = outs[0].shape[1]
    for step in range(groups):
        start = pl.multiple_of(far[step] * HEAD_SIZE, HEAD_SIZE)
        outs[step][:, :HEAD_SIZE] = wk[:, pl.ds(start, HEAD_SIZE)]
        outs[step][:, HEAD_SIZE:] = wv[:, pl.ds(start, HEAD_SIZE)]
        for part in range(parts):
            start = pl.multiple_of((far[step] * parts + part) * width, width)
            outs[(part + 1) * groups + step][...] = wq[:, pl.ds(start, width)]


def assemble_kernel(far, *refs):
    out = refs[-1]
    for step, piece in enumerate(refs[:-1]):
        rows = piece.shape[0]
        out[pl.ds(pl.multiple_of(far[step] * rows, rows), rows), :] = piece[...]


def places_kernel(cap, mine, order, mate, twist, doc_starts, owners, freqs, *refs):
    angles, key_hot, query_bar, slots, columns, coded, starts, local = refs
    shards, rows = owners.shape
    groups = mine.shape[0]
    team = shards // groups
    span = groups * cap
    owner_at = lax.broadcasted_iota(jnp.int32, (shards, rows), 0)
    upper = jnp.where(
        lax.broadcasted_iota(jnp.int32, (rows, rows), 0)
        < lax.broadcasted_iota(jnp.int32, (rows, rows), 1),
        1.0,
        0.0,
    ).astype(jnp.bfloat16)
    rank_at = lax.broadcasted_iota(jnp.int32, (rows, rows), 0).astype(jnp.float32)
    lane = lax.broadcasted_iota(jnp.int32, (1, rows), 1).astype(jnp.float32)
    before = jnp.zeros((shards, 1), jnp.float32)
    found = jnp.zeros((3 * shards, rows), jnp.float32)
    for shard in range(shards):
        hot = jnp.where(owners[shard : shard + 1, :] == owner_at, 1.0, 0.0)
        within = dot(hot.astype(jnp.bfloat16), upper)
        local[shard : shard + 1, :] = jnp.sum(hot * within, axis=0, keepdims=True)
        rank = jnp.sum(hot * (within + before), axis=0, keepdims=True)
        before = before + jnp.sum(hot, axis=1, keepdims=True)
        rank_hot = jnp.where(rank_at == rank, 1.0, 0.0).astype(jnp.bfloat16)
        codes = jnp.concatenate([hot * float(shard), hot * lane, hot * within], axis=0)
        found = found + dot_rows(codes.astype(jnp.bfloat16), rank_hot)
    shard_of = found[:shards]
    place = shard_of * rows + found[shards : 2 * shards]
    docs = doc_starts.shape[0]
    doc_lane = lax.broadcasted_iota(jnp.int32, (1, LANES), 1)
    doc_row = jnp.full((1, LANES), -1.0, jnp.float32)
    start = jnp.zeros_like(place)
    for doc in range(docs):
        value = doc_starts[doc].astype(jnp.float32)
        start = jnp.maximum(start, jnp.where(value <= place, value, 0.0))
        doc_row = jnp.where(doc_lane == doc, value, doc_row)
    to_shard = shard_of.astype(jnp.int32)
    to_group = jnp.zeros_like(to_shard)
    for group in range(1, groups):
        to_group = jnp.where(to_shard >= group * team, group, to_group)
    to_mate = (to_shard - to_group * team) ^ twist[0]
    inside = found[2 * shards :].astype(jnp.int32)
    coded[...] = (to_mate * groups + to_group) * span + inside
    starts[:shards, :] = start
    starts[shards : 2 * shards, :] = place - start
    flat = jnp.transpose(starts[...])
    which = lax.broadcasted_iota(jnp.int32, flat.shape, 1)
    column = lax.broadcasted_iota(jnp.int32, (rows, 1), 0)
    for group in range(groups):
        own = slice(group * rows, (group + 1) * rows)
        at = mine[group]
        offset = jnp.sum(jnp.where(which == at + shards, flat, 0.0), axis=1, keepdims=True)
        angles[own, :] = offset * freqs[...]
        slots[:, own] = coded[pl.ds(at, 1), :] + group * cap
        shard = group * team + mate[0]
        place = column + shard * rows
        begin = jnp.zeros_like(column)
        for doc in range(docs):
            begin = jnp.where(doc_starts[doc] <= place, doc_starts[doc], begin)
        query_bar[own, :] = jnp.where(begin.astype(jnp.float32) == doc_row, 0.0, OTHER).astype(
            jnp.bfloat16
        )
        owner = owners[pl.ds(shard, 1), :]
        owner_group = jnp.zeros_like(owner)
        for step in range(1, groups):
            owner_group = jnp.where(owner >= step * team, step, owner_group)
        owner_mate = (owner - owner_group * team) ^ twist[0]
        rank = local[pl.ds(shard, 1), :].astype(jnp.int32)
        columns[group : group + 1, :] = owner_mate * span + owner_group * cap + rank
    for block in range(shards):
        own = slice(block * rows, (block + 1) * rows)
        begin = jnp.sum(jnp.where(which == order[block], flat, 0.0), axis=1, keepdims=True)
        key_hot[own, :] = jnp.where(begin == doc_row, 1.0, 0.0).astype(jnp.bfloat16)


def rotate(raw, cosine, sine):
    return raw * cosine + pltpu.roll(raw, HEAD_SIZE // 2, 1) * sine


def project(tokens, weights):
    total = None
    start = 0
    for weight in weights:
        depth = weight.shape[0]
        part = dot(tokens[:, start : start + depth], weight[...])
        total = part if total is None else total + part
        start += depth
    return total


def kv_kernel(layout, places, table, *refs):
    row_blocks, col_chunks, blocks = layout
    count = row_blocks * col_chunks
    pieces, weights = refs[:count], refs[count:-5]
    cosine, sine, tokens, kv, loose = refs[-5:]
    rows, width = pieces[0].shape
    for row in range(row_blocks):
        there = pl.ds(pl.multiple_of(places[row] * rows, rows), rows)
        for col in range(col_chunks):
            loose[there, col * width : (col + 1) * width] = pieces[row * col_chunks + col][...]
    width = loose.shape[1] // blocks
    for block in range(blocks):
        source = pl.ds(pl.multiple_of(table[block] * width, width), width)
        tokens[:, block * width : (block + 1) * width] = loose[:, source]
    total = project(tokens, weights)
    kv[:, :HEAD_SIZE] = rotate(total[:, :HEAD_SIZE], cosine[...], sine[...]).astype(kv.dtype)
    kv[:, HEAD_SIZE:] = total[:, HEAD_SIZE:].astype(kv.dtype)


def query_kernel(parts, tokens, *refs):
    weights = refs[:parts]
    cosine, sine, slots = refs[parts : parts + 3]
    outs, queries = refs[parts + 3 : -1], refs[-1]
    raw = project(tokens, weights)
    for head in range(queries.shape[1] // HEAD_SIZE):
        cols = slice(head * HEAD_SIZE, (head + 1) * HEAD_SIZE)
        queries[:, cols] = rotate(raw[:, cols], cosine[...], sine[...]).astype(queries.dtype)
    count = outs[0].shape[0]
    at = lax.broadcasted_iota(jnp.int32, (count, queries.shape[0]), 0)
    for step, out in enumerate(outs):
        hot = jnp.where(at + step * count == slots[...], 1.0, 0.0).astype(jnp.bfloat16)
        out[...] = dot(hot, queries[...]).astype(out.dtype)


def attention_kernel(layout, far, columns, query_bar, key_hot, *refs):
    query_parts, kv_parts, block_rows = layout
    arrived = refs[:query_parts]
    kvs = refs[query_parts : query_parts + kv_parts]
    outs = refs[query_parts + kv_parts : -5]
    keys, values, long, scores, context = refs[-5:]
    groups, rows = columns.shape
    heads = arrived[0].shape[1] // HEAD_SIZE
    start = 0
    for kv in kvs:
        own = slice(start, start + kv.shape[0])
        keys[own, :HEAD_SIZE] = kv[:, :HEAD_SIZE]
        values[own, :] = kv[:, HEAD_SIZE:]
        start += kv.shape[0]
    keys[:, HEAD_SIZE:] = key_hot[...]
    span = arrived[0].shape[0] // groups
    at = lax.broadcasted_iota(jnp.int32, (span * query_parts, rows), 0)
    for group in range(groups):
        hot = jnp.where(at == columns[group : group + 1, :], 1.0, 0.0).astype(jnp.bfloat16)
        there = slice(group * span, (group + 1) * span)
        slab = jnp.concatenate([part[there, :] for part in arrived], axis=0)
        picked = lax.dot_general(
            hot, slab, (((0,), (0,)), ((), ())), preferred_element_type=jnp.float32
        ).astype(jnp.bfloat16)
        own = slice(group * rows, (group + 1) * rows)
        for head in range(heads):
            long[head, own, :HEAD_SIZE] = picked[:, head * HEAD_SIZE : (head + 1) * HEAD_SIZE]
            long[head, own, HEAD_SIZE:] = query_bar[own, :]
    factor = 1.4426950408889634 / HEAD_SIZE**0.5
    blocks = groups * rows // block_rows
    steps = [(block, head) for block in range(blocks) for head in range(heads)]

    def score(step):
        block, head = steps[step]
        own = slice(block * block_rows, (block + 1) * block_rows)
        scores[step % 2] = dot_rows(long[head, own, :], keys[...])

    score(0)
    for step, (block, head) in enumerate(steps):
        if step + 1 < len(steps):
            score(step + 1)
        own = slice(block * block_rows, (block + 1) * block_rows)
        held = scores[step % 2]
        top = jnp.max(held, axis=1, keepdims=True)
        kept = jnp.exp2((held - top) * factor)
        total = jnp.sum(kept, axis=1, keepdims=True)
        mixed = dot(kept.astype(jnp.bfloat16), values[...])
        context[own, head * HEAD_SIZE : (head + 1) * HEAD_SIZE] = (mixed / total).astype(
            context.dtype
        )
    for step, out in enumerate(outs):
        out[...] = context[pl.ds(pl.multiple_of(far[step] * rows, rows), rows), :]


def finish_kernel(far, *refs):
    out = refs[-1]
    groups = far.shape[0]
    parts = (len(refs) - 1) // groups
    width = refs[0].shape[1]
    for part in range(parts):
        for step in range(groups):
            start = pl.multiple_of((far[step] * parts + part) * width, width)
            out[:, pl.ds(start, width)] = refs[part * groups + step][...]


def turn(value, axis, bits):
    count = lax.axis_size(axis)
    return lax.ppermute(value, axis, [(i, i ^ bits) for i in range(count)])


def after(value, *others):
    return lax.optimization_barrier((value, *others))[0]


def spread(value, *others):
    across = turn(value, "team", 2)
    last = turn(after(across, *others), "team", 1)
    return [value, across, turn(value, "team", 1), last]


def body(stored, source_owner, doc_ids, doc_starts, wq, wk, wv):
    groups, team = lax.axis_size("line"), lax.axis_size("team")
    nctx, ntp = groups * team, lax.axis_size("tp")
    group, mate = lax.axis_index("line"), lax.axis_index("team")
    rows = stored.shape[0]
    cap = 2 * rows // nctx
    size = HEAD_SIZE
    depth = wq.shape[0]
    split = groups > 1
    pair = 2 * size
    parts = wq.shape[1] // groups // pair
    total_rows = groups * rows
    width = stored.shape[1] * ntp
    keys = nctx * rows
    far = group ^ jnp.arange(groups, dtype=jnp.int32)

    def flip(value):
        return lax.ppermute(value, "tp", [(0, 1), (1, 0)])

    slabs = call(
        weights_kernel,
        [jax.ShapeDtypeStruct((depth, pair), jnp.bfloat16)] * (groups * (1 + parts)),
        [far, wq, wk, wv],
        smem=(0,),
    )
    slabs = [slabs[at * groups : (at + 1) * groups] for at in range(1 + parts)]
    owners = lax.all_to_all(
        jnp.broadcast_to(source_owner[None, :], (nctx, rows)), ("line", "team"), 0, 0, tiled=True
    )

    if split:
        inner, outer = [(1, 2), (2, 1)], [(1, 0), (2, 3)]
        near = turn(stored, "line", 1)
        over = lax.ppermute(stored, "line", inner)
        flips = [flip(stored)]
        flips.append(flip(after(near, flips[0])))
        over_near = lax.ppermute(
            after(near, over, flips[0], owners, *slabs[0]), "line", inner
        )
        end = lax.ppermute(after(over, near), "line", outer)
        edge = (group == 0) | (group == groups - 1)
        third = jnp.where(edge, end, over)
        flips.append(flip(after(third, flips[1])))
        end_near = lax.ppermute(after(over_near, flips[1]), "line", outer)
        fourth = jnp.where(edge, end_near, over_near)
        flips.append(flip(after(fourth, flips[2])))
        places = jnp.stack(
            [group, group ^ 1, group ^ jnp.where(edge, 2, 3), group ^ jnp.where(edge, 3, 2)]
        )
        pieces = [
            chunk for both in zip((stored, near, third, fourth), flips) for chunk in both
        ]
        chunks = ntp

        moved = []

        def move(at, step, *others):
            earlier = moved[-2:-1] if at < parts else ()
            moved.append(turn(after(slabs[at][step], *earlier, *others), "line", step))
            return moved[-1]

        def assemble(at, *steps):
            return call(
                assemble_kernel,
                jax.ShapeDtypeStruct((groups * depth, pair), jnp.bfloat16),
                [far, slabs[at][0], *reversed(steps)],
                smem=(0,),
            )

        sets = []
        level = over_near, end, flips[1]
        held = assemble(0, move(0, 3, *level), move(0, 2, *level), move(0, 1))
        sets.append(spread(held))
        held = assemble(1, move(1, 3), move(1, 2), move(1, 1))
        sets.append(spread(after(held, sets[0][1])))
        level = end_near, flips[2], sets[0][1]
        last_held = assemble(2, *(move(2, step, *level) for step in (3, 2, 1)))
    else:
        pieces = [lax.all_gather(stored, "tp", axis=1, tiled=True)]
        places = jnp.zeros((1,), jnp.int32)
        chunks = 1
        sets = [[lax.all_gather(slab[0], "team", axis=0, tiled=True)] for slab in slabs]

    if split:
        rel = jnp.arange(groups, dtype=jnp.int32)
        turns = mate ^ jnp.array([0, 2, 1, 3], dtype=jnp.int32)
        order = (rel[None, :] * team + turns[:, None]).reshape(-1)
        mine = rel * team + mate
        twist = mate[None]
        share = nctx // ntp
        table = order % share + jnp.where(order // share == lax.axis_index("tp"), 0, share)
    else:
        order = jnp.arange(nctx, dtype=jnp.int32)
        mine = mate[None]
        twist = table = jnp.zeros((1,), jnp.int32)

    freqs = ROPE_BASE ** (-np.arange(size // 2) * 2.0 / size)
    freqs = jnp.asarray(np.concatenate([freqs, freqs])[None, :], jnp.float32)
    sign = jnp.asarray(np.repeat([-1.0, 1.0], size // 2)[None, :], jnp.float32)
    angles, key_hot, query_bar, slots, columns = call(
        functools.partial(places_kernel, cap),
        [
            jax.ShapeDtypeStruct((total_rows, size), jnp.float32),
            jax.ShapeDtypeStruct((keys, LANES), jnp.bfloat16),
            jax.ShapeDtypeStruct((total_rows, LANES), jnp.bfloat16),
            jax.ShapeDtypeStruct((1, total_rows), jnp.int32),
            jax.ShapeDtypeStruct((groups, rows), jnp.int32),
        ],
        [mine, order, mate[None], twist, doc_starts, owners, freqs],
        scratch=[
            pltpu.VMEM((nctx, rows), jnp.int32),
            pltpu.VMEM((max(2 * nctx, LANES), rows), jnp.float32),
            pltpu.VMEM((nctx, rows), jnp.float32),
        ],
        flops=10**9,
        smem=(0, 1, 2, 3, 4),
    )
    cosine = jnp.cos(angles)
    sine = jnp.sin(angles) * sign

    tokens, kv = call(
        functools.partial(kv_kernel, (groups, chunks, nctx if split else 1)),
        [
            jax.ShapeDtypeStruct((total_rows, width), jnp.bfloat16),
            jax.ShapeDtypeStruct((total_rows, pair), jnp.bfloat16),
        ],
        [places, table, *pieces, *sets[0], cosine, sine],
        scratch=[pltpu.VMEM((total_rows, width), jnp.bfloat16)],
        flops=2 * total_rows * width * pair,
        smem=(0, 1),
        vmem=28,
    )
    block_rows = min(2 * rows, total_rows)
    lanes_out = team if split else 1
    slot_count = nctx * groups * cap

    def project_part(part):
        return call(
            functools.partial(query_kernel, len(sets[1 + part])),
            [jax.ShapeDtypeStruct((slot_count // lanes_out, pair), jnp.bfloat16)] * lanes_out,
            [tokens, *sets[1 + part], cosine, sine, slots],
            scratch=[pltpu.VMEM((total_rows, pair), jnp.bfloat16)],
            flops=2 * total_rows * (width + slot_count) * pair,
        )

    def attend(arrived):
        context = call(
            functools.partial(attention_kernel, (len(arrived), len(kvs), block_rows)),
            [jax.ShapeDtypeStruct((rows, pair), jnp.bfloat16)] * groups,
            [far, columns, query_bar, key_hot, *arrived, *kvs],
            scratch=[
                pltpu.VMEM((keys, size + LANES), jnp.bfloat16),
                pltpu.VMEM((keys, size), jnp.bfloat16),
                pltpu.VMEM((pair // size, total_rows, size + LANES), jnp.bfloat16),
                pltpu.VMEM((2, block_rows, keys), jnp.float32),
                pltpu.VMEM((total_rows, pair), jnp.bfloat16),
            ],
            flops=8 * total_rows * pair * keys,
            smem=(0,),
            vmem=40,
        )
        return [context[0]] + [turn(context[step], "line", step) for step in range(1, groups)]

    def exchange(leaving):
        if split:
            return [leaving[0]] + [turn(leaving[e], "team", e) for e in range(1, team)]
        return [lax.all_to_all(leaving[0], "team", 0, 0, tiled=True)]

    if split:
        across = turn(after(kv, last_held), "team", 2)
        leaving = project_part(0)
        last_held = after(last_held, sets[1][1], across)
        sets.append(spread(last_held, leaving[0]))
        kvs = [kv, across, turn(kv, "team", 1), turn(after(across, leaving[0]), "team", 1)]
    else:
        kvs = [lax.all_gather(kv, "team", axis=0, tiled=True)]
        leaving = project_part(0)
    arrived = [exchange(leaving)] + [exchange(project_part(part)) for part in range(1, parts)]
    ready = [piece for queries in arrived for piece in attend(queries)]

    return call(
        finish_kernel,
        jax.ShapeDtypeStruct((rows, wq.shape[1]), jnp.bfloat16),
        [far, *ready],
        smem=(0,),
    )


def solution(mesh):
    def program(stored, source_owner, doc_ids, doc_starts, wq, wk, wv):
        ctx, tp = mesh.shape["ctx"], mesh.shape["tp"]
        groups = wk.shape[1] // HEAD_SIZE // tp
        parts = jax.sharding.Mesh(
            mesh.devices.reshape(groups, ctx // groups, tp), ("line", "team", "tp")
        )
        both = ("line", "team")
        return jax.shard_map(
            body,
            mesh=parts,
            in_specs=(
                P(both, "tp"),
                P(both),
                P(both),
                P(),
                P(both, "tp"),
                P(both, "tp"),
                P(both, "tp"),
            ),
            out_specs=P(both, "tp"),
            check_vma=False,
        )(stored, source_owner, doc_ids, doc_starts, wq, wk, wv)

    return program
```

```python
import functools

import jax
import jax.numpy as jnp
import numpy as np
from jax import lax
from jax.experimental import pallas as pl
from jax.experimental.pallas import tpu as pltpu
from jax.sharding import PartitionSpec as P

HEAD_SIZE = 128
LANES = 128
ROPE_BASE = 500000.0
OTHER = -(2.0**100)

VMEM_SPEC = pl.BlockSpec(memory_space=pltpu.VMEM)
SMEM_SPEC = pl.BlockSpec(memory_space=pltpu.SMEM)


def dot(a, b):
    return jnp.dot(a, b, preferred_element_type=jnp.float32)


def dot_rows(a, b):
    return lax.dot_general(
        a, b, (((1,), (1,)), ((), ())), preferred_element_type=jnp.float32
    )


def call(kernel, out_shape, operands, scratch=(), flops=0, smem=(), vmem=24):
    specs = [SMEM_SPEC if at in smem else VMEM_SPEC for at in range(len(operands))]
    many = isinstance(out_shape, (list, tuple))
    outs = out_shape if many else [out_shape]
    moved = sum(x.size * x.dtype.itemsize for x in [*operands, *outs])
    return pl.pallas_call(
        kernel,
        out_shape=out_shape,
        in_specs=specs,
        out_specs=[VMEM_SPEC] * len(out_shape) if many else VMEM_SPEC,
        scratch_shapes=list(scratch),
        compiler_params=pltpu.CompilerParams(vmem_limit_bytes=vmem * 2**20),
        cost_estimate=pl.CostEstimate(flops=flops, bytes_accessed=moved, transcendentals=0),
    )(*operands)


def weights_kernel(far, owner, wq, wk, wv, *outs):
    groups = far.shape[0]
    depth, width = wq.shape[0], outs[groups].shape[1]
    for step in range(groups):
        start = pl.multiple_of(far[step] * HEAD_SIZE, HEAD_SIZE)
        out = outs[step]
        out[:depth, :HEAD_SIZE] = wk[:, pl.ds(start, HEAD_SIZE)]
        out[:depth, HEAD_SIZE:] = wv[:, pl.ds(start, HEAD_SIZE)]
        below = out.shape[0] - depth
        if below:
            row = jnp.concatenate([owner[...], jnp.zeros_like(owner)], axis=1)
            row = row.astype(jnp.float32).astype(jnp.bfloat16)
            out[depth:, :] = jnp.broadcast_to(row, (below, row.shape[1]))
        start = pl.multiple_of(far[step] * width, width)
        outs[groups + step][...] = wq[:, pl.ds(start, width)]


def assemble_kernel(depth, *refs):
    out = refs[-1]
    pieces = refs[:-1]
    below = pieces[0].shape[0] - depth
    for step, piece in enumerate(pieces):
        out[step * depth : (step + 1) * depth, :] = piece[:depth, :]
        if below:
            start = len(pieces) * depth + step * below
            out[start : start + below, :] = piece[depth:, :]


def places_kernel(cap, mine, order, came, mate, twist, doc_starts, freqs, *refs):
    angles, key_hot, query_bar, slots, columns, coded, starts, local, owners = refs[-9:]
    shards, rows = owners.shape
    sources = refs[:-9]
    if len(sources) == 1:
        owners[...] = sources[0][...]
    else:
        each = shards // len(sources)
        below = sources[0].shape[0] % LANES // each
        for source in range(shards):
            part = sources[source // each]
            row = part.shape[0] - (each - source % each) * below
            value = part[row : row + below, :rows].astype(jnp.float32).astype(jnp.int32)
            owners[pl.ds(came[source], 1), :] = value[:1, :]
    groups = mine.shape[0]
    team = shards // groups
    span = groups * cap
    owner_at = lax.broadcasted_iota(jnp.int32, (shards, rows), 0)
    upper = jnp.where(
        lax.broadcasted_iota(jnp.int32, (rows, rows), 0)
        < lax.broadcasted_iota(jnp.int32, (rows, rows), 1),
        1.0,
        0.0,
    ).astype(jnp.bfloat16)
    rank_at = lax.broadcasted_iota(jnp.int32, (rows, rows), 0).astype(jnp.float32)
    lane = lax.broadcasted_iota(jnp.int32, (1, rows), 1).astype(jnp.float32)
    before = jnp.zeros((shards, 1), jnp.float32)
    found = jnp.zeros((3 * shards, rows), jnp.float32)
    for shard in range(shards):
        hot = jnp.where(owners[shard : shard + 1, :] == owner_at, 1.0, 0.0)
        within = dot(hot.astype(jnp.bfloat16), upper)
        local[shard : shard + 1, :] = jnp.sum(hot * within, axis=0, keepdims=True)
        rank = jnp.sum(hot * (within + before), axis=0, keepdims=True)
        before = before + jnp.sum(hot, axis=1, keepdims=True)
        rank_hot = jnp.where(rank_at == rank, 1.0, 0.0).astype(jnp.bfloat16)
        codes = jnp.concatenate([hot * float(shard), hot * lane, hot * within], axis=0)
        found = found + dot_rows(codes.astype(jnp.bfloat16), rank_hot)
    shard_of = found[:shards]
    place = shard_of * rows + found[shards : 2 * shards]
    docs = doc_starts.shape[0]
    doc_lane = lax.broadcasted_iota(jnp.int32, (1, LANES), 1)
    doc_row = jnp.full((1, LANES), -1.0, jnp.float32)
    start = jnp.zeros_like(place)
    for doc in range(docs):
        value = doc_starts[doc].astype(jnp.float32)
        start = jnp.maximum(start, jnp.where(value <= place, value, 0.0))
        doc_row = jnp.where(doc_lane == doc, value, doc_row)
    to_shard = shard_of.astype(jnp.int32)
    to_group = jnp.zeros_like(to_shard)
    for group in range(1, groups):
        to_group = jnp.where(to_shard >= group * team, group, to_group)
    to_mate = (to_shard - to_group * team) ^ twist[0]
    inside = found[2 * shards :].astype(jnp.int32)
    coded[...] = (to_mate * groups + to_group) * span + inside
    starts[:shards, :] = start
    starts[shards : 2 * shards, :] = place - start
    flat = jnp.transpose(starts[...])
    which = lax.broadcasted_iota(jnp.int32, flat.shape, 1)
    column = lax.broadcasted_iota(jnp.int32, (rows, 1), 0)
    for group in range(groups):
        own = slice(group * rows, (group + 1) * rows)
        at = mine[group]
        offset = jnp.sum(jnp.where(which == at + shards, flat, 0.0), axis=1, keepdims=True)
        angles[own, :] = offset * freqs[...]
        slots[:, own] = coded[pl.ds(at, 1), :] + group * cap
        shard = group * team + mate[0]
        place = column + shard * rows
        begin = jnp.zeros_like(column)
        for doc in range(docs):
            begin = jnp.where(doc_starts[doc] <= place, doc_starts[doc], begin)
        query_bar[own, :] = jnp.where(begin.astype(jnp.float32) == doc_row, 0.0, OTHER).astype(
            jnp.bfloat16
        )
        owner = owners[pl.ds(shard, 1), :]
        owner_group = jnp.zeros_like(owner)
        for step in range(1, groups):
            owner_group = jnp.where(owner >= step * team, step, owner_group)
        owner_mate = (owner - owner_group * team) ^ twist[0]
        rank = local[pl.ds(shard, 1), :].astype(jnp.int32)
        columns[group : group + 1, :] = owner_mate * span + owner_group * cap + rank
    for block in range(shards):
        own = slice(block * rows, (block + 1) * rows)
        begin = jnp.sum(jnp.where(which == order[block], flat, 0.0), axis=1, keepdims=True)
        key_hot[own, :] = jnp.where(begin == doc_row, 1.0, 0.0).astype(jnp.bfloat16)


def rotate(raw, cosine, sine):
    return raw * cosine + pltpu.roll(raw, HEAD_SIZE // 2, 1) * sine


def project(tokens, weights, cols=slice(None)):
    total = None
    start = 0
    for weight in weights:
        depth = weight.shape[0] // LANES * LANES
        part = dot(tokens[:, start : start + depth], weight[:depth, cols])
        total = part if total is None else total + part
        start += depth
    return total


def kv_kernel(layout, places, table, *refs):
    row_blocks, col_chunks, blocks = layout
    count = row_blocks * col_chunks
    pieces, weights = refs[:count], refs[count:-5]
    cosine, sine, tokens, kv, loose = refs[-5:]
    rows, width = pieces[0].shape
    for row in range(row_blocks):
        there = pl.ds(pl.multiple_of(places[row] * rows, rows), rows)
        for col in range(col_chunks):
            loose[there, col * width : (col + 1) * width] = pieces[row * col_chunks + col][...]
    width = loose.shape[1] // blocks
    for block in range(blocks):
        source = pl.ds(pl.multiple_of(table[block] * width, width), width)
        tokens[:, block * width : (block + 1) * width] = loose[:, source]
    total = project(tokens, weights)
    kv[:, :HEAD_SIZE] = rotate(total[:, :HEAD_SIZE], cosine[...], sine[...]).astype(kv.dtype)
    kv[:, HEAD_SIZE:] = total[:, HEAD_SIZE:].astype(kv.dtype)


def query_kernel(layout, tokens, *refs):
    parts, start = layout
    weights = refs[:parts]
    cosine, sine, slots = refs[parts : parts + 3]
    outs, queries = refs[parts + 3 : -1], refs[-1]
    raw = project(tokens, weights, slice(start, start + queries.shape[1]))
    for head in range(queries.shape[1] // HEAD_SIZE):
        cols = slice(head * HEAD_SIZE, (head + 1) * HEAD_SIZE)
        queries[:, cols] = rotate(raw[:, cols], cosine[...], sine[...]).astype(queries.dtype)
    count = outs[0].shape[0]
    at = lax.broadcasted_iota(jnp.int32, (count, queries.shape[0]), 0)
    for step, out in enumerate(outs):
        hot = jnp.where(at + step * count == slots[...], 1.0, 0.0).astype(jnp.bfloat16)
        out[...] = dot(hot, queries[...]).astype(out.dtype)


def attention_kernel(layout, far, columns, query_bar, key_hot, *refs):
    query_parts, kv_parts, block_rows = layout
    arrived = refs[:query_parts]
    kvs = refs[query_parts : query_parts + kv_parts]
    outs = refs[query_parts + kv_parts : -5]
    keys, values, long, scores, context = refs[-5:]
    groups, rows = columns.shape
    heads = arrived[0].shape[1] // HEAD_SIZE
    start = 0
    for kv in kvs:
        own = slice(start, start + kv.shape[0])
        keys[own, :HEAD_SIZE] = kv[:, :HEAD_SIZE]
        values[own, :] = kv[:, HEAD_SIZE:]
        start += kv.shape[0]
    keys[:, HEAD_SIZE:] = key_hot[...]
    span = arrived[0].shape[0] // groups
    at = lax.broadcasted_iota(jnp.int32, (span * query_parts, rows), 0)
    for group in range(groups):
        hot = jnp.where(at == columns[group : group + 1, :], 1.0, 0.0).astype(jnp.bfloat16)
        there = slice(group * span, (group + 1) * span)
        slab = jnp.concatenate([part[there, :] for part in arrived], axis=0)
        picked = lax.dot_general(
            hot, slab, (((0,), (0,)), ((), ())), preferred_element_type=jnp.float32
        ).astype(jnp.bfloat16)
        own = slice(group * rows, (group + 1) * rows)
        for head in range(heads):
            long[head, own, :HEAD_SIZE] = picked[:, head * HEAD_SIZE : (head + 1) * HEAD_SIZE]
            long[head, own, HEAD_SIZE:] = query_bar[own, :]
    factor = 1.4426950408889634 / HEAD_SIZE**0.5
    blocks = groups * rows // block_rows
    steps = [(block, head) for block in range(blocks) for head in range(heads)]

    def score(step):
        block, head = steps[step]
        own = slice(block * block_rows, (block + 1) * block_rows)
        scores[step % 2] = dot_rows(long[head, own, :], keys[...])

    score(0)
    for step, (block, head) in enumerate(steps):
        if step + 1 < len(steps):
            score(step + 1)
        own = slice(block * block_rows, (block + 1) * block_rows)
        held = scores[step % 2]
        top = jnp.max(held, axis=1, keepdims=True)
        kept = jnp.exp2((held - top) * factor)
        total = jnp.sum(kept, axis=1, keepdims=True)
        mixed = dot(kept.astype(jnp.bfloat16), values[...])
        context[own, head * HEAD_SIZE : (head + 1) * HEAD_SIZE] = (mixed / total).astype(
            context.dtype
        )
    for step, out in enumerate(outs):
        out[...] = context[pl.ds(pl.multiple_of(far[step] * rows, rows), rows), :]


def finish_kernel(far, *refs):
    out = refs[-1]
    groups = far.shape[0]
    parts = (len(refs) - 1) // groups
    width = refs[0].shape[1]
    for part in range(parts):
        for step in range(groups):
            start = pl.multiple_of((far[step] * parts + part) * width, width)
            out[:, pl.ds(start, width)] = refs[part * groups + step][...]


def turn(value, axis, bits):
    count = lax.axis_size(axis)
    return lax.ppermute(value, axis, [(i, i ^ bits) for i in range(count)])


def after(value, *others):
    return lax.optimization_barrier((value, *others))[0]


def spread(value, *others):
    across = turn(value, "team", 2)
    last = turn(after(across, *others), "team", 1)
    return [value, across, turn(value, "team", 1), last]


def body(stored, source_owner, doc_ids, doc_starts, wq, wk, wv):
    groups, team = lax.axis_size("line"), lax.axis_size("team")
    nctx, ntp = groups * team, lax.axis_size("tp")
    group, mate = lax.axis_index("line"), lax.axis_index("team")
    rows = stored.shape[0]
    cap = 2 * rows // nctx
    size = HEAD_SIZE
    depth = wq.shape[0]
    split = groups > 1
    pair = 2 * size
    parts = wq.shape[1] // groups // pair
    total_rows = groups * rows
    width = stored.shape[1] * ntp
    keys = nctx * rows
    far = group ^ jnp.arange(groups, dtype=jnp.int32)

    def flip(value):
        return lax.ppermute(value, "tp", [(0, 1), (1, 0)])

    below = 16 if split else 0
    slabs = call(
        weights_kernel,
        [jax.ShapeDtypeStruct((depth + below, pair), jnp.bfloat16)] * groups
        + [jax.ShapeDtypeStruct((depth, parts * pair), jnp.bfloat16)] * groups,
        [far, source_owner[None, :], wq, wk, wv],
        smem=(0,),
    )
    kv_slabs, query_slabs = slabs[:groups], slabs[groups:]

    if split:
        def send(slabs, step, *others):
            return turn(after(slabs[step], *others), "line", step)

        def assemble(*pieces):
            count = len(pieces)
            shape = (count * pieces[0].shape[0], pieces[0].shape[1])
            return call(
                functools.partial(assemble_kernel, depth),
                jax.ShapeDtypeStruct(shape, jnp.bfloat16),
                pieces,
            )

        inner, outer = [(1, 2), (2, 1)], [(1, 0), (2, 3)]
        near = turn(stored, "line", 1)
        over = lax.ppermute(stored, "line", inner)
        flips = [flip(stored)]
        query_near = send(query_slabs, 1)
        kv_third = send(kv_slabs, 3)
        over_near = lax.ppermute(after(near, over, flips[0], *slabs), "line", inner)
        end = lax.ppermute(after(over, near, query_near), "line", outer)
        flips.append(flip(after(near, flips[0], kv_third)))
        first = spread(assemble(query_slabs[0], query_near))
        kv_second = send(kv_slabs, 2, kv_third, near, over)
        edge = (group == 0) | (group == groups - 1)
        third = jnp.where(edge, end, over)
        end_near = lax.ppermute(after(over_near, flips[1]), "line", outer)
        flips.append(flip(after(third, flips[1])))
        kv_near = send(kv_slabs, 1, over_near, end)
        query_third = send(query_slabs, 3, kv_second, over_near)
        fourth = jnp.where(edge, end_near, over_near)
        flips.append(flip(after(fourth, flips[2], query_third)))
        kv_held = assemble(kv_slabs[0], kv_near, kv_second, kv_third)
        kv_weights = spread(after(kv_held, first[1]))
        query_second = send(query_slabs, 2, kv_near, end_near, flips[2])
        second_held = assemble(query_second, query_third)
        second_held = after(second_held, kv_weights[1], flips[3])
        places = jnp.stack(
            [group, group ^ 1, group ^ jnp.where(edge, 2, 3), group ^ jnp.where(edge, 3, 2)]
        )
        pieces = [
            chunk for both in zip((stored, near, third, fourth), flips) for chunk in both
        ]
        chunks = ntp
        owners = kv_weights
    else:
        pieces = [lax.all_gather(stored, "tp", axis=1, tiled=True)]
        places = jnp.zeros((1,), jnp.int32)
        chunks = 1
        kv_weights = [lax.all_gather(kv_slabs[0], "team", axis=0, tiled=True)]
        query_weights = [lax.all_gather(query_slabs[0], "team", axis=0, tiled=True)]
        owners = [lax.all_gather(source_owner, "team", axis=0)]

    if split:
        rel = jnp.arange(groups, dtype=jnp.int32)
        turns = mate ^ jnp.array([0, 2, 1, 3], dtype=jnp.int32)
        order = (rel[None, :] * team + turns[:, None]).reshape(-1)
        came = (far[None, :] * team + turns[:, None]).reshape(-1)
        mine = rel * team + mate
        twist = mate[None]
        share = nctx // ntp
        table = came % share + jnp.where(came // share == lax.axis_index("tp"), 0, share)
    else:
        order = came = jnp.arange(nctx, dtype=jnp.int32)
        mine = mate[None]
        twist = table = jnp.zeros((1,), jnp.int32)

    freqs = ROPE_BASE ** (-np.arange(size // 2) * 2.0 / size)
    freqs = jnp.asarray(np.concatenate([freqs, freqs])[None, :], jnp.float32)
    sign = jnp.asarray(np.repeat([-1.0, 1.0], size // 2)[None, :], jnp.float32)
    angles, key_hot, query_bar, slots, columns = call(
        functools.partial(places_kernel, cap),
        [
            jax.ShapeDtypeStruct((total_rows, size), jnp.float32),
            jax.ShapeDtypeStruct((keys, LANES), jnp.bfloat16),
            jax.ShapeDtypeStruct((total_rows, LANES), jnp.bfloat16),
            jax.ShapeDtypeStruct((1, total_rows), jnp.int32),
            jax.ShapeDtypeStruct((groups, rows), jnp.int32),
        ],
        [mine, order, came, mate[None], twist, doc_starts, freqs, *owners],
        scratch=[
            pltpu.VMEM((nctx, rows), jnp.int32),
            pltpu.VMEM((max(2 * nctx, LANES), rows), jnp.float32),
            pltpu.VMEM((nctx, rows), jnp.float32),
            pltpu.VMEM((nctx, rows), jnp.int32),
        ],
        flops=10**9,
        smem=(0, 1, 2, 3, 4, 5),
    )
    cosine = jnp.cos(angles)
    sine = jnp.sin(angles) * sign

    tokens, kv = call(
        functools.partial(kv_kernel, (groups, chunks, nctx if split else 1)),
        [
            jax.ShapeDtypeStruct((total_rows, width), jnp.bfloat16),
            jax.ShapeDtypeStruct((total_rows, pair), jnp.bfloat16),
        ],
        [places, table, *pieces, *kv_weights, cosine, sine],
        scratch=[pltpu.VMEM((total_rows, width), jnp.bfloat16)],
        flops=2 * total_rows * width * pair,
        smem=(0, 1),
        vmem=28,
    )
    if split:
        second = spread(second_held, kv)
        query_weights = [part for both in zip(first, second) for part in both]

    block_rows = min(2 * rows, total_rows)
    lanes_out = team if split else 1
    slot_count = nctx * groups * cap

    def project_part(part):
        return call(
            functools.partial(query_kernel, (len(query_weights), part * pair)),
            [jax.ShapeDtypeStruct((slot_count // lanes_out, pair), jnp.bfloat16)] * lanes_out,
            [tokens, *query_weights, cosine, sine, slots],
            scratch=[pltpu.VMEM((total_rows, pair), jnp.bfloat16)],
            flops=2 * total_rows * (width + slot_count) * pair,
        )

    def attend(arrived):
        context = call(
            functools.partial(attention_kernel, (len(arrived), len(kvs), block_rows)),
            [jax.ShapeDtypeStruct((rows, pair), jnp.bfloat16)] * groups,
            [far, columns, query_bar, key_hot, *arrived, *kvs],
            scratch=[
                pltpu.VMEM((keys, size + LANES), jnp.bfloat16),
                pltpu.VMEM((keys, size), jnp.bfloat16),
                pltpu.VMEM((pair // size, total_rows, size + LANES), jnp.bfloat16),
                pltpu.VMEM((2, block_rows, keys), jnp.float32),
                pltpu.VMEM((total_rows, pair), jnp.bfloat16),
            ],
            flops=8 * total_rows * pair * keys,
            smem=(0,),
            vmem=40,
        )
        return [context[0]] + [turn(context[step], "line", step) for step in range(1, groups)]

    def exchange(leaving):
        if split:
            return [leaving[0]] + [turn(leaving[e], "team", e) for e in range(1, team)]
        return [lax.all_to_all(leaving[0], "team", 0, 0, tiled=True)]

    leaving = [project_part(part) for part in range(parts)]
    arrived = [exchange(part) for part in leaving]
    if split:
        across = turn(after(kv, second[1]), "team", 2)
        last = turn(after(across, leaving[-1][0]), "team", 1)
        kvs = [kv, across, turn(kv, "team", 1), last]
    else:
        kvs = [lax.all_gather(kv, "team", axis=0, tiled=True)]
    ready = [piece for queries in arrived for piece in attend(queries)]

    return call(
        finish_kernel,
        jax.ShapeDtypeStruct((rows, wq.shape[1]), jnp.bfloat16),
        [far, *ready],
        smem=(0,),
    )


def solution(mesh):
    def program(stored, source_owner, doc_ids, doc_starts, wq, wk, wv):
        ctx, tp = mesh.shape["ctx"], mesh.shape["tp"]
        groups = wk.shape[1] // HEAD_SIZE // tp
        parts = jax.sharding.Mesh(
            mesh.devices.reshape(groups, ctx // groups, tp), ("line", "team", "tp")
        )
        both = ("line", "team")
        return jax.shard_map(
            body,
            mesh=parts,
            in_specs=(
                P(both, "tp"),
                P(both),
                P(both),
                P(),
                P(both, "tp"),
                P(both, "tp"),
                P(both, "tp"),
            ),
            out_specs=P(both, "tp"),
            check_vma=False,
        )(stored, source_owner, doc_ids, doc_starts, wq, wk, wv)

    return program
```

```python
import functools

import jax
import jax.numpy as jnp
import numpy as np
from jax import lax
from jax.experimental import pallas as pl
from jax.experimental.pallas import tpu as pltpu
from jax.sharding import PartitionSpec as P

HEAD_SIZE = 128
LANES = 128
ROPE_BASE = 500000.0
OTHER = -(2.0**100)

VMEM_SPEC = pl.BlockSpec(memory_space=pltpu.VMEM)
SMEM_SPEC = pl.BlockSpec(memory_space=pltpu.SMEM)
ANY_SPEC = pl.BlockSpec(memory_space=pl.ANY)


def dot(a, b):
    return jnp.dot(a, b, preferred_element_type=jnp.float32)


def dot_rows(a, b):
    return lax.dot_general(
        a, b, (((1,), (1,)), ((), ())), preferred_element_type=jnp.float32
    )


def call(kernel, out_shape, operands, scratch=(), flops=0, smem=(), anywhere=(), vmem=24):
    specs = [
        SMEM_SPEC if at in smem else ANY_SPEC if at in anywhere else VMEM_SPEC
        for at in range(len(operands))
    ]
    many = isinstance(out_shape, (list, tuple))
    outs = out_shape if many else [out_shape]
    moved = sum(x.size * x.dtype.itemsize for x in [*operands, *outs])
    return pl.pallas_call(
        kernel,
        out_shape=out_shape,
        in_specs=specs,
        out_specs=[VMEM_SPEC] * len(out_shape) if many else VMEM_SPEC,
        scratch_shapes=list(scratch),
        compiler_params=pltpu.CompilerParams(vmem_limit_bytes=vmem * 2**20),
        cost_estimate=pl.CostEstimate(flops=flops, bytes_accessed=moved, transcendentals=0),
    )(*operands)


def weights_kernel(far, owner, wq, wk, wv, *outs):
    depth = wq.shape[0]
    for step, out in enumerate(outs):
        start = pl.multiple_of(far[step] * HEAD_SIZE, HEAD_SIZE)
        width = out.shape[1] - 2 * HEAD_SIZE
        out[:depth, :HEAD_SIZE] = wk[:, pl.ds(start, HEAD_SIZE)]
        out[:depth, HEAD_SIZE : 2 * HEAD_SIZE] = wv[:, pl.ds(start, HEAD_SIZE)]
        start = pl.multiple_of(far[step] * width, width)
        out[:depth, 2 * HEAD_SIZE :] = wq[:, pl.ds(start, width)]
        below = out.shape[0] - depth
        if below:
            row = owner[...].astype(jnp.float32).astype(jnp.bfloat16)
            out[depth:, :] = jnp.zeros((below, out.shape[1]), jnp.bfloat16)
            out[depth:, : row.shape[1]] = jnp.broadcast_to(row, (below, row.shape[1]))


def join_kernel(depth, first, *refs):
    blocks, second, out = refs[:-2], refs[-2], refs[-1]
    tile = out.shape[0] - depth * len(blocks)
    count = LANES
    for step, block in enumerate(blocks):
        out[step * depth : (step + 1) * depth, :] = block[:depth, :]
    row = lax.broadcasted_iota(jnp.int32, (tile, count), 0)

    def spread_row(ref):
        if ref.shape[0] == 1:
            return jnp.broadcast_to(ref[...].astype(jnp.float32), (tile, count))
        return ref[depth:, :count].astype(jnp.float32)

    both = jnp.where(row == 0, spread_row(first), spread_row(second)).astype(out.dtype)
    out[depth * len(blocks) :, :] = jnp.zeros((tile, out.shape[1]), out.dtype)
    out[depth * len(blocks) :, :count] = both


def places_kernel(cap, mine, order, came, mate, twist, doc_starts, freqs, *refs):
    outs, scratch = refs[-11:-6], refs[-6:]
    angles, key_hot, query_bar, slots, columns = outs
    coded, starts, local, owners, landed, semaphore = scratch
    shards, rows = owners.shape
    sources = refs[:-11]
    tile = landed.shape[1]
    copies = []
    for at, source in enumerate(sources):
        bottom = source.at[source.shape[0] - tile :, :rows]
        copies.append(pltpu.make_async_copy(bottom, landed.at[at], semaphore.at[at]))
        copies[-1].start()
    for copy in copies:
        copy.wait()
    each = shards // len(sources)
    for source in range(shards):
        value = landed[source // each].astype(jnp.float32).astype(jnp.int32)
        owners[pl.ds(came[source], 1), :] = value[source % each : source % each + 1, :]
    groups = mine.shape[0]
    team = shards // groups
    span = groups * cap
    owner_at = lax.broadcasted_iota(jnp.int32, (shards, rows), 0)
    upper = jnp.where(
        lax.broadcasted_iota(jnp.int32, (rows, rows), 0)
        < lax.broadcasted_iota(jnp.int32, (rows, rows), 1),
        1.0,
        0.0,
    ).astype(jnp.bfloat16)
    rank_at = lax.broadcasted_iota(jnp.int32, (rows, rows), 0).astype(jnp.float32)
    lane = lax.broadcasted_iota(jnp.int32, (1, rows), 1).astype(jnp.float32)
    before = jnp.zeros((shards, 1), jnp.float32)
    found = jnp.zeros((3 * shards, rows), jnp.float32)
    for shard in range(shards):
        hot = jnp.where(owners[shard : shard + 1, :] == owner_at, 1.0, 0.0)
        within = dot(hot.astype(jnp.bfloat16), upper)
        local[shard : shard + 1, :] = jnp.sum(hot * within, axis=0, keepdims=True)
        rank = jnp.sum(hot * (within + before), axis=0, keepdims=True)
        before = before + jnp.sum(hot, axis=1, keepdims=True)
        rank_hot = jnp.where(rank_at == rank, 1.0, 0.0).astype(jnp.bfloat16)
        codes = jnp.concatenate([hot * float(shard), hot * lane, hot * within], axis=0)
        found = found + dot_rows(codes.astype(jnp.bfloat16), rank_hot)
    shard_of = found[:shards]
    place = shard_of * rows + found[shards : 2 * shards]
    docs = doc_starts.shape[0]
    doc_lane = lax.broadcasted_iota(jnp.int32, (1, LANES), 1)
    doc_row = jnp.full((1, LANES), -1.0, jnp.float32)
    start = jnp.zeros_like(place)
    for doc in range(docs):
        value = doc_starts[doc].astype(jnp.float32)
        start = jnp.maximum(start, jnp.where(value <= place, value, 0.0))
        doc_row = jnp.where(doc_lane == doc, value, doc_row)
    to_shard = shard_of.astype(jnp.int32)
    to_group = jnp.zeros_like(to_shard)
    for group in range(1, groups):
        to_group = jnp.where(to_shard >= group * team, group, to_group)
    to_mate = (to_shard - to_group * team) ^ twist[0]
    inside = found[2 * shards :].astype(jnp.int32)
    coded[...] = (to_mate * groups + to_group) * span + inside
    starts[:shards, :] = start
    starts[shards : 2 * shards, :] = place - start
    flat = jnp.transpose(starts[...])
    which = lax.broadcasted_iota(jnp.int32, flat.shape, 1)
    column = lax.broadcasted_iota(jnp.int32, (rows, 1), 0)
    for group in range(groups):
        own = slice(group * rows, (group + 1) * rows)
        at = mine[group]
        offset = jnp.sum(jnp.where(which == at + shards, flat, 0.0), axis=1, keepdims=True)
        angles[own, :] = offset * freqs[...]
        slots[:, own] = coded[pl.ds(at, 1), :] + group * cap
        shard = group * team + mate[0]
        place = column + shard * rows
        begin = jnp.zeros_like(column)
        for doc in range(docs):
            begin = jnp.where(doc_starts[doc] <= place, doc_starts[doc], begin)
        query_bar[own, :] = jnp.where(begin.astype(jnp.float32) == doc_row, 0.0, OTHER).astype(
            jnp.bfloat16
        )
        owner = owners[pl.ds(shard, 1), :]
        owner_group = jnp.zeros_like(owner)
        for step in range(1, groups):
            owner_group = jnp.where(owner >= step * team, step, owner_group)
        owner_mate = (owner - owner_group * team) ^ twist[0]
        rank = local[pl.ds(shard, 1), :].astype(jnp.int32)
        columns[group : group + 1, :] = owner_mate * span + owner_group * cap + rank
    for block in range(shards):
        own = slice(block * rows, (block + 1) * rows)
        begin = jnp.sum(jnp.where(which == order[block], flat, 0.0), axis=1, keepdims=True)
        key_hot[own, :] = jnp.where(begin == doc_row, 1.0, 0.0).astype(jnp.bfloat16)


def rotate(raw, cosine, sine):
    return raw * cosine + pltpu.roll(raw, HEAD_SIZE // 2, 1) * sine


def project(tokens, weights, cols=slice(None)):
    total = None
    start = 0
    for weight in weights:
        depth = weight.shape[0] // LANES * LANES
        part = dot(tokens[:, start : start + depth], weight[:depth, cols])
        total = part if total is None else total + part
        start += depth
    return total


def tokens_kernel(layout, places, table, *refs):
    row_blocks, col_chunks, blocks = layout
    count = row_blocks * col_chunks
    pieces, weights = refs[:count], refs[count:-4]
    total, later, tokens, loose = refs[-4:]
    rows, width = pieces[0].shape
    for row in range(row_blocks):
        there = pl.ds(pl.multiple_of(places[row] * rows, rows), rows)
        for col in range(col_chunks):
            loose[there, col * width : (col + 1) * width] = pieces[row * col_chunks + col][...]
    width = loose.shape[1] // blocks
    for block in range(blocks):
        source = pl.ds(pl.multiple_of(table[block] * width, width), width)
        tokens[:, block * width : (block + 1) * width] = loose[:, source]
    if later.shape[1] < tokens.shape[1]:
        later[...] = tokens[:, tokens.shape[1] - later.shape[1] :]
    for start in range(0, total.shape[1], 2 * HEAD_SIZE):
        cols = slice(start, start + 2 * HEAD_SIZE)
        total[:, cols] = project(tokens, weights, cols)


def finish_projection(total, later, weights, cols):
    if not weights:
        return total[:, cols]
    return total[:, cols] + project(later, weights, cols)


def kv_kernel(total, later, *refs):
    weights = refs[:-3]
    cosine, sine, kv = refs[-3:]
    raw = finish_projection(total, later, weights, slice(0, 2 * HEAD_SIZE))
    kv[:, :HEAD_SIZE] = rotate(raw[:, :HEAD_SIZE], cosine[...], sine[...]).astype(kv.dtype)
    kv[:, HEAD_SIZE:] = raw[:, HEAD_SIZE:].astype(kv.dtype)


def query_kernel(layout, total, later, *refs):
    parts, start = layout
    weights = refs[:parts]
    cosine, sine, slots = refs[parts : parts + 3]
    outs, queries = refs[parts + 3 : -1], refs[-1]
    raw = finish_projection(total, later, weights, slice(start, start + queries.shape[1]))
    for head in range(queries.shape[1] // HEAD_SIZE):
        cols = slice(head * HEAD_SIZE, (head + 1) * HEAD_SIZE)
        queries[:, cols] = rotate(raw[:, cols], cosine[...], sine[...]).astype(queries.dtype)
    count = outs[0].shape[0]
    at = lax.broadcasted_iota(jnp.int32, (count, queries.shape[0]), 0)
    for step, out in enumerate(outs):
        hot = jnp.where(at + step * count == slots[...], 1.0, 0.0).astype(jnp.bfloat16)
        out[...] = dot(hot, queries[...]).astype(out.dtype)


def attention_kernel(layout, far, columns, query_bar, key_hot, *refs):
    query_parts, kv_parts, block_rows = layout
    arrived = refs[:query_parts]
    kvs = refs[query_parts : query_parts + kv_parts]
    outs = refs[query_parts + kv_parts : -5]
    keys, values, long, scores, context = refs[-5:]
    groups, rows = columns.shape
    heads = arrived[0].shape[1] // HEAD_SIZE
    start = 0
    for kv in kvs:
        own = slice(start, start + kv.shape[0])
        keys[own, :HEAD_SIZE] = kv[:, :HEAD_SIZE]
        values[own, :] = kv[:, HEAD_SIZE:]
        start += kv.shape[0]
    keys[:, HEAD_SIZE:] = key_hot[...]
    span = arrived[0].shape[0] // groups
    at = lax.broadcasted_iota(jnp.int32, (span * query_parts, rows), 0)
    for group in range(groups):
        hot = jnp.where(at == columns[group : group + 1, :], 1.0, 0.0).astype(jnp.bfloat16)
        there = slice(group * span, (group + 1) * span)
        slab = jnp.concatenate([part[there, :] for part in arrived], axis=0)
        picked = lax.dot_general(
            hot, slab, (((0,), (0,)), ((), ())), preferred_element_type=jnp.float32
        ).astype(jnp.bfloat16)
        own = slice(group * rows, (group + 1) * rows)
        for head in range(heads):
            long[head, own, :HEAD_SIZE] = picked[:, head * HEAD_SIZE : (head + 1) * HEAD_SIZE]
            long[head, own, HEAD_SIZE:] = query_bar[own, :]
    factor = 1.4426950408889634 / HEAD_SIZE**0.5
    blocks = groups * rows // block_rows
    steps = [(block, head) for block in range(blocks) for head in range(heads)]

    def score(step):
        block, head = steps[step]
        own = slice(block * block_rows, (block + 1) * block_rows)
        scores[step % 2] = dot_rows(long[head, own, :], keys[...])

    score(0)
    for step, (block, head) in enumerate(steps):
        if step + 1 < len(steps):
            score(step + 1)
        own = slice(block * block_rows, (block + 1) * block_rows)
        held = scores[step % 2]
        top = jnp.max(held, axis=1, keepdims=True)
        kept = jnp.exp2((held - top) * factor)
        total = jnp.sum(kept, axis=1, keepdims=True)
        mixed = dot(kept.astype(jnp.bfloat16), values[...])
        context[own, head * HEAD_SIZE : (head + 1) * HEAD_SIZE] = (mixed / total).astype(
            context.dtype
        )
    for step, out in enumerate(outs):
        out[...] = context[pl.ds(pl.multiple_of(far[step] * rows, rows), rows), :]


def finish_kernel(far, *refs):
    out = refs[-1]
    groups = far.shape[0]
    parts = (len(refs) - 1) // groups
    width = refs[0].shape[1]
    for part in range(parts):
        for step in range(groups):
            start = pl.multiple_of((far[step] * parts + part) * width, width)
            out[:, pl.ds(start, width)] = refs[part * groups + step][...]


def turn(value, axis, bits):
    count = lax.axis_size(axis)
    return lax.ppermute(value, axis, [(i, i ^ bits) for i in range(count)])


def after(value, *others):
    return lax.optimization_barrier((value, *others))[0]


def spread(value, *others):
    across = turn(value, "team", 2)
    last = turn(after(across, *others), "team", 1)
    return [value, across, turn(value, "team", 1), last]


def body(stored, source_owner, doc_ids, doc_starts, wq, wk, wv):
    groups, team = lax.axis_size("line"), lax.axis_size("team")
    nctx, ntp = groups * team, lax.axis_size("tp")
    group, mate = lax.axis_index("line"), lax.axis_index("team")
    rows = stored.shape[0]
    cap = 2 * rows // nctx
    size = HEAD_SIZE
    depth = wq.shape[0]
    split = groups > 1
    pair = 2 * size
    parts = wq.shape[1] // groups // pair
    total_rows = groups * rows
    width = stored.shape[1] * ntp
    keys = nctx * rows
    far = group ^ jnp.arange(groups, dtype=jnp.int32)

    def flip(value):
        return lax.ppermute(value, "tp", [(0, 1), (1, 0)])

    columns_each = (1 + parts) * pair
    tile = 16
    slabs = call(
        weights_kernel,
        [
            jax.ShapeDtypeStruct((depth + tile * (step % 2), columns_each), jnp.bfloat16)
            for step in range(groups)
        ],
        [far, source_owner[None, :], wq, wk, wv],
        smem=(0,),
    )

    if split:
        def join(first, blocks, second):
            shape = (depth * len(blocks) + tile, columns_each)
            return call(
                functools.partial(join_kernel, depth),
                jax.ShapeDtypeStruct(shape, jnp.bfloat16),
                [first, *blocks, second],
            )

        inner, outer = [(1, 2), (2, 1)], [(1, 0), (2, 3)]
        near = turn(stored, "line", 1)
        over = lax.ppermute(stored, "line", inner)
        flips = [flip(stored)]
        weights_near = turn(slabs[1], "line", 1)
        weights_third = turn(slabs[3], "line", 3)
        over_near = lax.ppermute(after(near, over, flips[0], *slabs), "line", inner)
        end = lax.ppermute(after(over, near, weights_near), "line", outer)
        flips.append(flip(after(near, flips[0], weights_third)))
        held = join(source_owner[None, :], [slabs[0], weights_near], weights_near)
        second_owner = turn(after(source_owner, weights_near), "line", 2)[None, :]
        first = spread(held)
        edge = (group == 0) | (group == groups - 1)
        third = jnp.where(edge, end, over)
        end_near = lax.ppermute(after(over_near, flips[1]), "line", outer)
        flips.append(flip(after(third, flips[1], second_owner)))
        weights_second = turn(after(slabs[2], over_near, end, first[1]), "line", 2)
        fourth = jnp.where(edge, end_near, over_near)
        flips.append(flip(after(fourth, flips[2])))
        third_held = join(weights_third, [weights_third], second_owner)
        second = spread(after(third_held, flips[2], first[1]))
        last_held = after(weights_second, flips[3], second[1])
        early = [part for both in zip(first, second) for part in both]
        places = jnp.stack(
            [group, group ^ 1, group ^ jnp.where(edge, 2, 3), group ^ jnp.where(edge, 3, 2)]
        )
        pieces = [
            chunk for both in zip((stored, near, third, fourth), flips) for chunk in both
        ]
        chunks = ntp
        owners = early
    else:
        pieces = [lax.all_gather(stored, "tp", axis=1, tiled=True)]
        places = jnp.zeros((1,), jnp.int32)
        chunks = 1
        early = [lax.all_gather(slabs[0], "team", axis=0, tiled=True)]
        owners = [lax.all_gather(source_owner, "team", axis=0)]

    if split:
        rel = jnp.arange(groups, dtype=jnp.int32)
        turns = mate ^ jnp.array([0, 2, 1, 3], dtype=jnp.int32)
        order = (rel[None, :] * team + turns[:, None]).reshape(-1)
        came = (far[jnp.array([0, 1, 3, 2])][None, :] * team + turns[:, None]).reshape(-1)
        rows_of = jnp.concatenate(
            [came.reshape(team, groups)[:, :3].reshape(-1), came.reshape(team, groups)[:, 3]]
        )
        mine = rel * team + mate
        twist = mate[None]
        share = nctx // ntp
        table = rows_of % share + jnp.where(rows_of // share == lax.axis_index("tp"), 0, share)
    else:
        order = came = jnp.arange(nctx, dtype=jnp.int32)
        mine = mate[None]
        twist = table = jnp.zeros((1,), jnp.int32)

    freqs = ROPE_BASE ** (-np.arange(size // 2) * 2.0 / size)
    freqs = jnp.asarray(np.concatenate([freqs, freqs])[None, :], jnp.float32)
    sign = jnp.asarray(np.repeat([-1.0, 1.0], size // 2)[None, :], jnp.float32)
    angles, key_hot, query_bar, slots, columns = call(
        functools.partial(places_kernel, cap),
        [
            jax.ShapeDtypeStruct((total_rows, size), jnp.float32),
            jax.ShapeDtypeStruct((keys, LANES), jnp.bfloat16),
            jax.ShapeDtypeStruct((total_rows, LANES), jnp.bfloat16),
            jax.ShapeDtypeStruct((1, total_rows), jnp.int32),
            jax.ShapeDtypeStruct((groups, rows), jnp.int32),
        ],
        [mine, order, came, mate[None], twist, doc_starts, freqs, *owners],
        scratch=[
            pltpu.VMEM((nctx, rows), jnp.int32),
            pltpu.VMEM((max(2 * nctx, LANES), rows), jnp.float32),
            pltpu.VMEM((nctx, rows), jnp.float32),
            pltpu.VMEM((nctx, rows), jnp.int32),
            pltpu.VMEM((len(owners), tile if split else nctx, rows), owners[0].dtype),
            pltpu.SemaphoreType.DMA((len(owners),)),
        ],
        flops=10**9,
        smem=(0, 1, 2, 3, 4, 5),
        anywhere=range(7, 7 + len(owners)),
    )
    cosine = jnp.cos(angles)
    sine = jnp.sin(angles) * sign

    rest = width // groups if split else width
    total, later = call(
        functools.partial(tokens_kernel, (groups, chunks, nctx if split else 1)),
        [
            jax.ShapeDtypeStruct((total_rows, columns_each), jnp.float32),
            jax.ShapeDtypeStruct((total_rows, rest if split else LANES), jnp.bfloat16),
        ],
        [places, table, *pieces, *early],
        scratch=[
            pltpu.VMEM((total_rows, width), jnp.bfloat16),
            pltpu.VMEM((total_rows, width), jnp.bfloat16),
        ],
        flops=2 * total_rows * width * columns_each,
        smem=(0, 1),
        vmem=32,
    )
    late = spread(last_held, total, cosine) if split else []
    kv = call(
        kv_kernel,
        jax.ShapeDtypeStruct((total_rows, pair), jnp.bfloat16),
        [total, later, *late, cosine, sine],
        flops=2 * total_rows * rest * pair,
    )

    block_rows = min(2 * rows, total_rows)
    lanes_out = team if split else 1
    slot_count = nctx * groups * cap

    def project_part(part):
        return call(
            functools.partial(query_kernel, (len(late), (1 + part) * pair)),
            [jax.ShapeDtypeStruct((slot_count // lanes_out, pair), jnp.bfloat16)] * lanes_out,
            [total, later, *late, cosine, sine, slots],
            scratch=[pltpu.VMEM((total_rows, pair), jnp.bfloat16)],
            flops=2 * total_rows * (rest + slot_count) * pair,
        )

    def attend(arrived):
        context = call(
            functools.partial(attention_kernel, (len(arrived), len(kvs), block_rows)),
            [jax.ShapeDtypeStruct((rows, pair), jnp.bfloat16)] * groups,
            [far, columns, query_bar, key_hot, *arrived, *kvs],
            scratch=[
                pltpu.VMEM((keys, size + LANES), jnp.bfloat16),
                pltpu.VMEM((keys, size), jnp.bfloat16),
                pltpu.VMEM((pair // size, total_rows, size + LANES), jnp.bfloat16),
                pltpu.VMEM((2, block_rows, keys), jnp.float32),
                pltpu.VMEM((total_rows, pair), jnp.bfloat16),
            ],
            flops=8 * total_rows * pair * keys,
            smem=(0,),
            vmem=40,
        )
        return [context[0]] + [turn(context[step], "line", step) for step in range(1, groups)]

    def exchange(leaving):
        if split:
            return [leaving[0]] + [turn(leaving[e], "team", e) for e in range(1, team)]
        return [lax.all_to_all(leaving[0], "team", 0, 0, tiled=True)]

    leaving = [project_part(part) for part in range(parts)]
    arrived = [exchange(part) for part in leaving]
    if split:
        across = turn(kv, "team", 2)
        last = turn(after(across, leaving[-1][0]), "team", 1)
        kvs = [kv, across, turn(kv, "team", 1), last]
    else:
        kvs = [lax.all_gather(kv, "team", axis=0, tiled=True)]
    ready = [piece for queries in arrived for piece in attend(queries)]

    return call(
        finish_kernel,
        jax.ShapeDtypeStruct((rows, wq.shape[1]), jnp.bfloat16),
        [far, *ready],
        smem=(0,),
    )


def solution(mesh):
    def program(stored, source_owner, doc_ids, doc_starts, wq, wk, wv):
        ctx, tp = mesh.shape["ctx"], mesh.shape["tp"]
        groups = wk.shape[1] // HEAD_SIZE // tp
        parts = jax.sharding.Mesh(
            mesh.devices.reshape(groups, ctx // groups, tp), ("line", "team", "tp")
        )
        both = ("line", "team")
        return jax.shard_map(
            body,
            mesh=parts,
            in_specs=(
                P(both, "tp"),
                P(both),
                P(both),
                P(),
                P(both, "tp"),
                P(both, "tp"),
                P(both, "tp"),
            ),
            out_specs=P(both, "tp"),
            check_vma=False,
        )(stored, source_owner, doc_ids, doc_starts, wq, wk, wv)

    return program
```

```python
import functools

import jax
import jax.numpy as jnp
import numpy as np
from jax import lax
from jax.experimental import pallas as pl
from jax.experimental.pallas import tpu as pltpu
from jax.sharding import PartitionSpec as P

HEAD_SIZE = 128
LANES = 128
ROPE_BASE = 500000.0
OTHER = -(2.0**100)

VMEM_SPEC = pl.BlockSpec(memory_space=pltpu.VMEM)
SMEM_SPEC = pl.BlockSpec(memory_space=pltpu.SMEM)
ANY_SPEC = pl.BlockSpec(memory_space=pl.ANY)


def dot(a, b):
    return jnp.dot(a, b, preferred_element_type=jnp.float32)


def dot_rows(a, b):
    return lax.dot_general(
        a, b, (((1,), (1,)), ((), ())), preferred_element_type=jnp.float32
    )


def call(kernel, out_shape, operands, scratch=(), flops=0, smem=(), anywhere=(), vmem=24):
    specs = [
        SMEM_SPEC if at in smem else ANY_SPEC if at in anywhere else VMEM_SPEC
        for at in range(len(operands))
    ]
    many = isinstance(out_shape, (list, tuple))
    outs = out_shape if many else [out_shape]
    moved = sum(x.size * x.dtype.itemsize for x in [*operands, *outs])
    return pl.pallas_call(
        kernel,
        out_shape=out_shape,
        in_specs=specs,
        out_specs=[VMEM_SPEC] * len(out_shape) if many else VMEM_SPEC,
        scratch_shapes=list(scratch),
        compiler_params=pltpu.CompilerParams(vmem_limit_bytes=vmem * 2**20),
        cost_estimate=pl.CostEstimate(flops=flops, bytes_accessed=moved, transcendentals=0),
    )(*operands)


def weights_kernel(far, owner, near_owner, wq, wk, wv, *outs):
    depth = wq.shape[0]
    for step in range(far.shape[0]):
        out = outs[step]
        start = pl.multiple_of(far[step] * HEAD_SIZE, HEAD_SIZE)
        width = out.shape[1] - 2 * HEAD_SIZE
        out[:depth, :HEAD_SIZE] = wk[:, pl.ds(start, HEAD_SIZE)]
        out[:depth, HEAD_SIZE : 2 * HEAD_SIZE] = wv[:, pl.ds(start, HEAD_SIZE)]
        start = pl.multiple_of(far[step] * width, width)
        out[:depth, 2 * HEAD_SIZE :] = wq[:, pl.ds(start, width)]
    if len(outs) > far.shape[0]:
        bottom, leaving = outs[-1], outs[-2]
        tile, count = bottom.shape[0], owner.shape[1]
        row = lax.broadcasted_iota(jnp.int32, (tile, count), 0)
        both = jnp.where(row == 0, owner[...], near_owner[...]).astype(jnp.float32)
        bottom[...] = jnp.zeros_like(bottom)
        bottom[:, :count] = both.astype(bottom.dtype)
        leaving[depth:, :] = bottom[...]


def join_kernel(own, near, bottom, held):
    depth = own.shape[0]
    held[:depth, :] = own[...]
    held[depth : 2 * depth, :] = near[...]
    held[2 * depth :, :] = bottom[...]


def places_kernel(cap, mine, order, came, mate, twist, doc_starts, freqs, *refs):
    outs, scratch = refs[-11:-6], refs[-6:]
    angles, key_hot, query_bar, slots, columns = outs
    coded, starts, local, owners, landed, semaphore = scratch
    shards, rows = owners.shape
    sources = refs[:-11]
    tile = landed.shape[1]
    copies = []
    for at, source in enumerate(sources):
        bottom = source.at[source.shape[0] - tile :, :rows]
        copies.append(pltpu.make_async_copy(bottom, landed.at[at], semaphore.at[at]))
        copies[-1].start()
    for copy in copies:
        copy.wait()
    each = shards // len(sources)
    for source in range(shards):
        value = landed[source // each].astype(jnp.float32).astype(jnp.int32)
        owners[pl.ds(came[source], 1), :] = value[source % each : source % each + 1, :]
    groups = mine.shape[0]
    team = shards // groups
    span = groups * cap
    owner_at = lax.broadcasted_iota(jnp.int32, (shards, rows), 0)
    upper = jnp.where(
        lax.broadcasted_iota(jnp.int32, (rows, rows), 0)
        < lax.broadcasted_iota(jnp.int32, (rows, rows), 1),
        1.0,
        0.0,
    ).astype(jnp.bfloat16)
    rank_at = lax.broadcasted_iota(jnp.int32, (rows, rows), 0).astype(jnp.float32)
    lane = lax.broadcasted_iota(jnp.int32, (1, rows), 1).astype(jnp.float32)
    before = jnp.zeros((shards, 1), jnp.float32)
    found = jnp.zeros((3 * shards, rows), jnp.float32)
    for shard in range(shards):
        hot = jnp.where(owners[shard : shard + 1, :] == owner_at, 1.0, 0.0)
        within = dot(hot.astype(jnp.bfloat16), upper)
        local[shard : shard + 1, :] = jnp.sum(hot * within, axis=0, keepdims=True)
        rank = jnp.sum(hot * (within + before), axis=0, keepdims=True)
        before = before + jnp.sum(hot, axis=1, keepdims=True)
        rank_hot = jnp.where(rank_at == rank, 1.0, 0.0).astype(jnp.bfloat16)
        codes = jnp.concatenate([hot * float(shard), hot * lane, hot * within], axis=0)
        found = found + dot_rows(codes.astype(jnp.bfloat16), rank_hot)
    shard_of = found[:shards]
    place = shard_of * rows + found[shards : 2 * shards]
    docs = doc_starts.shape[0]
    doc_lane = lax.broadcasted_iota(jnp.int32, (1, LANES), 1)
    doc_row = jnp.full((1, LANES), -1.0, jnp.float32)
    start = jnp.zeros_like(place)
    for doc in range(docs):
        value = doc_starts[doc].astype(jnp.float32)
        start = jnp.maximum(start, jnp.where(value <= place, value, 0.0))
        doc_row = jnp.where(doc_lane == doc, value, doc_row)
    to_shard = shard_of.astype(jnp.int32)
    to_group = jnp.zeros_like(to_shard)
    for group in range(1, groups):
        to_group = jnp.where(to_shard >= group * team, group, to_group)
    to_mate = (to_shard - to_group * team) ^ twist[0]
    inside = found[2 * shards :].astype(jnp.int32)
    coded[...] = (to_mate * groups + to_group) * span + inside
    starts[:shards, :] = start
    starts[shards : 2 * shards, :] = place - start
    flat = jnp.transpose(starts[...])
    which = lax.broadcasted_iota(jnp.int32, flat.shape, 1)
    column = lax.broadcasted_iota(jnp.int32, (rows, 1), 0)
    for group in range(groups):
        own = slice(group * rows, (group + 1) * rows)
        at = mine[group]
        offset = jnp.sum(jnp.where(which == at + shards, flat, 0.0), axis=1, keepdims=True)
        angles[own, :] = offset * freqs[...]
        slots[:, own] = coded[pl.ds(at, 1), :] + group * cap
        shard = group * team + mate[0]
        place = column + shard * rows
        begin = jnp.zeros_like(column)
        for doc in range(docs):
            begin = jnp.where(doc_starts[doc] <= place, doc_starts[doc], begin)
        query_bar[own, :] = jnp.where(begin.astype(jnp.float32) == doc_row, 0.0, OTHER).astype(
            jnp.bfloat16
        )
        owner = owners[pl.ds(shard, 1), :]
        owner_group = jnp.zeros_like(owner)
        for step in range(1, groups):
            owner_group = jnp.where(owner >= step * team, step, owner_group)
        owner_mate = (owner - owner_group * team) ^ twist[0]
        rank = local[pl.ds(shard, 1), :].astype(jnp.int32)
        columns[group : group + 1, :] = owner_mate * span + owner_group * cap + rank
    for block in range(shards):
        own = slice(block * rows, (block + 1) * rows)
        begin = jnp.sum(jnp.where(which == order[block], flat, 0.0), axis=1, keepdims=True)
        key_hot[own, :] = jnp.where(begin == doc_row, 1.0, 0.0).astype(jnp.bfloat16)


def rotate(raw, cosine, sine):
    return raw * cosine + pltpu.roll(raw, HEAD_SIZE // 2, 1) * sine


def project(tokens, weights, cols=slice(None)):
    total = None
    start = 0
    for weight in weights:
        depth = weight.shape[0] // LANES * LANES
        part = dot(tokens[:, start : start + depth], weight[:depth, cols])
        total = part if total is None else total + part
        start += depth
    return total


def tokens_kernel(layout, places, table, *refs):
    row_blocks, col_chunks, blocks = layout
    count = row_blocks * col_chunks
    pieces, weights = refs[:count], refs[count:-4]
    total, later, tokens, loose = refs[-4:]
    rows, width = pieces[0].shape
    for row in range(row_blocks):
        there = pl.ds(pl.multiple_of(places[row] * rows, rows), rows)
        for col in range(col_chunks):
            loose[there, col * width : (col + 1) * width] = pieces[row * col_chunks + col][...]
    width = loose.shape[1] // blocks
    for block in range(blocks):
        source = pl.ds(pl.multiple_of(table[block] * width, width), width)
        tokens[:, block * width : (block + 1) * width] = loose[:, source]
    if later.shape[1] < tokens.shape[1]:
        later[...] = tokens[:, tokens.shape[1] - later.shape[1] :]
    for start in range(0, total.shape[1], 2 * HEAD_SIZE):
        cols = slice(start, start + 2 * HEAD_SIZE)
        total[:, cols] = project(tokens, weights, cols)


def finish_projection(total, later, weights, cols):
    if not weights:
        return total[:, cols]
    return total[:, cols] + project(later, weights, cols)


def kv_kernel(total, later, *refs):
    weights = refs[:-3]
    cosine, sine, kv = refs[-3:]
    raw = finish_projection(total, later, weights, slice(0, 2 * HEAD_SIZE))
    kv[:, :HEAD_SIZE] = rotate(raw[:, :HEAD_SIZE], cosine[...], sine[...]).astype(kv.dtype)
    kv[:, HEAD_SIZE:] = raw[:, HEAD_SIZE:].astype(kv.dtype)


def query_kernel(layout, total, later, *refs):
    parts, start = layout
    weights = refs[:parts]
    cosine, sine, slots = refs[parts : parts + 3]
    outs, queries = refs[parts + 3 : -1], refs[-1]
    raw = finish_projection(total, later, weights, slice(start, start + queries.shape[1]))
    for head in range(queries.shape[1] // HEAD_SIZE):
        cols = slice(head * HEAD_SIZE, (head + 1) * HEAD_SIZE)
        queries[:, cols] = rotate(raw[:, cols], cosine[...], sine[...]).astype(queries.dtype)
    count = outs[0].shape[0]
    at = lax.broadcasted_iota(jnp.int32, (count, queries.shape[0]), 0)
    for step, out in enumerate(outs):
        hot = jnp.where(at + step * count == slots[...], 1.0, 0.0).astype(jnp.bfloat16)
        out[...] = dot(hot, queries[...]).astype(out.dtype)


def attention_kernel(layout, far, columns, query_bar, key_hot, *refs):
    query_parts, kv_parts, block_rows = layout
    arrived = refs[:query_parts]
    kvs = refs[query_parts : query_parts + kv_parts]
    outs = refs[query_parts + kv_parts : -5]
    keys, values, long, scores, context = refs[-5:]
    groups, rows = columns.shape
    heads = arrived[0].shape[1] // HEAD_SIZE
    start = 0
    for kv in kvs:
        own = slice(start, start + kv.shape[0])
        keys[own, :HEAD_SIZE] = kv[:, :HEAD_SIZE]
        values[own, :] = kv[:, HEAD_SIZE:]
        start += kv.shape[0]
    keys[:, HEAD_SIZE:] = key_hot[...]
    span = arrived[0].shape[0] // groups
    at = lax.broadcasted_iota(jnp.int32, (span * query_parts, rows), 0)
    for group in range(groups):
        hot = jnp.where(at == columns[group : group + 1, :], 1.0, 0.0).astype(jnp.bfloat16)
        there = slice(group * span, (group + 1) * span)
        slab = jnp.concatenate([part[there, :] for part in arrived], axis=0)
        picked = lax.dot_general(
            hot, slab, (((0,), (0,)), ((), ())), preferred_element_type=jnp.float32
        ).astype(jnp.bfloat16)
        own = slice(group * rows, (group + 1) * rows)
        for head in range(heads):
            long[head, own, :HEAD_SIZE] = picked[:, head * HEAD_SIZE : (head + 1) * HEAD_SIZE]
            long[head, own, HEAD_SIZE:] = query_bar[own, :]
    factor = 1.4426950408889634 / HEAD_SIZE**0.5
    blocks = groups * rows // block_rows
    steps = [(block, head) for block in range(blocks) for head in range(heads)]

    def score(step):
        block, head = steps[step]
        own = slice(block * block_rows, (block + 1) * block_rows)
        scores[step % 2] = dot_rows(long[head, own, :], keys[...])

    score(0)
    for step, (block, head) in enumerate(steps):
        if step + 1 < len(steps):
            score(step + 1)
        own = slice(block * block_rows, (block + 1) * block_rows)
        held = scores[step % 2]
        top = jnp.max(held, axis=1, keepdims=True)
        kept = jnp.exp2((held - top) * factor)
        total = jnp.sum(kept, axis=1, keepdims=True)
        mixed = dot(kept.astype(jnp.bfloat16), values[...])
        context[own, head * HEAD_SIZE : (head + 1) * HEAD_SIZE] = (mixed / total).astype(
            context.dtype
        )
    for step, out in enumerate(outs):
        out[...] = context[pl.ds(pl.multiple_of(far[step] * rows, rows), rows), :]


def finish_kernel(far, *refs):
    out = refs[-1]
    groups = far.shape[0]
    parts = (len(refs) - 1) // groups
    width = refs[0].shape[1]
    for part in range(parts):
        for step in range(groups):
            start = pl.multiple_of((far[step] * parts + part) * width, width)
            out[:, pl.ds(start, width)] = refs[part * groups + step][...]


def turn(value, axis, bits):
    count = lax.axis_size(axis)
    return lax.ppermute(value, axis, [(i, i ^ bits) for i in range(count)])


def after(value, *others):
    return lax.optimization_barrier((value, *others))[0]


def spread(value, *others):
    across = turn(value, "team", 2)
    last = turn(after(across, *others), "team", 1)
    return [value, across, turn(value, "team", 1), last]


def body(stored, source_owner, doc_ids, doc_starts, wq, wk, wv):
    groups, team = lax.axis_size("line"), lax.axis_size("team")
    nctx, ntp = groups * team, lax.axis_size("tp")
    group, mate = lax.axis_index("line"), lax.axis_index("team")
    rows = stored.shape[0]
    cap = 2 * rows // nctx
    size = HEAD_SIZE
    depth = wq.shape[0]
    split = groups > 1
    pair = 2 * size
    parts = wq.shape[1] // groups // pair
    total_rows = groups * rows
    width = stored.shape[1] * ntp
    keys = nctx * rows
    far = group ^ jnp.arange(groups, dtype=jnp.int32)

    def flip(value):
        return lax.ppermute(value, "tp", [(0, 1), (1, 0)])

    columns_each = (1 + parts) * pair
    tile = 16
    shapes = [(depth + tile * (step == 3), columns_each) for step in range(groups)]
    if split:
        near_owner = turn(source_owner, "line", 1)
        shapes.append((tile, columns_each))
    else:
        near_owner = source_owner
    slabs = call(
        weights_kernel,
        [jax.ShapeDtypeStruct(shape, jnp.bfloat16) for shape in shapes],
        [far, source_owner[None, :], near_owner[None, :], wq, wk, wv],
        smem=(0,),
    )

    if split:
        inner, outer = [(1, 2), (2, 1)], [(1, 0), (2, 3)]
        over = lax.ppermute(stored, "line", inner)
        flips = [flip(stored)]
        near = turn(after(stored, near_owner), "line", 1)
        weights_near = turn(slabs[1], "line", 1)
        weights_third = turn(slabs[3], "line", 3)
        over_near = lax.ppermute(after(near, over, flips[0], *slabs), "line", inner)
        end = lax.ppermute(after(over, near, weights_third), "line", outer)
        flips.append(flip(after(near, flips[0], weights_near)))
        held = call(
            join_kernel,
            jax.ShapeDtypeStruct((2 * depth + tile, columns_each), jnp.bfloat16),
            [slabs[0], weights_near, slabs[4]],
        )
        first = spread(held)
        edge = (group == 0) | (group == groups - 1)
        third = jnp.where(edge, end, over)
        end_near = lax.ppermute(after(over_near, flips[1]), "line", outer)
        flips.append(flip(after(third, flips[1])))
        weights_second = turn(after(slabs[2], over_near, end, flips[1]), "line", 2)
        fourth = jnp.where(edge, end_near, over_near)
        flips.append(flip(after(fourth, flips[2])))
        second = spread(after(weights_third, flips[2], first[1]))
        last_held = after(weights_second, flips[3], second[1])
        early = [part for both in zip(first, second) for part in both]
        places = jnp.stack(
            [group, group ^ 1, group ^ jnp.where(edge, 2, 3), group ^ jnp.where(edge, 3, 2)]
        )
        pieces = [
            chunk for both in zip((stored, near, third, fourth), flips) for chunk in both
        ]
        chunks = ntp
        owners = early
    else:
        pieces = [lax.all_gather(stored, "tp", axis=1, tiled=True)]
        places = jnp.zeros((1,), jnp.int32)
        chunks = 1
        early = [lax.all_gather(slabs[0], "team", axis=0, tiled=True)]
        owners = [lax.all_gather(source_owner, "team", axis=0)]

    if split:
        rel = jnp.arange(groups, dtype=jnp.int32)
        turns = mate ^ jnp.array([0, 2, 1, 3], dtype=jnp.int32)
        order = (rel[None, :] * team + turns[:, None]).reshape(-1)
        came = (far[jnp.array([0, 1, 3, 2])][None, :] * team + turns[:, None]).reshape(-1)
        rows_of = jnp.concatenate(
            [came.reshape(team, groups)[:, :3].reshape(-1), came.reshape(team, groups)[:, 3]]
        )
        mine = rel * team + mate
        twist = mate[None]
        share = nctx // ntp
        table = rows_of % share + jnp.where(rows_of // share == lax.axis_index("tp"), 0, share)
    else:
        order = came = jnp.arange(nctx, dtype=jnp.int32)
        mine = mate[None]
        twist = table = jnp.zeros((1,), jnp.int32)

    freqs = ROPE_BASE ** (-np.arange(size // 2) * 2.0 / size)
    freqs = jnp.asarray(np.concatenate([freqs, freqs])[None, :], jnp.float32)
    sign = jnp.asarray(np.repeat([-1.0, 1.0], size // 2)[None, :], jnp.float32)
    angles, key_hot, query_bar, slots, columns = call(
        functools.partial(places_kernel, cap),
        [
            jax.ShapeDtypeStruct((total_rows, size), jnp.float32),
            jax.ShapeDtypeStruct((keys, LANES), jnp.bfloat16),
            jax.ShapeDtypeStruct((total_rows, LANES), jnp.bfloat16),
            jax.ShapeDtypeStruct((1, total_rows), jnp.int32),
            jax.ShapeDtypeStruct((groups, rows), jnp.int32),
        ],
        [mine, order, came, mate[None], twist, doc_starts, freqs, *owners],
        scratch=[
            pltpu.VMEM((nctx, rows), jnp.int32),
            pltpu.VMEM((max(2 * nctx, LANES), rows), jnp.float32),
            pltpu.VMEM((nctx, rows), jnp.float32),
            pltpu.VMEM((nctx, rows), jnp.int32),
            pltpu.VMEM((len(owners), tile if split else nctx, rows), owners[0].dtype),
            pltpu.SemaphoreType.DMA((len(owners),)),
        ],
        flops=10**9,
        smem=(0, 1, 2, 3, 4, 5),
        anywhere=range(7, 7 + len(owners)),
    )
    cosine = jnp.cos(angles)
    sine = jnp.sin(angles) * sign

    rest = width // groups if split else width
    total, later = call(
        functools.partial(tokens_kernel, (groups, chunks, nctx if split else 1)),
        [
            jax.ShapeDtypeStruct((total_rows, columns_each), jnp.float32),
            jax.ShapeDtypeStruct((total_rows, rest if split else LANES), jnp.bfloat16),
        ],
        [places, table, *pieces, *early],
        scratch=[
            pltpu.VMEM((total_rows, width), jnp.bfloat16),
            pltpu.VMEM((total_rows, width), jnp.bfloat16),
        ],
        flops=2 * total_rows * width * columns_each,
        smem=(0, 1),
        vmem=32,
    )
    late = spread(last_held, total, cosine) if split else []
    kv = call(
        kv_kernel,
        jax.ShapeDtypeStruct((total_rows, pair), jnp.bfloat16),
        [total, later, *late, cosine, sine],
        flops=2 * total_rows * rest * pair,
    )

    block_rows = min(2 * rows, total_rows)
    lanes_out = team if split else 1
    slot_count = nctx * groups * cap

    def project_part(part):
        return call(
            functools.partial(query_kernel, (len(late), (1 + part) * pair)),
            [jax.ShapeDtypeStruct((slot_count // lanes_out, pair), jnp.bfloat16)] * lanes_out,
            [total, later, *late, cosine, sine, slots],
            scratch=[pltpu.VMEM((total_rows, pair), jnp.bfloat16)],
            flops=2 * total_rows * (rest + slot_count) * pair,
        )

    def attend(arrived):
        context = call(
            functools.partial(attention_kernel, (len(arrived), len(kvs), block_rows)),
            [jax.ShapeDtypeStruct((rows, pair), jnp.bfloat16)] * groups,
            [far, columns, query_bar, key_hot, *arrived, *kvs],
            scratch=[
                pltpu.VMEM((keys, size + LANES), jnp.bfloat16),
                pltpu.VMEM((keys, size), jnp.bfloat16),
                pltpu.VMEM((pair // size, total_rows, size + LANES), jnp.bfloat16),
                pltpu.VMEM((2, block_rows, keys), jnp.float32),
                pltpu.VMEM((total_rows, pair), jnp.bfloat16),
            ],
            flops=8 * total_rows * pair * keys,
            smem=(0,),
            vmem=40,
        )
        return [context[0]] + [turn(context[step], "line", step) for step in range(1, groups)]

    def exchange(leaving):
        if split:
            return [leaving[0]] + [turn(leaving[e], "team", e) for e in range(1, team)]
        return [lax.all_to_all(leaving[0], "team", 0, 0, tiled=True)]

    leaving = [project_part(part) for part in range(parts)]
    arrived = [exchange(part) for part in leaving]
    if split:
        across = turn(kv, "team", 2)
        last = turn(after(across, *arrived[0], leaving[-1][0]), "team", 1)
        kvs = [kv, across, turn(kv, "team", 1), last]
    else:
        kvs = [lax.all_gather(kv, "team", axis=0, tiled=True)]
    ready = [piece for queries in arrived for piece in attend(queries)]

    return call(
        finish_kernel,
        jax.ShapeDtypeStruct((rows, wq.shape[1]), jnp.bfloat16),
        [far, *ready],
        smem=(0,),
    )


def solution(mesh):
    def program(stored, source_owner, doc_ids, doc_starts, wq, wk, wv):
        ctx, tp = mesh.shape["ctx"], mesh.shape["tp"]
        groups = wk.shape[1] // HEAD_SIZE // tp
        parts = jax.sharding.Mesh(
            mesh.devices.reshape(groups, ctx // groups, tp), ("line", "team", "tp")
        )
        both = ("line", "team")
        return jax.shard_map(
            body,
            mesh=parts,
            in_specs=(
                P(both, "tp"),
                P(both),
                P(both),
                P(),
                P(both, "tp"),
                P(both, "tp"),
                P(both, "tp"),
            ),
            out_specs=P(both, "tp"),
            check_vma=False,
        )(stored, source_owner, doc_ids, doc_starts, wq, wk, wv)

    return program
```

```python
import functools

import jax
import jax.numpy as jnp
import numpy as np
from jax import lax
from jax.experimental import pallas as pl
from jax.experimental.pallas import tpu as pltpu
from jax.sharding import PartitionSpec as P

HEAD_SIZE = 128
LANES = 128
ROPE_BASE = 500000.0
OTHER = -(2.0**100)

VMEM_SPEC = pl.BlockSpec(memory_space=pltpu.VMEM)
SMEM_SPEC = pl.BlockSpec(memory_space=pltpu.SMEM)
ANY_SPEC = pl.BlockSpec(memory_space=pl.ANY)


def dot(a, b):
    return jnp.dot(a, b, preferred_element_type=jnp.float32)


def dot_rows(a, b):
    return lax.dot_general(
        a, b, (((1,), (1,)), ((), ())), preferred_element_type=jnp.float32
    )


def call(kernel, out_shape, operands, scratch=(), flops=0, smem=(), anywhere=(), vmem=24):
    specs = [
        SMEM_SPEC if at in smem else ANY_SPEC if at in anywhere else VMEM_SPEC
        for at in range(len(operands))
    ]
    many = isinstance(out_shape, (list, tuple))
    outs = out_shape if many else [out_shape]
    moved = sum(x.size * x.dtype.itemsize for x in [*operands, *outs])
    return pl.pallas_call(
        kernel,
        out_shape=out_shape,
        in_specs=specs,
        out_specs=[VMEM_SPEC] * len(out_shape) if many else VMEM_SPEC,
        scratch_shapes=list(scratch),
        compiler_params=pltpu.CompilerParams(vmem_limit_bytes=vmem * 2**20),
        cost_estimate=pl.CostEstimate(flops=flops, bytes_accessed=moved, transcendentals=0),
    )(*operands)


def weights_kernel(far, owner, wq, wk, wv, *outs):
    depth = wq.shape[0]
    for step, out in enumerate(outs):
        start = pl.multiple_of(far[step] * HEAD_SIZE, HEAD_SIZE)
        width = out.shape[1] - 2 * HEAD_SIZE
        out[:depth, :HEAD_SIZE] = wk[:, pl.ds(start, HEAD_SIZE)]
        out[:depth, HEAD_SIZE : 2 * HEAD_SIZE] = wv[:, pl.ds(start, HEAD_SIZE)]
        start = pl.multiple_of(far[step] * width, width)
        out[:depth, 2 * HEAD_SIZE :] = wq[:, pl.ds(start, width)]
        below = out.shape[0] - depth
        if below:
            row = owner[...].astype(jnp.float32).astype(jnp.bfloat16)
            out[depth:, :] = jnp.zeros((below, out.shape[1]), jnp.bfloat16)
            out[depth:, : row.shape[1]] = jnp.broadcast_to(row, (below, row.shape[1]))


def join_kernel(owner, own, near, third, held, leaving):
    depth = own.shape[0]
    count = owner.shape[1]
    tile = near.shape[0] - depth
    row = lax.broadcasted_iota(jnp.int32, (tile, count), 0)
    mine = jnp.broadcast_to(owner[...].astype(jnp.float32), (tile, count))
    theirs = near[depth:, :count].astype(jnp.float32)
    both = jnp.where(row == 0, mine, theirs).astype(jnp.bfloat16)
    held[:depth, :] = own[...]
    held[depth : 2 * depth, :] = near[:depth, :]
    leaving[:depth, :] = third[...]
    for out in (held, leaving):
        out[out.shape[0] - tile :, :] = jnp.zeros((tile, out.shape[1]), jnp.bfloat16)
        out[out.shape[0] - tile :, :count] = both


def places_kernel(cap, mine, order, came, mate, twist, doc_starts, freqs, *refs):
    outs, scratch = refs[-11:-6], refs[-6:]
    angles, key_hot, query_bar, slots, columns = outs
    coded, starts, local, owners, landed, semaphore = scratch
    shards, rows = owners.shape
    sources = refs[:-11]
    tile = landed.shape[1]
    copies = []
    for at, source in enumerate(sources):
        bottom = source.at[source.shape[0] - tile :, :rows]
        copies.append(pltpu.make_async_copy(bottom, landed.at[at], semaphore.at[at]))
        copies[-1].start()
    for copy in copies:
        copy.wait()
    each = shards // len(sources)
    for source in range(shards):
        value = landed[source // each].astype(jnp.float32).astype(jnp.int32)
        owners[pl.ds(came[source], 1), :] = value[source % each : source % each + 1, :]
    groups = mine.shape[0]
    team = shards // groups
    span = groups * cap
    owner_at = lax.broadcasted_iota(jnp.int32, (shards, rows), 0)
    upper = jnp.where(
        lax.broadcasted_iota(jnp.int32, (rows, rows), 0)
        < lax.broadcasted_iota(jnp.int32, (rows, rows), 1),
        1.0,
        0.0,
    ).astype(jnp.bfloat16)
    rank_at = lax.broadcasted_iota(jnp.int32, (rows, rows), 0).astype(jnp.float32)
    lane = lax.broadcasted_iota(jnp.int32, (1, rows), 1).astype(jnp.float32)
    before = jnp.zeros((shards, 1), jnp.float32)
    found = jnp.zeros((3 * shards, rows), jnp.float32)
    for shard in range(shards):
        hot = jnp.where(owners[shard : shard + 1, :] == owner_at, 1.0, 0.0)
        within = dot(hot.astype(jnp.bfloat16), upper)
        local[shard : shard + 1, :] = jnp.sum(hot * within, axis=0, keepdims=True)
        rank = jnp.sum(hot * (within + before), axis=0, keepdims=True)
        before = before + jnp.sum(hot, axis=1, keepdims=True)
        rank_hot = jnp.where(rank_at == rank, 1.0, 0.0).astype(jnp.bfloat16)
        codes = jnp.concatenate([hot * float(shard), hot * lane, hot * within], axis=0)
        found = found + dot_rows(codes.astype(jnp.bfloat16), rank_hot)
    shard_of = found[:shards]
    place = shard_of * rows + found[shards : 2 * shards]
    docs = doc_starts.shape[0]
    doc_lane = lax.broadcasted_iota(jnp.int32, (1, LANES), 1)
    doc_row = jnp.full((1, LANES), -1.0, jnp.float32)
    start = jnp.zeros_like(place)
    for doc in range(docs):
        value = doc_starts[doc].astype(jnp.float32)
        start = jnp.maximum(start, jnp.where(value <= place, value, 0.0))
        doc_row = jnp.where(doc_lane == doc, value, doc_row)
    to_shard = shard_of.astype(jnp.int32)
    to_group = jnp.zeros_like(to_shard)
    for group in range(1, groups):
        to_group = jnp.where(to_shard >= group * team, group, to_group)
    to_mate = (to_shard - to_group * team) ^ twist[0]
    inside = found[2 * shards :].astype(jnp.int32)
    coded[...] = (to_mate * groups + to_group) * span + inside
    starts[:shards, :] = start
    starts[shards : 2 * shards, :] = place - start
    flat = jnp.transpose(starts[...])
    which = lax.broadcasted_iota(jnp.int32, flat.shape, 1)
    column = lax.broadcasted_iota(jnp.int32, (rows, 1), 0)
    for group in range(groups):
        own = slice(group * rows, (group + 1) * rows)
        at = mine[group]
        offset = jnp.sum(jnp.where(which == at + shards, flat, 0.0), axis=1, keepdims=True)
        angles[own, :] = offset * freqs[...]
        slots[:, own] = coded[pl.ds(at, 1), :] + group * cap
        shard = group * team + mate[0]
        place = column + shard * rows
        begin = jnp.zeros_like(column)
        for doc in range(docs):
            begin = jnp.where(doc_starts[doc] <= place, doc_starts[doc], begin)
        query_bar[own, :] = jnp.where(begin.astype(jnp.float32) == doc_row, 0.0, OTHER).astype(
            jnp.bfloat16
        )
        owner = owners[pl.ds(shard, 1), :]
        owner_group = jnp.zeros_like(owner)
        for step in range(1, groups):
            owner_group = jnp.where(owner >= step * team, step, owner_group)
        owner_mate = (owner - owner_group * team) ^ twist[0]
        rank = local[pl.ds(shard, 1), :].astype(jnp.int32)
        columns[group : group + 1, :] = owner_mate * span + owner_group * cap + rank
    for block in range(shards):
        own = slice(block * rows, (block + 1) * rows)
        begin = jnp.sum(jnp.where(which == order[block], flat, 0.0), axis=1, keepdims=True)
        key_hot[own, :] = jnp.where(begin == doc_row, 1.0, 0.0).astype(jnp.bfloat16)


def rotate(raw, cosine, sine):
    return raw * cosine + pltpu.roll(raw, HEAD_SIZE // 2, 1) * sine


def project(tokens, weights, cols=slice(None)):
    total = None
    start = 0
    for weight in weights:
        depth = weight.shape[0] // LANES * LANES
        part = dot(tokens[:, start : start + depth], weight[:depth, cols])
        total = part if total is None else total + part
        start += depth
    return total


def tokens_kernel(layout, places, table, *refs):
    row_blocks, col_chunks, blocks = layout
    count = row_blocks * col_chunks
    pieces, weights = refs[:count], refs[count:-4]
    total, later, tokens, loose = refs[-4:]
    rows, width = pieces[0].shape
    for row in range(row_blocks):
        there = pl.ds(pl.multiple_of(places[row] * rows, rows), rows)
        for col in range(col_chunks):
            loose[there, col * width : (col + 1) * width] = pieces[row * col_chunks + col][...]
    width = loose.shape[1] // blocks
    for block in range(blocks):
        source = pl.ds(pl.multiple_of(table[block] * width, width), width)
        tokens[:, block * width : (block + 1) * width] = loose[:, source]
    if later.shape[1] < tokens.shape[1]:
        later[...] = tokens[:, tokens.shape[1] - later.shape[1] :]
    for start in range(0, total.shape[1], 2 * HEAD_SIZE):
        cols = slice(start, start + 2 * HEAD_SIZE)
        total[:, cols] = project(tokens, weights, cols)


def finish_projection(total, later, weights, cols):
    if not weights:
        return total[:, cols]
    return total[:, cols] + project(later, weights, cols)


def kv_kernel(total, later, *refs):
    weights = refs[:-3]
    cosine, sine, kv = refs[-3:]
    raw = finish_projection(total, later, weights, slice(0, 2 * HEAD_SIZE))
    kv[:, :HEAD_SIZE] = rotate(raw[:, :HEAD_SIZE], cosine[...], sine[...]).astype(kv.dtype)
    kv[:, HEAD_SIZE:] = raw[:, HEAD_SIZE:].astype(kv.dtype)


def query_kernel(layout, total, later, *refs):
    parts, start = layout
    weights = refs[:parts]
    cosine, sine, slots = refs[parts : parts + 3]
    outs, queries = refs[parts + 3 : -1], refs[-1]
    raw = finish_projection(total, later, weights, slice(start, start + queries.shape[1]))
    for head in range(queries.shape[1] // HEAD_SIZE):
        cols = slice(head * HEAD_SIZE, (head + 1) * HEAD_SIZE)
        queries[:, cols] = rotate(raw[:, cols], cosine[...], sine[...]).astype(queries.dtype)
    count = outs[0].shape[0]
    at = lax.broadcasted_iota(jnp.int32, (count, queries.shape[0]), 0)
    for step, out in enumerate(outs):
        hot = jnp.where(at + step * count == slots[...], 1.0, 0.0).astype(jnp.bfloat16)
        out[...] = dot(hot, queries[...]).astype(out.dtype)


def attention_kernel(layout, far, columns, query_bar, key_hot, *refs):
    query_parts, kv_parts, block_rows = layout
    arrived = refs[:query_parts]
    kvs = refs[query_parts : query_parts + kv_parts]
    outs = refs[query_parts + kv_parts : -5]
    keys, values, long, scores, context = refs[-5:]
    groups, rows = columns.shape
    heads = arrived[0].shape[1] // HEAD_SIZE
    start = 0
    for kv in kvs:
        own = slice(start, start + kv.shape[0])
        keys[own, :HEAD_SIZE] = kv[:, :HEAD_SIZE]
        values[own, :] = kv[:, HEAD_SIZE:]
        start += kv.shape[0]
    keys[:, HEAD_SIZE:] = key_hot[...]
    span = arrived[0].shape[0] // groups
    at = lax.broadcasted_iota(jnp.int32, (span * query_parts, rows), 0)
    for group in range(groups):
        hot = jnp.where(at == columns[group : group + 1, :], 1.0, 0.0).astype(jnp.bfloat16)
        there = slice(group * span, (group + 1) * span)
        slab = jnp.concatenate([part[there, :] for part in arrived], axis=0)
        picked = lax.dot_general(
            hot, slab, (((0,), (0,)), ((), ())), preferred_element_type=jnp.float32
        ).astype(jnp.bfloat16)
        own = slice(group * rows, (group + 1) * rows)
        for head in range(heads):
            long[head, own, :HEAD_SIZE] = picked[:, head * HEAD_SIZE : (head + 1) * HEAD_SIZE]
            long[head, own, HEAD_SIZE:] = query_bar[own, :]
    factor = 1.4426950408889634 / HEAD_SIZE**0.5
    blocks = groups * rows // block_rows
    steps = [(block, head) for block in range(blocks) for head in range(heads)]

    def score(step):
        block, head = steps[step]
        own = slice(block * block_rows, (block + 1) * block_rows)
        scores[step % 2] = dot_rows(long[head, own, :], keys[...])

    score(0)
    for step, (block, head) in enumerate(steps):
        if step + 1 < len(steps):
            score(step + 1)
        own = slice(block * block_rows, (block + 1) * block_rows)
        held = scores[step % 2]
        top = jnp.max(held, axis=1, keepdims=True)
        kept = jnp.exp2((held - top) * factor)
        total = jnp.sum(kept, axis=1, keepdims=True)
        mixed = dot(kept.astype(jnp.bfloat16), values[...])
        context[own, head * HEAD_SIZE : (head + 1) * HEAD_SIZE] = (mixed / total).astype(
            context.dtype
        )
    for step, out in enumerate(outs):
        out[...] = context[pl.ds(pl.multiple_of(far[step] * rows, rows), rows), :]


def finish_kernel(far, *refs):
    out = refs[-1]
    groups = far.shape[0]
    parts = (len(refs) - 1) // groups
    width = refs[0].shape[1]
    for part in range(parts):
        for step in range(groups):
            start = pl.multiple_of((far[step] * parts + part) * width, width)
            out[:, pl.ds(start, width)] = refs[part * groups + step][...]


def turn(value, axis, bits):
    count = lax.axis_size(axis)
    return lax.ppermute(value, axis, [(i, i ^ bits) for i in range(count)])


def after(value, *others):
    return lax.optimization_barrier((value, *others))[0]


def spread_across(value):
    return value, turn(value, "team", 2)


def spread_cores(value, across, *others):
    parts = [turn(after(part, *others), "team", 1) for part in (value, across)]
    return [value, across, *parts]


def body(stored, source_owner, doc_ids, doc_starts, wq, wk, wv):
    groups, team = lax.axis_size("line"), lax.axis_size("team")
    nctx, ntp = groups * team, lax.axis_size("tp")
    group, mate = lax.axis_index("line"), lax.axis_index("team")
    rows = stored.shape[0]
    cap = 2 * rows // nctx
    size = HEAD_SIZE
    depth = wq.shape[0]
    split = groups > 1
    pair = 2 * size
    parts = wq.shape[1] // groups // pair
    total_rows = groups * rows
    width = stored.shape[1] * ntp
    keys = nctx * rows
    far = group ^ jnp.arange(groups, dtype=jnp.int32)

    def flip(value):
        return lax.ppermute(value, "tp", [(0, 1), (1, 0)])

    columns_each = (1 + parts) * pair
    tile = 16
    slabs = call(
        weights_kernel,
        [
            jax.ShapeDtypeStruct((depth + tile * (step == 1), columns_each), jnp.bfloat16)
            for step in range(groups)
        ],
        [far, source_owner[None, :], wq, wk, wv],
        smem=(0,),
    )

    if split:
        inner, outer = [(1, 2), (2, 1)], [(1, 0), (2, 3)]
        near = turn(stored, "line", 1)
        over = lax.ppermute(stored, "line", inner)
        flips = [flip(stored)]
        weights_near = turn(slabs[1], "line", 1)
        over_near = lax.ppermute(after(near, over, flips[0], *slabs), "line", inner)
        end = lax.ppermute(after(over, near, weights_near), "line", outer)
        flips.append(flip(after(near, flips[0])))
        held, leaving = call(
            join_kernel,
            [
                jax.ShapeDtypeStruct((2 * depth + tile, columns_each), jnp.bfloat16),
                jax.ShapeDtypeStruct((depth + tile, columns_each), jnp.bfloat16),
            ],
            [source_owner[None, :], slabs[0], weights_near, slabs[3]],
        )
        weights_third = turn(after(leaving, over_near, flips[1]), "line", 3)
        first = spread_across(held)
        edge = (group == 0) | (group == groups - 1)
        third = jnp.where(edge, end, over)
        end_near = lax.ppermute(after(over_near, flips[1]), "line", outer)
        flips.append(flip(after(third, flips[1], weights_third)))
        weights_second = turn(after(slabs[2], weights_third, end_near), "line", 2)
        fourth = jnp.where(edge, end_near, over_near)
        flips.append(flip(after(fourth, flips[2])))
        second = spread_across(after(weights_third, first[1]))
        first = spread_cores(*first, second[1])
        second = spread_cores(*second)
        last_held = after(weights_second, second[1])
        early = [part for both in zip(first, second) for part in both]
        places = jnp.stack(
            [group, group ^ 1, group ^ jnp.where(edge, 2, 3), group ^ jnp.where(edge, 3, 2)]
        )
        pieces = [
            chunk for both in zip((stored, near, third, fourth), flips) for chunk in both
        ]
        chunks = ntp
        owners = early
    else:
        pieces = [lax.all_gather(stored, "tp", axis=1, tiled=True)]
        places = jnp.zeros((1,), jnp.int32)
        chunks = 1
        early = [lax.all_gather(slabs[0], "team", axis=0, tiled=True)]
        owners = [lax.all_gather(source_owner, "team", axis=0)]

    if split:
        rel = jnp.arange(groups, dtype=jnp.int32)
        turns = mate ^ jnp.array([0, 2, 1, 3], dtype=jnp.int32)
        order = (rel[None, :] * team + turns[:, None]).reshape(-1)
        came = (far[jnp.array([0, 1, 3, 2])][None, :] * team + turns[:, None]).reshape(-1)
        rows_of = jnp.concatenate(
            [came.reshape(team, groups)[:, :3].reshape(-1), came.reshape(team, groups)[:, 3]]
        )
        mine = rel * team + mate
        twist = mate[None]
        share = nctx // ntp
        table = rows_of % share + jnp.where(rows_of // share == lax.axis_index("tp"), 0, share)
    else:
        order = came = jnp.arange(nctx, dtype=jnp.int32)
        mine = mate[None]
        twist = table = jnp.zeros((1,), jnp.int32)

    freqs = ROPE_BASE ** (-np.arange(size // 2) * 2.0 / size)
    freqs = jnp.asarray(np.concatenate([freqs, freqs])[None, :], jnp.float32)
    sign = jnp.asarray(np.repeat([-1.0, 1.0], size // 2)[None, :], jnp.float32)
    angles, key_hot, query_bar, slots, columns = call(
        functools.partial(places_kernel, cap),
        [
            jax.ShapeDtypeStruct((total_rows, size), jnp.float32),
            jax.ShapeDtypeStruct((keys, LANES), jnp.bfloat16),
            jax.ShapeDtypeStruct((total_rows, LANES), jnp.bfloat16),
            jax.ShapeDtypeStruct((1, total_rows), jnp.int32),
            jax.ShapeDtypeStruct((groups, rows), jnp.int32),
        ],
        [mine, order, came, mate[None], twist, doc_starts, freqs, *owners],
        scratch=[
            pltpu.VMEM((nctx, rows), jnp.int32),
            pltpu.VMEM((max(2 * nctx, LANES), rows), jnp.float32),
            pltpu.VMEM((nctx, rows), jnp.float32),
            pltpu.VMEM((nctx, rows), jnp.int32),
            pltpu.VMEM((len(owners), tile if split else nctx, rows), owners[0].dtype),
            pltpu.SemaphoreType.DMA((len(owners),)),
        ],
        flops=10**9,
        smem=(0, 1, 2, 3, 4, 5),
        anywhere=range(7, 7 + len(owners)),
    )
    cosine = jnp.cos(angles)
    sine = jnp.sin(angles) * sign

    rest = width // groups if split else width
    total, later = call(
        functools.partial(tokens_kernel, (groups, chunks, nctx if split else 1)),
        [
            jax.ShapeDtypeStruct((total_rows, columns_each), jnp.float32),
            jax.ShapeDtypeStruct((total_rows, rest if split else LANES), jnp.bfloat16),
        ],
        [places, table, *pieces, *early],
        scratch=[
            pltpu.VMEM((total_rows, width), jnp.bfloat16),
            pltpu.VMEM((total_rows, width), jnp.bfloat16),
        ],
        smem=(0, 1),
        vmem=32,
    )
    late = []
    if split:
        last_held, across = spread_across(last_held)
        late = spread_cores(last_held, across, total, cosine)
    kv = call(
        kv_kernel,
        jax.ShapeDtypeStruct((total_rows, pair), jnp.bfloat16),
        [total, later, *late, cosine, sine],
        flops=2 * total_rows * rest * pair,
    )

    block_rows = min(2 * rows, total_rows)
    lanes_out = team if split else 1
    slot_count = nctx * groups * cap

    leaving = call(
        functools.partial(query_kernel, (len(late), pair)),
        [jax.ShapeDtypeStruct((slot_count // lanes_out, parts * pair), jnp.bfloat16)] * lanes_out,
        [total, later, *late, cosine, sine, slots],
        scratch=[pltpu.VMEM((total_rows, parts * pair), jnp.bfloat16)],
        flops=2 * total_rows * (rest + slot_count) * parts * pair,
    )
    if split:
        across = turn(kv, "team", 2)
        arrived = [leaving[0]] + [turn(leaving[e], "team", e) for e in range(1, team)]
        last = turn(after(across, arrived[1]), "team", 1)
        kvs = [kv, across, turn(kv, "team", 1), last]
    else:
        arrived = [lax.all_to_all(leaving[0], "team", 0, 0, tiled=True)]
        kvs = [lax.all_gather(kv, "team", axis=0, tiled=True)]
    context = call(
        functools.partial(attention_kernel, (len(arrived), len(kvs), block_rows)),
        [jax.ShapeDtypeStruct((rows, parts * pair), jnp.bfloat16)] * groups,
        [far, columns, query_bar, key_hot, *arrived, *kvs],
        scratch=[
            pltpu.VMEM((keys, size + LANES), jnp.bfloat16),
            pltpu.VMEM((keys, size), jnp.bfloat16),
            pltpu.VMEM((parts * pair // size, total_rows, size + LANES), jnp.bfloat16),
            pltpu.VMEM((2, block_rows, keys), jnp.float32),
            pltpu.VMEM((total_rows, parts * pair), jnp.bfloat16),
        ],
        flops=8 * total_rows * parts * pair * keys,
        smem=(0,),
        vmem=40,
    )
    moved = {step: turn(context[step], "line", step) for step in range(groups - 1, 0, -1)}
    ready = [context[0]] + [moved[step] for step in range(1, groups)]

    return call(
        finish_kernel,
        jax.ShapeDtypeStruct((rows, wq.shape[1]), jnp.bfloat16),
        [far, *ready],
        smem=(0,),
    )


def solution(mesh):
    def program(stored, source_owner, doc_ids, doc_starts, wq, wk, wv):
        ctx, tp = mesh.shape["ctx"], mesh.shape["tp"]
        groups = wk.shape[1] // HEAD_SIZE // tp
        parts = jax.sharding.Mesh(
            mesh.devices.reshape(groups, ctx // groups, tp), ("line", "team", "tp")
        )
        both = ("line", "team")
        return jax.shard_map(
            body,
            mesh=parts,
            in_specs=(
                P(both, "tp"),
                P(both),
                P(both),
                P(),
                P(both, "tp"),
                P(both, "tp"),
                P(both, "tp"),
            ),
            out_specs=P(both, "tp"),
            check_vma=False,
        )(stored, source_owner, doc_ids, doc_starts, wq, wk, wv)

    return program
```

```python
import functools

import jax
import jax.numpy as jnp
import numpy as np
from jax import lax
from jax.experimental import pallas as pl
from jax.experimental.pallas import tpu as pltpu
from jax.sharding import PartitionSpec as P

HEAD_SIZE = 128
LANES = 128
ROPE_BASE = 500000.0
OTHER = -(2.0**100)

VMEM_SPEC = pl.BlockSpec(memory_space=pltpu.VMEM)
SMEM_SPEC = pl.BlockSpec(memory_space=pltpu.SMEM)
ANY_SPEC = pl.BlockSpec(memory_space=pl.ANY)


def dot(a, b):
    return jnp.dot(a, b, preferred_element_type=jnp.float32)


def dot_rows(a, b):
    return lax.dot_general(
        a, b, (((1,), (1,)), ((), ())), preferred_element_type=jnp.float32
    )


def call(kernel, out_shape, operands, scratch=(), flops=0, smem=(), anywhere=(), vmem=16):
    specs = [
        SMEM_SPEC if at in smem else ANY_SPEC if at in anywhere else VMEM_SPEC
        for at in range(len(operands))
    ]
    many = isinstance(out_shape, (list, tuple))
    outs = out_shape if many else [out_shape]
    moved = sum(x.size * x.dtype.itemsize for x in [*operands, *outs])
    return pl.pallas_call(
        kernel,
        out_shape=out_shape,
        in_specs=specs,
        out_specs=[VMEM_SPEC] * len(out_shape) if many else VMEM_SPEC,
        scratch_shapes=list(scratch),
        compiler_params=pltpu.CompilerParams(vmem_limit_bytes=vmem * 2**20),
        cost_estimate=pl.CostEstimate(flops=flops, bytes_accessed=moved, transcendentals=0),
    )(*operands)


def weights_kernel(far, owner, wq, wk, wv, *outs):
    depth = wq.shape[0]
    for step, out in enumerate(outs):
        start = pl.multiple_of(far[step] * HEAD_SIZE, HEAD_SIZE)
        width = out.shape[1] - 2 * HEAD_SIZE
        out[:depth, :HEAD_SIZE] = wk[:, pl.ds(start, HEAD_SIZE)]
        out[:depth, HEAD_SIZE : 2 * HEAD_SIZE] = wv[:, pl.ds(start, HEAD_SIZE)]
        start = pl.multiple_of(far[step] * width, width)
        out[:depth, 2 * HEAD_SIZE :] = wq[:, pl.ds(start, width)]
        below = out.shape[0] - depth
        if below:
            row = owner[...].astype(jnp.float32).astype(jnp.bfloat16)
            out[depth:, :] = jnp.zeros((below, out.shape[1]), jnp.bfloat16)
            out[depth:, : row.shape[1]] = jnp.broadcast_to(row, (below, row.shape[1]))


def join_kernel(owner, own, near, third, held, leaving):
    depth = own.shape[0]
    count = owner.shape[1]
    tile = near.shape[0] - depth
    row = lax.broadcasted_iota(jnp.int32, (tile, count), 0)
    mine = jnp.broadcast_to(owner[...].astype(jnp.float32), (tile, count))
    theirs = near[depth:, :count].astype(jnp.float32)
    both = jnp.where(row == 0, mine, theirs).astype(jnp.bfloat16)
    held[:depth, :] = own[...]
    held[depth : 2 * depth, :] = near[:depth, :]
    leaving[:depth, :] = third[...]
    for out in (held, leaving):
        out[out.shape[0] - tile :, :] = jnp.zeros((tile, out.shape[1]), jnp.bfloat16)
        out[out.shape[0] - tile :, :count] = both


def places_kernel(cap, mine, order, came, mate, twist, doc_starts, freqs, *refs):
    outs, scratch = refs[-11:-6], refs[-6:]
    angles, key_hot, query_bar, slots, columns = outs
    coded, starts, local, owners, landed, semaphore = scratch
    shards, rows = owners.shape
    sources = refs[:-11]
    tile = landed.shape[1]
    copies = []
    for at, source in enumerate(sources):
        bottom = source.at[source.shape[0] - tile :, :rows]
        copies.append(pltpu.make_async_copy(bottom, landed.at[at], semaphore.at[at]))
        copies[-1].start()
    for copy in copies:
        copy.wait()
    each = shards // len(sources)
    for source in range(shards):
        value = landed[source // each].astype(jnp.float32).astype(jnp.int32)
        owners[pl.ds(came[source], 1), :] = value[source % each : source % each + 1, :]
    groups = mine.shape[0]
    team = shards // groups
    span = groups * cap
    owner_at = lax.broadcasted_iota(jnp.int32, (shards, rows), 0)
    upper = jnp.where(
        lax.broadcasted_iota(jnp.int32, (rows, rows), 0)
        < lax.broadcasted_iota(jnp.int32, (rows, rows), 1),
        1.0,
        0.0,
    ).astype(jnp.bfloat16)
    rank_at = lax.broadcasted_iota(jnp.int32, (rows, rows), 0).astype(jnp.float32)
    lane = lax.broadcasted_iota(jnp.int32, (1, rows), 1).astype(jnp.float32)
    before = jnp.zeros((shards, 1), jnp.float32)
    found = jnp.zeros((3 * shards, rows), jnp.float32)
    for shard in range(shards):
        hot = jnp.where(owners[shard : shard + 1, :] == owner_at, 1.0, 0.0)
        within = dot(hot.astype(jnp.bfloat16), upper)
        local[shard : shard + 1, :] = jnp.sum(hot * within, axis=0, keepdims=True)
        rank = jnp.sum(hot * (within + before), axis=0, keepdims=True)
        before = before + jnp.sum(hot, axis=1, keepdims=True)
        rank_hot = jnp.where(rank_at == rank, 1.0, 0.0).astype(jnp.bfloat16)
        codes = jnp.concatenate([hot * float(shard), hot * lane, hot * within], axis=0)
        found = found + dot_rows(codes.astype(jnp.bfloat16), rank_hot)
    shard_of = found[:shards]
    place = shard_of * rows + found[shards : 2 * shards]
    docs = doc_starts.shape[0]
    doc_lane = lax.broadcasted_iota(jnp.int32, (1, LANES), 1)
    doc_row = jnp.full((1, LANES), -1.0, jnp.float32)
    start = jnp.zeros_like(place)
    for doc in range(docs):
        value = doc_starts[doc].astype(jnp.float32)
        start = jnp.maximum(start, jnp.where(value <= place, value, 0.0))
        doc_row = jnp.where(doc_lane == doc, value, doc_row)
    to_shard = shard_of.astype(jnp.int32)
    to_group = jnp.zeros_like(to_shard)
    for group in range(1, groups):
        to_group = jnp.where(to_shard >= group * team, group, to_group)
    to_mate = (to_shard - to_group * team) ^ twist[0]
    inside = found[2 * shards :].astype(jnp.int32)
    coded[...] = (to_mate * groups + to_group) * span + inside
    starts[:shards, :] = start
    starts[shards : 2 * shards, :] = place - start
    flat = jnp.transpose(starts[...])
    which = lax.broadcasted_iota(jnp.int32, flat.shape, 1)
    column = lax.broadcasted_iota(jnp.int32, (rows, 1), 0)
    for group in range(groups):
        own = slice(group * rows, (group + 1) * rows)
        at = mine[group]
        offset = jnp.sum(jnp.where(which == at + shards, flat, 0.0), axis=1, keepdims=True)
        angles[own, :] = offset * freqs[...]
        slots[:, own] = coded[pl.ds(at, 1), :] + group * cap
        shard = group * team + mate[0]
        place = column + shard * rows
        begin = jnp.zeros_like(column)
        for doc in range(docs):
            begin = jnp.where(doc_starts[doc] <= place, doc_starts[doc], begin)
        query_bar[own, :] = jnp.where(begin.astype(jnp.float32) == doc_row, 0.0, OTHER).astype(
            jnp.bfloat16
        )
        owner = owners[pl.ds(shard, 1), :]
        owner_group = jnp.zeros_like(owner)
        for step in range(1, groups):
            owner_group = jnp.where(owner >= step * team, step, owner_group)
        owner_mate = (owner - owner_group * team) ^ twist[0]
        rank = local[pl.ds(shard, 1), :].astype(jnp.int32)
        columns[group : group + 1, :] = owner_mate * span + owner_group * cap + rank
    for block in range(shards):
        own = slice(block * rows, (block + 1) * rows)
        begin = jnp.sum(jnp.where(which == order[block], flat, 0.0), axis=1, keepdims=True)
        key_hot[own, :] = jnp.where(begin == doc_row, 1.0, 0.0).astype(jnp.bfloat16)


def rotate(raw, cosine, sine):
    return raw * cosine + pltpu.roll(raw, HEAD_SIZE // 2, 1) * sine


def project(tokens, weights, cols=slice(None)):
    total = None
    start = 0
    for weight in weights:
        depth = weight.shape[0] // LANES * LANES
        part = dot(tokens[:, start : start + depth], weight[:depth, cols])
        total = part if total is None else total + part
        start += depth
    return total


def tokens_kernel(layout, places, table, *refs):
    row_unit, col_chunks, blocks = layout
    row_blocks = places.shape[0]
    count = row_blocks * col_chunks
    pieces, weights = refs[:count], refs[count:-4]
    total, later, tokens, loose = refs[-4:]
    width = pieces[0].shape[1]
    for row in range(row_blocks):
        rows = pieces[row * col_chunks].shape[0]
        there = pl.ds(pl.multiple_of(places[row] * row_unit, row_unit), rows)
        for col in range(col_chunks):
            loose[there, col * width : (col + 1) * width] = pieces[row * col_chunks + col][...]
    width = loose.shape[1] // blocks
    for block in range(blocks):
        source = pl.ds(pl.multiple_of(table[block] * width, width), width)
        tokens[:, block * width : (block + 1) * width] = loose[:, source]
    if later.shape[1] < tokens.shape[1]:
        later[...] = tokens[:, tokens.shape[1] - later.shape[1] :]
    for start in range(0, total.shape[1], 2 * HEAD_SIZE):
        cols = slice(start, start + 2 * HEAD_SIZE)
        total[:, cols] = project(tokens, weights, cols)


def finish_projection(total, later, weights, cols):
    if not weights:
        return total[:, cols]
    return total[:, cols] + project(later, weights, cols)


def kv_kernel(total, later, *refs):
    weights = refs[:-3]
    cosine, sine, kv = refs[-3:]
    raw = finish_projection(total, later, weights, slice(0, 2 * HEAD_SIZE))
    kv[:, :HEAD_SIZE] = rotate(raw[:, :HEAD_SIZE], cosine[...], sine[...]).astype(kv.dtype)
    kv[:, HEAD_SIZE:] = raw[:, HEAD_SIZE:].astype(kv.dtype)


def query_kernel(layout, total, later, *refs):
    parts, start = layout
    weights = refs[:parts]
    cosine, sine, slots = refs[parts : parts + 3]
    outs, queries = refs[parts + 3 : -1], refs[-1]
    raw = finish_projection(total, later, weights, slice(start, start + queries.shape[1]))
    for head in range(queries.shape[1] // HEAD_SIZE):
        cols = slice(head * HEAD_SIZE, (head + 1) * HEAD_SIZE)
        queries[:, cols] = rotate(raw[:, cols], cosine[...], sine[...]).astype(queries.dtype)
    count = outs[0].shape[0]
    at = lax.broadcasted_iota(jnp.int32, (count, queries.shape[0]), 0)
    for step, out in enumerate(outs):
        hot = jnp.where(at + step * count == slots[...], 1.0, 0.0).astype(jnp.bfloat16)
        out[...] = dot(hot, queries[...]).astype(out.dtype)


def attention_kernel(layout, far, columns, query_bar, key_hot, *refs):
    query_parts, kv_parts, block_rows = layout
    arrived = refs[:query_parts]
    kvs = refs[query_parts : query_parts + kv_parts]
    outs = refs[query_parts + kv_parts : -5]
    keys, values, long, scores, context = refs[-5:]
    groups, rows = columns.shape
    heads = arrived[0].shape[1] // HEAD_SIZE
    start = 0
    for kv in kvs:
        own = slice(start, start + kv.shape[0])
        keys[own, :HEAD_SIZE] = kv[:, :HEAD_SIZE]
        values[own, :] = kv[:, HEAD_SIZE:]
        start += kv.shape[0]
    keys[:, HEAD_SIZE:] = key_hot[...]
    span = arrived[0].shape[0] // groups
    at = lax.broadcasted_iota(jnp.int32, (span * query_parts, rows), 0)
    for group in range(groups):
        hot = jnp.where(at == columns[group : group + 1, :], 1.0, 0.0).astype(jnp.bfloat16)
        there = slice(group * span, (group + 1) * span)
        slab = jnp.concatenate([part[there, :] for part in arrived], axis=0)
        picked = lax.dot_general(
            hot, slab, (((0,), (0,)), ((), ())), preferred_element_type=jnp.float32
        ).astype(jnp.bfloat16)
        own = slice(group * rows, (group + 1) * rows)
        for head in range(heads):
            long[head, own, :HEAD_SIZE] = picked[:, head * HEAD_SIZE : (head + 1) * HEAD_SIZE]
            long[head, own, HEAD_SIZE:] = query_bar[own, :]
    factor = 1.4426950408889634 / HEAD_SIZE**0.5
    blocks = groups * rows // block_rows
    steps = [(block, head) for block in range(blocks) for head in range(heads)]

    def score(step):
        block, head = steps[step]
        own = slice(block * block_rows, (block + 1) * block_rows)
        scores[step % 2] = dot_rows(long[head, own, :], keys[...])

    score(0)
    for step, (block, head) in enumerate(steps):
        if step + 1 < len(steps):
            score(step + 1)
        own = slice(block * block_rows, (block + 1) * block_rows)
        held = scores[step % 2]
        top = jnp.max(held, axis=1, keepdims=True)
        kept = jnp.exp2((held - top) * factor)
        total = jnp.sum(kept, axis=1, keepdims=True)
        mixed = dot(kept.astype(jnp.bfloat16), values[...])
        context[own, head * HEAD_SIZE : (head + 1) * HEAD_SIZE] = (mixed / total).astype(
            context.dtype
        )
    for step, out in enumerate(outs):
        out[...] = context[pl.ds(pl.multiple_of(far[step] * rows, rows), rows), :]


def finish_kernel(far, *refs):
    out = refs[-1]
    groups = far.shape[0]
    parts = (len(refs) - 1) // groups
    width = refs[0].shape[1]
    for part in range(parts):
        for step in range(groups):
            start = pl.multiple_of((far[step] * parts + part) * width, width)
            out[:, pl.ds(start, width)] = refs[part * groups + step][...]


def turn(value, axis, bits):
    count = lax.axis_size(axis)
    return lax.ppermute(value, axis, [(i, i ^ bits) for i in range(count)])


def after(value, *others):
    return lax.optimization_barrier((value, *others))[0]


def spread_across(value):
    return value, turn(value, "team", 2)


def spread_cores(value, across, *others):
    parts = [turn(after(part, *others), "team", 1) for part in (value, across)]
    return [value, across, *parts]


def body(stored, source_owner, doc_ids, doc_starts, wq, wk, wv):
    groups, team = lax.axis_size("line"), lax.axis_size("team")
    nctx, ntp = groups * team, lax.axis_size("tp")
    group, mate = lax.axis_index("line"), lax.axis_index("team")
    rows = stored.shape[0]
    cap = 2 * rows // nctx
    size = HEAD_SIZE
    depth = wq.shape[0]
    split = groups > 1
    pair = 2 * size
    parts = wq.shape[1] // groups // pair
    total_rows = groups * rows
    width = stored.shape[1] * ntp
    keys = nctx * rows
    far = group ^ jnp.arange(groups, dtype=jnp.int32)

    def flip(value):
        return lax.ppermute(value, "tp", [(0, 1), (1, 0)])

    columns_each = (1 + parts) * pair
    tile = 16
    slabs = call(
        weights_kernel,
        [
            jax.ShapeDtypeStruct((depth + tile * (step == 1), columns_each), jnp.bfloat16)
            for step in range(groups)
        ],
        [far, source_owner[None, :], wq, wk, wv],
        smem=(0,),
    )

    if split:
        inner, outer = [(1, 2), (2, 1)], [(1, 0), (2, 3)]
        near = turn(stored, "line", 1)
        over = lax.ppermute(stored, "line", inner)
        flips = [flip(stored)]
        weights_near = turn(slabs[1], "line", 1)
        over_near = lax.ppermute(after(near, over, flips[0], *slabs), "line", inner)
        end = lax.ppermute(after(over, near, weights_near), "line", outer)
        flips.append(flip(after(near, flips[0])))
        held, leaving = call(
            join_kernel,
            [
                jax.ShapeDtypeStruct((2 * depth + tile, columns_each), jnp.bfloat16),
                jax.ShapeDtypeStruct((depth + tile, columns_each), jnp.bfloat16),
            ],
            [source_owner[None, :], slabs[0], weights_near, slabs[3]],
        )
        weights_third = turn(after(leaving, over_near, flips[1]), "line", 3)
        first = spread_across(held)
        edge = (group == 0) | (group == groups - 1)
        third = jnp.where(edge, end, over)
        middle = rows // 2
        end_near = [lax.ppermute(after(over_near[:middle], flips[1]), "line", outer)]
        end_near.append(
            lax.ppermute(after(over_near[middle:], end_near[0]), "line", outer)
        )
        flips.append(flip(after(third, flips[1], weights_third)))
        weights_second = turn(after(slabs[2], weights_third, end_near[0]), "line", 2)
        fourth = jnp.where(edge, jnp.concatenate(end_near), over_near)
        flips.append(flip(after(fourth, flips[-1])))
        second = spread_across(after(weights_third, first[1]))
        first = spread_cores(*first)
        second = spread_cores(*second, *first[2:])
        last_held = after(weights_second, second[1], flips[-1])
        early = [part for both in zip(first, second) for part in both]
        places = jnp.stack(
            [group, group ^ 1, group ^ jnp.where(edge, 2, 3), group ^ jnp.where(edge, 3, 2)]
        )
        pieces = [
            chunk for both in zip((stored, near, third, fourth), flips) for chunk in both
        ]
        chunks = ntp
        owners = early
    else:
        pieces = [lax.all_gather(stored, "tp", axis=1, tiled=True)]
        places = jnp.zeros((1,), jnp.int32)
        chunks = 1
        early = [lax.all_gather(slabs[0], "team", axis=0, tiled=True)]
        owners = [lax.all_gather(source_owner, "team", axis=0)]

    if split:
        rel = jnp.arange(groups, dtype=jnp.int32)
        turns = mate ^ jnp.array([0, 2, 1, 3], dtype=jnp.int32)
        order = (rel[None, :] * team + turns[:, None]).reshape(-1)
        came = (far[jnp.array([0, 1, 3, 2])][None, :] * team + turns[:, None]).reshape(-1)
        rows_of = jnp.concatenate(
            [came.reshape(team, groups)[:, :3].reshape(-1), came.reshape(team, groups)[:, 3]]
        )
        mine = rel * team + mate
        twist = mate[None]
        share = nctx // ntp
        table = rows_of % share + jnp.where(rows_of // share == lax.axis_index("tp"), 0, share)
    else:
        order = came = jnp.arange(nctx, dtype=jnp.int32)
        mine = mate[None]
        twist = table = jnp.zeros((1,), jnp.int32)

    freqs = ROPE_BASE ** (-np.arange(size // 2) * 2.0 / size)
    freqs = jnp.asarray(np.concatenate([freqs, freqs])[None, :], jnp.float32)
    sign = jnp.asarray(np.repeat([-1.0, 1.0], size // 2)[None, :], jnp.float32)
    angles, key_hot, query_bar, slots, columns = call(
        functools.partial(places_kernel, cap),
        [
            jax.ShapeDtypeStruct((total_rows, size), jnp.float32),
            jax.ShapeDtypeStruct((keys, LANES), jnp.bfloat16),
            jax.ShapeDtypeStruct((total_rows, LANES), jnp.bfloat16),
            jax.ShapeDtypeStruct((1, total_rows), jnp.int32),
            jax.ShapeDtypeStruct((groups, rows), jnp.int32),
        ],
        [mine, order, came, mate[None], twist, doc_starts, freqs, *owners],
        scratch=[
            pltpu.VMEM((nctx, rows), jnp.int32),
            pltpu.VMEM((max(2 * nctx, LANES), rows), jnp.float32),
            pltpu.VMEM((nctx, rows), jnp.float32),
            pltpu.VMEM((nctx, rows), jnp.int32),
            pltpu.VMEM((len(owners), tile if split else nctx, rows), owners[0].dtype),
            pltpu.SemaphoreType.DMA((len(owners),)),
        ],
        flops=4 * 10**9,
        smem=(0, 1, 2, 3, 4, 5),
        anywhere=range(7, 7 + len(owners)),
    )
    cosine = jnp.cos(angles)
    sine = jnp.sin(angles) * sign

    rest = width // groups if split else width
    total, later = call(
        functools.partial(tokens_kernel, (rows, chunks, nctx if split else 1)),
        [
            jax.ShapeDtypeStruct((total_rows, columns_each), jnp.float32),
            jax.ShapeDtypeStruct((total_rows, rest if split else LANES), jnp.bfloat16),
        ],
        [places, table, *pieces, *early],
        scratch=[
            pltpu.VMEM((total_rows, width), jnp.bfloat16),
            pltpu.VMEM((total_rows, width), jnp.bfloat16),
        ],
        flops=3 * total_rows * width * columns_each,
        smem=(0, 1),
        vmem=20 if split else 32,
    )
    late = []
    if split:
        last_held, across = spread_across(after(last_held, cosine))
        late = spread_cores(last_held, across, total)
    kv = call(
        kv_kernel,
        jax.ShapeDtypeStruct((total_rows, pair), jnp.bfloat16),
        [total, later, *late, cosine, sine],
        flops=2 * total_rows * rest * pair,
    )

    block_rows = min(2 * rows, total_rows)
    lanes_out = team if split else 1
    slot_count = nctx * groups * cap

    leaving = call(
        functools.partial(query_kernel, (len(late), pair)),
        [jax.ShapeDtypeStruct((slot_count // lanes_out, parts * pair), jnp.bfloat16)] * lanes_out,
        [after(total, kv), later, *late, cosine, sine, slots],
        scratch=[pltpu.VMEM((total_rows, parts * pair), jnp.bfloat16)],
        flops=2 * total_rows * (rest + slot_count) * parts * pair,
    )
    if split:
        across = turn(kv, "team", 2)
        arrived = [leaving[0]] + [turn(leaving[e], "team", e) for e in range(1, team)]
        last = turn(after(across, arrived[1]), "team", 1)
        kvs = [kv, across, turn(kv, "team", 1), last]
    else:
        arrived = [lax.all_to_all(leaving[0], "team", 0, 0, tiled=True)]
        kvs = [lax.all_gather(kv, "team", axis=0, tiled=True)]
    context = call(
        functools.partial(attention_kernel, (len(arrived), len(kvs), block_rows)),
        [jax.ShapeDtypeStruct((rows, parts * pair), jnp.bfloat16)] * groups,
        [far, columns, query_bar, key_hot, *arrived, *kvs],
        scratch=[
            pltpu.VMEM((keys, size + LANES), jnp.bfloat16),
            pltpu.VMEM((keys, size), jnp.bfloat16),
            pltpu.VMEM((parts * pair // size, total_rows, size + LANES), jnp.bfloat16),
            pltpu.VMEM((2, block_rows, keys), jnp.float32),
            pltpu.VMEM((total_rows, parts * pair), jnp.bfloat16),
        ],
        flops=8 * total_rows * parts * pair * keys,
        smem=(0,),
        vmem=20 if split else 40,
    )
    moved = {step: turn(context[step], "line", step) for step in range(groups - 1, 0, -1)}
    ready = [context[0]] + [moved[step] for step in range(1, groups)]

    return call(
        finish_kernel,
        jax.ShapeDtypeStruct((rows, wq.shape[1]), jnp.bfloat16),
        [far, *ready],
        smem=(0,),
    )


def solution(mesh):
    def program(stored, source_owner, doc_ids, doc_starts, wq, wk, wv):
        ctx, tp = mesh.shape["ctx"], mesh.shape["tp"]
        groups = wk.shape[1] // HEAD_SIZE // tp
        parts = jax.sharding.Mesh(
            mesh.devices.reshape(groups, ctx // groups, tp), ("line", "team", "tp")
        )
        both = ("line", "team")
        return jax.shard_map(
            body,
            mesh=parts,
            in_specs=(
                P(both, "tp"),
                P(both),
                P(both),
                P(),
                P(both, "tp"),
                P(both, "tp"),
                P(both, "tp"),
            ),
            out_specs=P(both, "tp"),
            check_vma=False,
        )(stored, source_owner, doc_ids, doc_starts, wq, wk, wv)

    return program
```

```python
import functools

import jax
import jax.numpy as jnp
import numpy as np
from jax import lax
from jax.experimental import pallas as pl
from jax.experimental.pallas import tpu as pltpu
from jax.sharding import PartitionSpec as P

HEAD_SIZE = 128
LANES = 128
ROPE_BASE = 500000.0
OTHER = -(2.0**100)

VMEM_SPEC = pl.BlockSpec(memory_space=pltpu.VMEM)
SMEM_SPEC = pl.BlockSpec(memory_space=pltpu.SMEM)
ANY_SPEC = pl.BlockSpec(memory_space=pl.ANY)


def dot(a, b):
    return jnp.dot(a, b, preferred_element_type=jnp.float32)


def dot_rows(a, b):
    return lax.dot_general(
        a, b, (((1,), (1,)), ((), ())), preferred_element_type=jnp.float32
    )


def call(kernel, out_shape, operands, scratch=(), flops=0, smem=(), anywhere=(), vmem=24):
    specs = [
        SMEM_SPEC if at in smem else ANY_SPEC if at in anywhere else VMEM_SPEC
        for at in range(len(operands))
    ]
    many = isinstance(out_shape, (list, tuple))
    outs = out_shape if many else [out_shape]
    moved = sum(x.size * x.dtype.itemsize for x in [*operands, *outs])
    return pl.pallas_call(
        kernel,
        out_shape=out_shape,
        in_specs=specs,
        out_specs=[VMEM_SPEC] * len(out_shape) if many else VMEM_SPEC,
        scratch_shapes=list(scratch),
        compiler_params=pltpu.CompilerParams(vmem_limit_bytes=vmem * 2**20),
        cost_estimate=pl.CostEstimate(flops=flops, bytes_accessed=moved, transcendentals=0),
    )(*operands)


def weights_kernel(far, owner, wq, wk, wv, *outs):
    depth = wq.shape[0]
    for step, out in enumerate(outs):
        start = pl.multiple_of(far[step] * HEAD_SIZE, HEAD_SIZE)
        width = out.shape[1] - 2 * HEAD_SIZE
        out[:depth, :HEAD_SIZE] = wk[:, pl.ds(start, HEAD_SIZE)]
        out[:depth, HEAD_SIZE : 2 * HEAD_SIZE] = wv[:, pl.ds(start, HEAD_SIZE)]
        start = pl.multiple_of(far[step] * width, width)
        out[:depth, 2 * HEAD_SIZE :] = wq[:, pl.ds(start, width)]
        below = out.shape[0] - depth
        if below:
            row = owner[...].astype(jnp.float32).astype(jnp.bfloat16)
            out[depth:, :] = jnp.zeros((below, out.shape[1]), jnp.bfloat16)
            out[depth:, : row.shape[1]] = jnp.broadcast_to(row, (below, row.shape[1]))


def join_kernel(depth, first, *refs):
    blocks, second, out = refs[:-2], refs[-2], refs[-1]
    tile = out.shape[0] - depth * len(blocks)
    count = LANES
    for step, block in enumerate(blocks):
        out[step * depth : (step + 1) * depth, :] = block[:depth, :]
    row = lax.broadcasted_iota(jnp.int32, (tile, count), 0)

    def spread_row(ref):
        if ref.shape[0] == 1:
            return jnp.broadcast_to(ref[...].astype(jnp.float32), (tile, count))
        return ref[depth:, :count].astype(jnp.float32)

    both = jnp.where(row == 0, spread_row(first), spread_row(second)).astype(out.dtype)
    out[depth * len(blocks) :, :] = jnp.zeros((tile, out.shape[1]), out.dtype)
    out[depth * len(blocks) :, :count] = both


def split_kernel(value, left, right):
    left[...] = value[:, : left.shape[1]]
    right[...] = value[:, left.shape[1] :]


def places_kernel(cap, mine, order, came, mate, twist, doc_starts, freqs, *refs):
    outs, scratch = refs[-11:-6], refs[-6:]
    angles, key_hot, query_bar, slots, columns = outs
    coded, starts, local, owners, landed, semaphore = scratch
    shards, rows = owners.shape
    sources = refs[:-11]
    tile = landed.shape[1]
    copies = []
    for at, source in enumerate(sources):
        bottom = source.at[source.shape[0] - tile :, :rows]
        copies.append(pltpu.make_async_copy(bottom, landed.at[at], semaphore.at[at]))
        copies[-1].start()
    for copy in copies:
        copy.wait()
    each = shards // len(sources)
    for source in range(shards):
        value = landed[source // each].astype(jnp.float32).astype(jnp.int32)
        owners[pl.ds(came[source], 1), :] = value[source % each : source % each + 1, :]
    groups = mine.shape[0]
    team = shards // groups
    span = groups * cap
    owner_at = lax.broadcasted_iota(jnp.int32, (shards, rows), 0)
    upper = jnp.where(
        lax.broadcasted_iota(jnp.int32, (rows, rows), 0)
        < lax.broadcasted_iota(jnp.int32, (rows, rows), 1),
        1.0,
        0.0,
    ).astype(jnp.bfloat16)
    rank_at = lax.broadcasted_iota(jnp.int32, (rows, rows), 0).astype(jnp.float32)
    lane = lax.broadcasted_iota(jnp.int32, (1, rows), 1).astype(jnp.float32)
    before = jnp.zeros((shards, 1), jnp.float32)
    found = jnp.zeros((3 * shards, rows), jnp.float32)
    for shard in range(shards):
        hot = jnp.where(owners[shard : shard + 1, :] == owner_at, 1.0, 0.0)
        within = dot(hot.astype(jnp.bfloat16), upper)
        local[shard : shard + 1, :] = jnp.sum(hot * within, axis=0, keepdims=True)
        rank = jnp.sum(hot * (within + before), axis=0, keepdims=True)
        before = before + jnp.sum(hot, axis=1, keepdims=True)
        rank_hot = jnp.where(rank_at == rank, 1.0, 0.0).astype(jnp.bfloat16)
        codes = jnp.concatenate([hot * float(shard), hot * lane, hot * within], axis=0)
        found = found + dot_rows(codes.astype(jnp.bfloat16), rank_hot)
    shard_of = found[:shards]
    place = shard_of * rows + found[shards : 2 * shards]
    docs = doc_starts.shape[0]
    doc_lane = lax.broadcasted_iota(jnp.int32, (1, LANES), 1)
    doc_row = jnp.full((1, LANES), -1.0, jnp.float32)
    start = jnp.zeros_like(place)
    for doc in range(docs):
        value = doc_starts[doc].astype(jnp.float32)
        start = jnp.maximum(start, jnp.where(value <= place, value, 0.0))
        doc_row = jnp.where(doc_lane == doc, value, doc_row)
    to_shard = shard_of.astype(jnp.int32)
    to_group = jnp.zeros_like(to_shard)
    for group in range(1, groups):
        to_group = jnp.where(to_shard >= group * team, group, to_group)
    to_mate = (to_shard - to_group * team) ^ twist[0]
    inside = found[2 * shards :].astype(jnp.int32)
    coded[...] = (to_mate * groups + to_group) * span + inside
    starts[:shards, :] = start
    starts[shards : 2 * shards, :] = place - start
    flat = jnp.transpose(starts[...])
    which = lax.broadcasted_iota(jnp.int32, flat.shape, 1)
    column = lax.broadcasted_iota(jnp.int32, (rows, 1), 0)
    for group in range(groups):
        own = slice(group * rows, (group + 1) * rows)
        at = mine[group]
        offset = jnp.sum(jnp.where(which == at + shards, flat, 0.0), axis=1, keepdims=True)
        angles[own, :] = offset * freqs[...]
        slots[:, own] = coded[pl.ds(at, 1), :] + group * cap
        shard = group * team + mate[0]
        place = column + shard * rows
        begin = jnp.zeros_like(column)
        for doc in range(docs):
            begin = jnp.where(doc_starts[doc] <= place, doc_starts[doc], begin)
        query_bar[own, :] = jnp.where(begin.astype(jnp.float32) == doc_row, 0.0, OTHER).astype(
            jnp.bfloat16
        )
        owner = owners[pl.ds(shard, 1), :]
        owner_group = jnp.zeros_like(owner)
        for step in range(1, groups):
            owner_group = jnp.where(owner >= step * team, step, owner_group)
        owner_mate = (owner - owner_group * team) ^ twist[0]
        rank = local[pl.ds(shard, 1), :].astype(jnp.int32)
        columns[group : group + 1, :] = owner_mate * span + owner_group * cap + rank
    for block in range(shards):
        own = slice(block * rows, (block + 1) * rows)
        begin = jnp.sum(jnp.where(which == order[block], flat, 0.0), axis=1, keepdims=True)
        key_hot[own, :] = jnp.where(begin == doc_row, 1.0, 0.0).astype(jnp.bfloat16)


def rotate(raw, cosine, sine):
    return raw * cosine + pltpu.roll(raw, HEAD_SIZE // 2, 1) * sine


def project(tokens, weights, cols=slice(None)):
    total = None
    start = 0
    for weight in weights:
        depth = weight.shape[0] // LANES * LANES
        part = dot(tokens[:, start : start + depth], weight[:depth, cols])
        total = part if total is None else total + part
        start += depth
    return total


def tokens_kernel(layout, places, table, *refs):
    row_blocks, col_chunks, blocks = layout
    count = row_blocks * col_chunks
    pieces, weights = refs[:count], refs[count:-4]
    total, later, tokens, loose = refs[-4:]
    rows, width = pieces[0].shape
    for row in range(row_blocks):
        there = pl.ds(pl.multiple_of(places[row] * rows, rows), rows)
        for col in range(col_chunks):
            loose[there, col * width : (col + 1) * width] = pieces[row * col_chunks + col][...]
    width = loose.shape[1] // blocks
    for block in range(blocks):
        source = pl.ds(pl.multiple_of(table[block] * width, width), width)
        tokens[:, block * width : (block + 1) * width] = loose[:, source]
    if later.shape[1] < tokens.shape[1]:
        later[...] = tokens[:, tokens.shape[1] - later.shape[1] :]
    for start in range(0, total.shape[1], 2 * HEAD_SIZE):
        cols = slice(start, start + 2 * HEAD_SIZE)
        total[:, cols] = project(tokens, weights, cols)


def finish_projection(total, later, weights, cols, skip=0):
    if not weights:
        return total[:, cols]
    return total[:, cols] + project(later, weights, slice(cols.start - skip, cols.stop - skip))


def kv_kernel(total, later, *refs):
    weights = refs[:-3]
    cosine, sine, kv = refs[-3:]
    raw = finish_projection(total, later, weights, slice(0, 2 * HEAD_SIZE))
    kv[:, :HEAD_SIZE] = rotate(raw[:, :HEAD_SIZE], cosine[...], sine[...]).astype(kv.dtype)
    kv[:, HEAD_SIZE:] = raw[:, HEAD_SIZE:].astype(kv.dtype)


def query_kernel(layout, total, later, *refs):
    parts, start = layout
    weights = refs[:parts]
    cosine, sine, slots = refs[parts : parts + 3]
    outs, queries = refs[parts + 3 : -1], refs[-1]
    cols = slice(start, start + queries.shape[1])
    raw = finish_projection(total, later, weights, cols, 2 * HEAD_SIZE)
    for head in range(queries.shape[1] // HEAD_SIZE):
        cols = slice(head * HEAD_SIZE, (head + 1) * HEAD_SIZE)
        queries[:, cols] = rotate(raw[:, cols], cosine[...], sine[...]).astype(queries.dtype)
    count = outs[0].shape[0]
    at = lax.broadcasted_iota(jnp.int32, (count, queries.shape[0]), 0)
    for step, out in enumerate(outs):
        hot = jnp.where(at + step * count == slots[...], 1.0, 0.0).astype(jnp.bfloat16)
        out[...] = dot(hot, queries[...]).astype(out.dtype)


def attention_kernel(layout, far, columns, query_bar, key_hot, *refs):
    query_parts, kv_parts, block_rows = layout
    arrived = refs[:query_parts]
    kvs = refs[query_parts : query_parts + kv_parts]
    outs = refs[query_parts + kv_parts : -5]
    keys, values, long, scores, context = refs[-5:]
    groups, rows = columns.shape
    heads = arrived[0].shape[1] // HEAD_SIZE
    start = 0
    for kv in kvs:
        own = slice(start, start + kv.shape[0])
        keys[own, :HEAD_SIZE] = kv[:, :HEAD_SIZE]
        values[own, :] = kv[:, HEAD_SIZE:]
        start += kv.shape[0]
    keys[:, HEAD_SIZE:] = key_hot[...]
    span = arrived[0].shape[0] // groups
    at = lax.broadcasted_iota(jnp.int32, (span * query_parts, rows), 0)
    for group in range(groups):
        hot = jnp.where(at == columns[group : group + 1, :], 1.0, 0.0).astype(jnp.bfloat16)
        there = slice(group * span, (group + 1) * span)
        slab = jnp.concatenate([part[there, :] for part in arrived], axis=0)
        picked = lax.dot_general(
            hot, slab, (((0,), (0,)), ((), ())), preferred_element_type=jnp.float32
        ).astype(jnp.bfloat16)
        own = slice(group * rows, (group + 1) * rows)
        for head in range(heads):
            long[head, own, :HEAD_SIZE] = picked[:, head * HEAD_SIZE : (head + 1) * HEAD_SIZE]
            long[head, own, HEAD_SIZE:] = query_bar[own, :]
    factor = 1.4426950408889634 / HEAD_SIZE**0.5
    blocks = groups * rows // block_rows
    steps = [(block, head) for block in range(blocks) for head in range(heads)]

    def score(step):
        block, head = steps[step]
        own = slice(block * block_rows, (block + 1) * block_rows)
        scores[step % 2] = dot_rows(long[head, own, :], keys[...])

    score(0)
    for step, (block, head) in enumerate(steps):
        if step + 1 < len(steps):
            score(step + 1)
        own = slice(block * block_rows, (block + 1) * block_rows)
        held = scores[step % 2]
        top = jnp.max(held, axis=1, keepdims=True)
        kept = jnp.exp2((held - top) * factor)
        total = jnp.sum(kept, axis=1, keepdims=True)
        mixed = dot(kept.astype(jnp.bfloat16), values[...])
        context[own, head * HEAD_SIZE : (head + 1) * HEAD_SIZE] = (mixed / total).astype(
            context.dtype
        )
    for step, out in enumerate(outs):
        out[...] = context[pl.ds(pl.multiple_of(far[step] * rows, rows), rows), :]


def finish_kernel(far, *refs):
    out = refs[-1]
    groups = far.shape[0]
    parts = (len(refs) - 1) // groups
    width = refs[0].shape[1]
    for part in range(parts):
        for step in range(groups):
            start = pl.multiple_of((far[step] * parts + part) * width, width)
            out[:, pl.ds(start, width)] = refs[part * groups + step][...]


def turn(value, axis, bits):
    count = lax.axis_size(axis)
    return lax.ppermute(value, axis, [(i, i ^ bits) for i in range(count)])


def after(value, *others):
    return lax.optimization_barrier((value, *others))[0]


def spread(value, *others):
    across = turn(value, "team", 2)
    last = turn(after(across, *others), "team", 1)
    return [value, across, turn(value, "team", 1), last]


def body(stored, source_owner, doc_ids, doc_starts, wq, wk, wv):
    groups, team = lax.axis_size("line"), lax.axis_size("team")
    nctx, ntp = groups * team, lax.axis_size("tp")
    group, mate = lax.axis_index("line"), lax.axis_index("team")
    rows = stored.shape[0]
    cap = 2 * rows // nctx
    size = HEAD_SIZE
    depth = wq.shape[0]
    split = groups > 1
    pair = 2 * size
    parts = wq.shape[1] // groups // pair
    total_rows = groups * rows
    width = stored.shape[1] * ntp
    keys = nctx * rows
    far = group ^ jnp.arange(groups, dtype=jnp.int32)

    def flip(value):
        return lax.ppermute(value, "tp", [(0, 1), (1, 0)])

    columns_each = (1 + parts) * pair
    tile = 16
    slabs = call(
        weights_kernel,
        [
            jax.ShapeDtypeStruct((depth + tile * (step % 2), columns_each), jnp.bfloat16)
            for step in range(groups)
        ],
        [far, source_owner[None, :], wq, wk, wv],
        smem=(0,),
    )

    if split:
        def join(first, blocks, second):
            shape = (depth * len(blocks) + tile, columns_each)
            return call(
                functools.partial(join_kernel, depth),
                jax.ShapeDtypeStruct(shape, jnp.bfloat16),
                [first, *blocks, second],
            )

        inner, outer = [(1, 2), (2, 1)], [(1, 0), (2, 3)]
        near = turn(stored, "line", 1)
        over = lax.ppermute(stored, "line", inner)
        flips = [flip(stored)]
        weights_near = turn(slabs[1], "line", 1)
        weights_third = turn(slabs[3], "line", 3)
        over_near = lax.ppermute(after(near, over, flips[0], *slabs), "line", inner)
        end = lax.ppermute(after(over, near, weights_near), "line", outer)
        flips.append(flip(after(near, flips[0], weights_third)))
        held = join(source_owner[None, :], [slabs[0], weights_near], weights_near)
        second_owner = turn(after(source_owner, weights_near), "line", 2)[None, :]
        first = spread(held)
        edge = (group == 0) | (group == groups - 1)
        third = jnp.where(edge, end, over)
        end_near = lax.ppermute(after(over_near, flips[1]), "line", outer)
        flips.append(flip(after(third, flips[1], second_owner)))
        weights_second = turn(after(slabs[2], over_near, end, first[1]), "line", 2)
        fourth = jnp.where(edge, end_near, over_near)
        flips.append(flip(after(fourth, flips[2])))
        third_held = join(weights_third, [weights_third], second_owner)
        second = spread(after(third_held, flips[2], first[1]))
        kv_second, query_second = call(
            split_kernel,
            [
                jax.ShapeDtypeStruct((depth, pair), jnp.bfloat16),
                jax.ShapeDtypeStruct((depth, parts * pair), jnp.bfloat16),
            ],
            [after(weights_second, flips[3], second[1])],
        )
        early = [part for both in zip(first, second) for part in both]
        places = jnp.stack(
            [group, group ^ 1, group ^ jnp.where(edge, 2, 3), group ^ jnp.where(edge, 3, 2)]
        )
        pieces = [
            chunk for both in zip((stored, near, third, fourth), flips) for chunk in both
        ]
        chunks = ntp
        owners = early
    else:
        pieces = [lax.all_gather(stored, "tp", axis=1, tiled=True)]
        places = jnp.zeros((1,), jnp.int32)
        chunks = 1
        early = [lax.all_gather(slabs[0], "team", axis=0, tiled=True)]
        owners = [lax.all_gather(source_owner, "team", axis=0)]

    if split:
        rel = jnp.arange(groups, dtype=jnp.int32)
        turns = mate ^ jnp.array([0, 2, 1, 3], dtype=jnp.int32)
        order = (rel[None, :] * team + turns[:, None]).reshape(-1)
        came = (far[jnp.array([0, 1, 3, 2])][None, :] * team + turns[:, None]).reshape(-1)
        rows_of = jnp.concatenate(
            [came.reshape(team, groups)[:, :3].reshape(-1), came.reshape(team, groups)[:, 3]]
        )
        mine = rel * team + mate
        twist = mate[None]
        share = nctx // ntp
        table = rows_of % share + jnp.where(rows_of // share == lax.axis_index("tp"), 0, share)
    else:
        order = came = jnp.arange(nctx, dtype=jnp.int32)
        mine = mate[None]
        twist = table = jnp.zeros((1,), jnp.int32)

    freqs = ROPE_BASE ** (-np.arange(size // 2) * 2.0 / size)
    freqs = jnp.asarray(np.concatenate([freqs, freqs])[None, :], jnp.float32)
    sign = jnp.asarray(np.repeat([-1.0, 1.0], size // 2)[None, :], jnp.float32)
    angles, key_hot, query_bar, slots, columns = call(
        functools.partial(places_kernel, cap),
        [
            jax.ShapeDtypeStruct((total_rows, size), jnp.float32),
            jax.ShapeDtypeStruct((keys, LANES), jnp.bfloat16),
            jax.ShapeDtypeStruct((total_rows, LANES), jnp.bfloat16),
            jax.ShapeDtypeStruct((1, total_rows), jnp.int32),
            jax.ShapeDtypeStruct((groups, rows), jnp.int32),
        ],
        [mine, order, came, mate[None], twist, doc_starts, freqs, *owners],
        scratch=[
            pltpu.VMEM((nctx, rows), jnp.int32),
            pltpu.VMEM((max(2 * nctx, LANES), rows), jnp.float32),
            pltpu.VMEM((nctx, rows), jnp.float32),
            pltpu.VMEM((nctx, rows), jnp.int32),
            pltpu.VMEM((len(owners), tile if split else nctx, rows), owners[0].dtype),
            pltpu.SemaphoreType.DMA((len(owners),)),
        ],
        flops=10**9,
        smem=(0, 1, 2, 3, 4, 5),
        anywhere=range(7, 7 + len(owners)),
    )
    cosine = jnp.cos(angles)
    sine = jnp.sin(angles) * sign

    rest = width // groups if split else width
    total, later = call(
        functools.partial(tokens_kernel, (groups, chunks, nctx if split else 1)),
        [
            jax.ShapeDtypeStruct((total_rows, columns_each), jnp.float32),
            jax.ShapeDtypeStruct((total_rows, rest if split else LANES), jnp.bfloat16),
        ],
        [places, table, *pieces, *early],
        scratch=[
            pltpu.VMEM((total_rows, width), jnp.bfloat16),
            pltpu.VMEM((total_rows, width), jnp.bfloat16),
        ],
        flops=2 * total_rows * width * columns_each,
        smem=(0, 1),
        vmem=32,
    )
    kv_late = spread(kv_second, total, cosine) if split else []
    kv = call(
        kv_kernel,
        jax.ShapeDtypeStruct((total_rows, pair), jnp.bfloat16),
        [total, later, *kv_late, cosine, sine],
        flops=2 * total_rows * rest * pair,
    )
    late = spread(query_second, kv) if split else []

    block_rows = min(2 * rows, total_rows)
    lanes_out = team if split else 1
    slot_count = nctx * groups * cap

    def project_part(part):
        return call(
            functools.partial(query_kernel, (len(late), (1 + part) * pair)),
            [jax.ShapeDtypeStruct((slot_count // lanes_out, pair), jnp.bfloat16)] * lanes_out,
            [total, later, *late, cosine, sine, slots],
            scratch=[pltpu.VMEM((total_rows, pair), jnp.bfloat16)],
            flops=2 * total_rows * (rest + slot_count) * pair,
        )

    def attend(arrived):
        context = call(
            functools.partial(attention_kernel, (len(arrived), len(kvs), block_rows)),
            [jax.ShapeDtypeStruct((rows, pair), jnp.bfloat16)] * groups,
            [far, columns, query_bar, key_hot, *arrived, *kvs],
            scratch=[
                pltpu.VMEM((keys, size + LANES), jnp.bfloat16),
                pltpu.VMEM((keys, size), jnp.bfloat16),
                pltpu.VMEM((pair // size, total_rows, size + LANES), jnp.bfloat16),
                pltpu.VMEM((2, block_rows, keys), jnp.float32),
                pltpu.VMEM((total_rows, pair), jnp.bfloat16),
            ],
            flops=8 * total_rows * pair * keys,
            smem=(0,),
            vmem=40,
        )
        return [context[0]] + [turn(context[step], "line", step) for step in range(1, groups)]

    def exchange(leaving):
        if split:
            return [leaving[0]] + [turn(leaving[e], "team", e) for e in range(1, team)]
        return [lax.all_to_all(leaving[0], "team", 0, 0, tiled=True)]

    leaving = [project_part(part) for part in range(parts)]
    arrived = [exchange(part) for part in leaving]
    if split:
        across = turn(kv, "team", 2)
        kvs = [kv, across] + [
            turn(after(part, arrived[0][1], leaving[-1][0]), "team", 1) for part in (kv, across)
        ]
    else:
        kvs = [lax.all_gather(kv, "team", axis=0, tiled=True)]
    ready = [piece for queries in arrived for piece in attend(queries)]

    return call(
        finish_kernel,
        jax.ShapeDtypeStruct((rows, wq.shape[1]), jnp.bfloat16),
        [far, *ready],
        smem=(0,),
    )


def solution(mesh):
    def program(stored, source_owner, doc_ids, doc_starts, wq, wk, wv):
        ctx, tp = mesh.shape["ctx"], mesh.shape["tp"]
        groups = wk.shape[1] // HEAD_SIZE // tp
        parts = jax.sharding.Mesh(
            mesh.devices.reshape(groups, ctx // groups, tp), ("line", "team", "tp")
        )
        both = ("line", "team")
        return jax.shard_map(
            body,
            mesh=parts,
            in_specs=(
                P(both, "tp"),
                P(both),
                P(both),
                P(),
                P(both, "tp"),
                P(both, "tp"),
                P(both, "tp"),
            ),
            out_specs=P(both, "tp"),
            check_vma=False,
        )(stored, source_owner, doc_ids, doc_starts, wq, wk, wv)

    return program
```

```python
import functools

import jax
import jax.numpy as jnp
import numpy as np
from jax import lax
from jax.experimental import pallas as pl
from jax.experimental.pallas import tpu as pltpu
from jax.sharding import PartitionSpec as P

HEAD_SIZE = 128
LANES = 128
ROPE_BASE = 500000.0
OTHER = -(2.0**100)

VMEM_SPEC = pl.BlockSpec(memory_space=pltpu.VMEM)
SMEM_SPEC = pl.BlockSpec(memory_space=pltpu.SMEM)
ANY_SPEC = pl.BlockSpec(memory_space=pl.ANY)


def dot(a, b):
    return jnp.dot(a, b, preferred_element_type=jnp.float32)


def dot_rows(a, b):
    return lax.dot_general(
        a, b, (((1,), (1,)), ((), ())), preferred_element_type=jnp.float32
    )


def call(kernel, out_shape, operands, scratch=(), flops=0, smem=(), anywhere=(), vmem=24):
    specs = [
        SMEM_SPEC if at in smem else ANY_SPEC if at in anywhere else VMEM_SPEC
        for at in range(len(operands))
    ]
    many = isinstance(out_shape, (list, tuple))
    outs = out_shape if many else [out_shape]
    moved = sum(x.size * x.dtype.itemsize for x in [*operands, *outs])
    return pl.pallas_call(
        kernel,
        out_shape=out_shape,
        in_specs=specs,
        out_specs=[VMEM_SPEC] * len(out_shape) if many else VMEM_SPEC,
        scratch_shapes=list(scratch),
        compiler_params=pltpu.CompilerParams(vmem_limit_bytes=vmem * 2**20),
        cost_estimate=pl.CostEstimate(flops=flops, bytes_accessed=moved, transcendentals=0),
    )(*operands)


def weights_kernel(far, owner, wq, wk, wv, *outs):
    depth = wq.shape[0]
    for step, out in enumerate(outs):
        start = pl.multiple_of(far[step] * HEAD_SIZE, HEAD_SIZE)
        width = out.shape[1] - 2 * HEAD_SIZE
        out[:depth, :HEAD_SIZE] = wk[:, pl.ds(start, HEAD_SIZE)]
        out[:depth, HEAD_SIZE : 2 * HEAD_SIZE] = wv[:, pl.ds(start, HEAD_SIZE)]
        start = pl.multiple_of(far[step] * width, width)
        out[:depth, 2 * HEAD_SIZE :] = wq[:, pl.ds(start, width)]
        below = out.shape[0] - depth
        if below:
            row = owner[...].astype(jnp.float32).astype(jnp.bfloat16)
            out[depth:, :] = jnp.zeros((below, out.shape[1]), jnp.bfloat16)
            out[depth:, : row.shape[1]] = jnp.broadcast_to(row, (below, row.shape[1]))


def join_kernel(depth, blocks, *refs):
    weights, owners, out = refs[:blocks], refs[blocks:-1], refs[-1]
    tile = out.shape[0] - depth * blocks
    count = LANES
    for step, block in enumerate(weights):
        out[step * depth : (step + 1) * depth, :] = block[:depth, :]
    row = lax.broadcasted_iota(jnp.int32, (tile, count), 0)
    together = jnp.zeros((tile, count), jnp.float32)
    for at, ref in enumerate(owners):
        if ref.shape[0] == 1:
            value = jnp.broadcast_to(ref[...].astype(jnp.float32), (tile, count))
        else:
            value = ref[depth:, :count].astype(jnp.float32)
        together = jnp.where(row == at, value, together)
    out[depth * blocks :, :] = jnp.zeros((tile, out.shape[1]), out.dtype)
    out[depth * blocks :, :count] = together.astype(out.dtype)


def split_kernel(value, left, right):
    left[...] = value[:, : left.shape[1]]
    right[...] = value[:, left.shape[1] :]


def places_kernel(cap, mine, order, came, mate, twist, doc_starts, freqs, *refs):
    outs, scratch = refs[-11:-6], refs[-6:]
    angles, key_hot, query_bar, slots, columns = outs
    coded, starts, local, owners, landed, semaphore = scratch
    shards, rows = owners.shape
    sources = refs[:-11]
    tile = landed.shape[1]
    copies = []
    for at, source in enumerate(sources):
        bottom = source.at[source.shape[0] - tile :, :rows]
        copies.append(pltpu.make_async_copy(bottom, landed.at[at], semaphore.at[at]))
        copies[-1].start()
    for copy in copies:
        copy.wait()
    each = shards // len(sources)
    for source in range(shards):
        value = landed[source // each].astype(jnp.float32).astype(jnp.int32)
        owners[pl.ds(came[source], 1), :] = value[source % each : source % each + 1, :]
    groups = mine.shape[0]
    team = shards // groups
    span = groups * cap
    owner_at = lax.broadcasted_iota(jnp.int32, (shards, rows), 0)
    upper = jnp.where(
        lax.broadcasted_iota(jnp.int32, (rows, rows), 0)
        < lax.broadcasted_iota(jnp.int32, (rows, rows), 1),
        1.0,
        0.0,
    ).astype(jnp.bfloat16)
    rank_at = lax.broadcasted_iota(jnp.int32, (rows, rows), 0).astype(jnp.float32)
    lane = lax.broadcasted_iota(jnp.int32, (1, rows), 1).astype(jnp.float32)
    before = jnp.zeros((shards, 1), jnp.float32)
    found = jnp.zeros((3 * shards, rows), jnp.float32)
    for shard in range(shards):
        hot = jnp.where(owners[shard : shard + 1, :] == owner_at, 1.0, 0.0)
        within = dot(hot.astype(jnp.bfloat16), upper)
        local[shard : shard + 1, :] = jnp.sum(hot * within, axis=0, keepdims=True)
        rank = jnp.sum(hot * (within + before), axis=0, keepdims=True)
        before = before + jnp.sum(hot, axis=1, keepdims=True)
        rank_hot = jnp.where(rank_at == rank, 1.0, 0.0).astype(jnp.bfloat16)
        codes = jnp.concatenate([hot * float(shard), hot * lane, hot * within], axis=0)
        found = found + dot_rows(codes.astype(jnp.bfloat16), rank_hot)
    shard_of = found[:shards]
    place = shard_of * rows + found[shards : 2 * shards]
    docs = doc_starts.shape[0]
    doc_lane = lax.broadcasted_iota(jnp.int32, (1, LANES), 1)
    doc_row = jnp.full((1, LANES), -1.0, jnp.float32)
    start = jnp.zeros_like(place)
    for doc in range(docs):
        value = doc_starts[doc].astype(jnp.float32)
        start = jnp.maximum(start, jnp.where(value <= place, value, 0.0))
        doc_row = jnp.where(doc_lane == doc, value, doc_row)
    to_shard = shard_of.astype(jnp.int32)
    to_group = jnp.zeros_like(to_shard)
    for group in range(1, groups):
        to_group = jnp.where(to_shard >= group * team, group, to_group)
    to_mate = (to_shard - to_group * team) ^ twist[0]
    inside = found[2 * shards :].astype(jnp.int32)
    coded[...] = (to_mate * groups + to_group) * span + inside
    starts[:shards, :] = start
    starts[shards : 2 * shards, :] = place - start
    flat = jnp.transpose(starts[...])
    which = lax.broadcasted_iota(jnp.int32, flat.shape, 1)
    column = lax.broadcasted_iota(jnp.int32, (rows, 1), 0)
    for group in range(groups):
        own = slice(group * rows, (group + 1) * rows)
        at = mine[group]
        offset = jnp.sum(jnp.where(which == at + shards, flat, 0.0), axis=1, keepdims=True)
        angles[own, :] = offset * freqs[...]
        slots[:, own] = coded[pl.ds(at, 1), :] + group * cap
        shard = group * team + mate[0]
        place = column + shard * rows
        begin = jnp.zeros_like(column)
        for doc in range(docs):
            begin = jnp.where(doc_starts[doc] <= place, doc_starts[doc], begin)
        query_bar[own, :] = jnp.where(begin.astype(jnp.float32) == doc_row, 0.0, OTHER).astype(
            jnp.bfloat16
        )
        owner = owners[pl.ds(shard, 1), :]
        owner_group = jnp.zeros_like(owner)
        for step in range(1, groups):
            owner_group = jnp.where(owner >= step * team, step, owner_group)
        owner_mate = (owner - owner_group * team) ^ twist[0]
        rank = local[pl.ds(shard, 1), :].astype(jnp.int32)
        columns[group : group + 1, :] = owner_mate * span + owner_group * cap + rank
    for block in range(shards):
        own = slice(block * rows, (block + 1) * rows)
        begin = jnp.sum(jnp.where(which == order[block], flat, 0.0), axis=1, keepdims=True)
        key_hot[own, :] = jnp.where(begin == doc_row, 1.0, 0.0).astype(jnp.bfloat16)


def rotate(raw, cosine, sine):
    return raw * cosine + pltpu.roll(raw, HEAD_SIZE // 2, 1) * sine


def project(tokens, weights, cols=slice(None)):
    total = None
    start = 0
    for weight in weights:
        depth = weight.shape[0] // LANES * LANES
        part = dot(tokens[:, start : start + depth], weight[:depth, cols])
        total = part if total is None else total + part
        start += depth
    return total


def tokens_kernel(layout, places, table, *refs):
    row_blocks, col_chunks, blocks = layout
    count = row_blocks * col_chunks
    pieces, weights = refs[:count], refs[count:-4]
    total, later, tokens, loose = refs[-4:]
    rows, width = pieces[0].shape
    for row in range(row_blocks):
        there = pl.ds(pl.multiple_of(places[row] * rows, rows), rows)
        for col in range(col_chunks):
            loose[there, col * width : (col + 1) * width] = pieces[row * col_chunks + col][...]
    width = loose.shape[1] // blocks
    for block in range(blocks):
        source = pl.ds(pl.multiple_of(table[block] * width, width), width)
        tokens[:, block * width : (block + 1) * width] = loose[:, source]
    if later.shape[1] < tokens.shape[1]:
        later[...] = tokens[:, tokens.shape[1] - later.shape[1] :]
    for start in range(0, total.shape[1], 2 * HEAD_SIZE):
        cols = slice(start, start + 2 * HEAD_SIZE)
        total[:, cols] = project(tokens, weights, cols)


def finish_projection(total, later, weights, cols, skip=0):
    if not weights:
        return total[:, cols]
    return total[:, cols] + project(later, weights, slice(cols.start - skip, cols.stop - skip))


def kv_kernel(total, later, *refs):
    weights = refs[:-3]
    cosine, sine, kv = refs[-3:]
    raw = finish_projection(total, later, weights, slice(0, 2 * HEAD_SIZE))
    kv[:, :HEAD_SIZE] = rotate(raw[:, :HEAD_SIZE], cosine[...], sine[...]).astype(kv.dtype)
    kv[:, HEAD_SIZE:] = raw[:, HEAD_SIZE:].astype(kv.dtype)


def query_kernel(layout, total, later, *refs):
    parts, start = layout
    weights = refs[:parts]
    cosine, sine, slots = refs[parts : parts + 3]
    outs, queries = refs[parts + 3 : -1], refs[-1]
    cols = slice(start, start + queries.shape[1])
    raw = finish_projection(total, later, weights, cols, 2 * HEAD_SIZE)
    for head in range(queries.shape[1] // HEAD_SIZE):
        cols = slice(head * HEAD_SIZE, (head + 1) * HEAD_SIZE)
        queries[:, cols] = rotate(raw[:, cols], cosine[...], sine[...]).astype(queries.dtype)
    count = outs[0].shape[0]
    at = lax.broadcasted_iota(jnp.int32, (count, queries.shape[0]), 0)
    for step, out in enumerate(outs):
        hot = jnp.where(at + step * count == slots[...], 1.0, 0.0).astype(jnp.bfloat16)
        out[...] = dot(hot, queries[...]).astype(out.dtype)


def attention_kernel(layout, far, columns, query_bar, key_hot, *refs):
    query_parts, kv_parts, block_rows = layout
    arrived = refs[:query_parts]
    kvs = refs[query_parts : query_parts + kv_parts]
    outs = refs[query_parts + kv_parts : -5]
    keys, values, long, scores, context = refs[-5:]
    groups, rows = columns.shape
    heads = arrived[0].shape[1] // HEAD_SIZE
    start = 0
    for kv in kvs:
        own = slice(start, start + kv.shape[0])
        keys[own, :HEAD_SIZE] = kv[:, :HEAD_SIZE]
        values[own, :] = kv[:, HEAD_SIZE:]
        start += kv.shape[0]
    keys[:, HEAD_SIZE:] = key_hot[...]
    span = arrived[0].shape[0] // groups
    at = lax.broadcasted_iota(jnp.int32, (span * query_parts, rows), 0)
    for group in range(groups):
        hot = jnp.where(at == columns[group : group + 1, :], 1.0, 0.0).astype(jnp.bfloat16)
        there = slice(group * span, (group + 1) * span)
        slab = jnp.concatenate([part[there, :] for part in arrived], axis=0)
        picked = lax.dot_general(
            hot, slab, (((0,), (0,)), ((), ())), preferred_element_type=jnp.float32
        ).astype(jnp.bfloat16)
        own = slice(group * rows, (group + 1) * rows)
        for head in range(heads):
            long[head, own, :HEAD_SIZE] = picked[:, head * HEAD_SIZE : (head + 1) * HEAD_SIZE]
            long[head, own, HEAD_SIZE:] = query_bar[own, :]
    factor = 1.4426950408889634 / HEAD_SIZE**0.5
    blocks = groups * rows // block_rows
    steps = [(block, head) for block in range(blocks) for head in range(heads)]

    def score(step):
        block, head = steps[step]
        own = slice(block * block_rows, (block + 1) * block_rows)
        scores[step % 2] = dot_rows(long[head, own, :], keys[...])

    score(0)
    for step, (block, head) in enumerate(steps):
        if step + 1 < len(steps):
            score(step + 1)
        own = slice(block * block_rows, (block + 1) * block_rows)
        held = scores[step % 2]
        top = jnp.max(held, axis=1, keepdims=True)
        kept = jnp.exp2((held - top) * factor)
        total = jnp.sum(kept, axis=1, keepdims=True)
        mixed = dot(kept.astype(jnp.bfloat16), values[...])
        context[own, head * HEAD_SIZE : (head + 1) * HEAD_SIZE] = (mixed / total).astype(
            context.dtype
        )
    for step, out in enumerate(outs):
        out[...] = context[pl.ds(pl.multiple_of(far[step] * rows, rows), rows), :]


def finish_kernel(far, *refs):
    out = refs[-1]
    groups = far.shape[0]
    parts = (len(refs) - 1) // groups
    width = refs[0].shape[1]
    for part in range(parts):
        for step in range(groups):
            start = pl.multiple_of((far[step] * parts + part) * width, width)
            out[:, pl.ds(start, width)] = refs[part * groups + step][...]


def turn(value, axis, bits):
    count = lax.axis_size(axis)
    return lax.ppermute(value, axis, [(i, i ^ bits) for i in range(count)])


def after(value, *others):
    return lax.optimization_barrier((value, *others))[0]


def spread(value, *others):
    across = turn(value, "team", 2)
    last = turn(after(across, *others), "team", 1)
    return [value, across, turn(after(value, across), "team", 1), last]


def body(stored, source_owner, doc_ids, doc_starts, wq, wk, wv):
    groups, team = lax.axis_size("line"), lax.axis_size("team")
    nctx, ntp = groups * team, lax.axis_size("tp")
    group, mate = lax.axis_index("line"), lax.axis_index("team")
    rows = stored.shape[0]
    cap = 2 * rows // nctx
    size = HEAD_SIZE
    depth = wq.shape[0]
    split = groups > 1
    pair = 2 * size
    parts = wq.shape[1] // groups // pair
    total_rows = groups * rows
    width = stored.shape[1] * ntp
    keys = nctx * rows
    far = group ^ jnp.arange(groups, dtype=jnp.int32)

    def flip(value):
        return lax.ppermute(value, "tp", [(0, 1), (1, 0)])

    columns_each = (1 + parts) * pair
    tile = 16
    slabs = call(
        weights_kernel,
        [
            jax.ShapeDtypeStruct((depth + tile * (step % 2), columns_each), jnp.bfloat16)
            for step in range(groups)
        ],
        [far, source_owner[None, :], wq, wk, wv],
        smem=(0,),
    )

    if split:
        inner, outer = [(1, 2), (2, 1)], [(1, 0), (2, 3)]
        near = turn(stored, "line", 1)
        over = lax.ppermute(stored, "line", inner)
        flips = [flip(stored)]
        weights_near = turn(slabs[1], "line", 1)
        weights_third = turn(slabs[3], "line", 3)
        over_near = lax.ppermute(after(near, over, flips[0], *slabs), "line", inner)
        end = lax.ppermute(after(over, near, weights_near), "line", outer)
        flips.append(flip(after(near, flips[0], weights_third)))
        second_owner = turn(after(source_owner, weights_near), "line", 2)[None, :]
        held = call(
            functools.partial(join_kernel, depth, 2),
            jax.ShapeDtypeStruct((2 * depth + tile, columns_each), jnp.bfloat16),
            [slabs[0], weights_near, source_owner[None, :]]
            + [weights_near, weights_third, second_owner],
        )
        first = spread(held)
        edge = (group == 0) | (group == groups - 1)
        third = jnp.where(edge, end, over)
        end_near = lax.ppermute(after(over_near, flips[1]), "line", outer)
        flips.append(flip(after(third, flips[1])))
        weights_second = turn(after(slabs[2], over_near, end, first[1]), "line", 2)
        fourth = jnp.where(edge, end_near, over_near)
        flips.append(flip(after(fourth, flips[2])))
        second = spread(after(weights_third, flips[2], first[1]))
        early = [part for both in zip(first, second) for part in both]
        places = jnp.stack(
            [group, group ^ 1, group ^ jnp.where(edge, 2, 3), group ^ jnp.where(edge, 3, 2)]
        )
        pieces = [
            chunk for both in zip((stored, near, third, fourth), flips) for chunk in both
        ]
        chunks = ntp
        owners = first
    else:
        pieces = [lax.all_gather(stored, "tp", axis=1, tiled=True)]
        places = jnp.zeros((1,), jnp.int32)
        chunks = 1
        early = [lax.all_gather(slabs[0], "team", axis=0, tiled=True)]
        owners = [lax.all_gather(source_owner, "team", axis=0)]

    if split:
        rel = jnp.arange(groups, dtype=jnp.int32)
        turns = mate ^ jnp.array([0, 2, 1, 3], dtype=jnp.int32)
        order = (rel[None, :] * team + turns[:, None]).reshape(-1)
        came = (far[jnp.array([0, 1, 3, 2])][None, :] * team + turns[:, None]).reshape(-1)
        rows_of = jnp.concatenate(
            [came.reshape(team, groups)[:, :3].reshape(-1), came.reshape(team, groups)[:, 3]]
        )
        mine = rel * team + mate
        twist = mate[None]
        share = nctx // ntp
        table = rows_of % share + jnp.where(rows_of // share == lax.axis_index("tp"), 0, share)
    else:
        order = came = jnp.arange(nctx, dtype=jnp.int32)
        mine = mate[None]
        twist = table = jnp.zeros((1,), jnp.int32)

    freqs = ROPE_BASE ** (-np.arange(size // 2) * 2.0 / size)
    freqs = jnp.asarray(np.concatenate([freqs, freqs])[None, :], jnp.float32)
    sign = jnp.asarray(np.repeat([-1.0, 1.0], size // 2)[None, :], jnp.float32)
    angles, key_hot, query_bar, slots, columns = call(
        functools.partial(places_kernel, cap),
        [
            jax.ShapeDtypeStruct((total_rows, size), jnp.float32),
            jax.ShapeDtypeStruct((keys, LANES), jnp.bfloat16),
            jax.ShapeDtypeStruct((total_rows, LANES), jnp.bfloat16),
            jax.ShapeDtypeStruct((1, total_rows), jnp.int32),
            jax.ShapeDtypeStruct((groups, rows), jnp.int32),
        ],
        [mine, order, came, mate[None], twist, doc_starts, freqs, *owners],
        scratch=[
            pltpu.VMEM((nctx, rows), jnp.int32),
            pltpu.VMEM((max(2 * nctx, LANES), rows), jnp.float32),
            pltpu.VMEM((nctx, rows), jnp.float32),
            pltpu.VMEM((nctx, rows), jnp.int32),
            pltpu.VMEM((len(owners), tile if split else nctx, rows), owners[0].dtype),
            pltpu.SemaphoreType.DMA((len(owners),)),
        ],
        flops=10**9,
        smem=(0, 1, 2, 3, 4, 5),
        anywhere=range(7, 7 + len(owners)),
    )
    cosine = jnp.cos(angles)
    sine = jnp.sin(angles) * sign

    rest = width // groups if split else width
    total, later = call(
        functools.partial(tokens_kernel, (groups, chunks, nctx if split else 1)),
        [
            jax.ShapeDtypeStruct((total_rows, columns_each), jnp.float32),
            jax.ShapeDtypeStruct((total_rows, rest if split else LANES), jnp.bfloat16),
        ],
        [places, table, *pieces, *early],
        scratch=[
            pltpu.VMEM((total_rows, width), jnp.bfloat16),
            pltpu.VMEM((total_rows, width), jnp.bfloat16),
        ],
        flops=2 * total_rows * width * columns_each,
        smem=(0, 1),
        vmem=32,
    )
    if split:
        kv_second, query_second = call(
            split_kernel,
            [
                jax.ShapeDtypeStruct((depth, pair), jnp.bfloat16),
                jax.ShapeDtypeStruct((depth, parts * pair), jnp.bfloat16),
            ],
            [weights_second],
            flops=6 * 10**9,
        )
        kv_second = after(kv_second, flips[3], second[1])
    kv_late = spread(kv_second, total, cosine) if split else []
    kv = call(
        kv_kernel,
        jax.ShapeDtypeStruct((total_rows, pair), jnp.bfloat16),
        [total, later, *kv_late, cosine, sine],
        flops=2 * total_rows * rest * pair,
    )
    late = spread(query_second, kv) if split else []

    block_rows = min(2 * rows, total_rows)
    lanes_out = team if split else 1
    slot_count = nctx * groups * cap

    def project_part(part):
        return call(
            functools.partial(query_kernel, (len(late), (1 + part) * pair)),
            [jax.ShapeDtypeStruct((slot_count // lanes_out, pair), jnp.bfloat16)] * lanes_out,
            [total, later, *late, cosine, sine, slots],
            scratch=[pltpu.VMEM((total_rows, pair), jnp.bfloat16)],
            flops=2 * total_rows * (rest + slot_count) * pair,
        )

    def attend(arrived):
        context = call(
            functools.partial(attention_kernel, (len(arrived), len(kvs), block_rows)),
            [jax.ShapeDtypeStruct((rows, pair), jnp.bfloat16)] * groups,
            [far, columns, query_bar, key_hot, *arrived, *kvs],
            scratch=[
                pltpu.VMEM((keys, size + LANES), jnp.bfloat16),
                pltpu.VMEM((keys, size), jnp.bfloat16),
                pltpu.VMEM((pair // size, total_rows, size + LANES), jnp.bfloat16),
                pltpu.VMEM((2, block_rows, keys), jnp.float32),
                pltpu.VMEM((total_rows, pair), jnp.bfloat16),
            ],
            flops=8 * total_rows * pair * keys,
            smem=(0,),
            vmem=40,
        )
        return [context[0]] + [turn(context[step], "line", step) for step in range(1, groups)]

    def exchange(leaving):
        if split:
            return [leaving[0]] + [turn(leaving[e], "team", e) for e in range(1, team)]
        return [lax.all_to_all(leaving[0], "team", 0, 0, tiled=True)]

    leaving = [project_part(part) for part in range(parts)]
    arrived = [exchange(part) for part in leaving]
    if split:
        across = turn(kv, "team", 2)
        kvs = [kv, across] + [
            turn(after(part, arrived[0][1], leaving[-1][0]), "team", 1) for part in (kv, across)
        ]
    else:
        kvs = [lax.all_gather(kv, "team", axis=0, tiled=True)]
    ready = [piece for queries in arrived for piece in attend(queries)]

    return call(
        finish_kernel,
        jax.ShapeDtypeStruct((rows, wq.shape[1]), jnp.bfloat16),
        [far, *ready],
        smem=(0,),
    )


def solution(mesh):
    def program(stored, source_owner, doc_ids, doc_starts, wq, wk, wv):
        ctx, tp = mesh.shape["ctx"], mesh.shape["tp"]
        groups = wk.shape[1] // HEAD_SIZE // tp
        parts = jax.sharding.Mesh(
            mesh.devices.reshape(groups, ctx // groups, tp), ("line", "team", "tp")
        )
        both = ("line", "team")
        return jax.shard_map(
            body,
            mesh=parts,
            in_specs=(
                P(both, "tp"),
                P(both),
                P(both),
                P(),
                P(both, "tp"),
                P(both, "tp"),
                P(both, "tp"),
            ),
            out_specs=P(both, "tp"),
            check_vma=False,
        )(stored, source_owner, doc_ids, doc_starts, wq, wk, wv)

    return program
```

```python
import functools

import jax
import jax.numpy as jnp
import numpy as np
from jax import lax
from jax.experimental import pallas as pl
from jax.experimental.pallas import tpu as pltpu
from jax.sharding import PartitionSpec as P

HEAD_SIZE = 128
LANES = 128
ROPE_BASE = 500000.0
OTHER = -(2.0**100)

VMEM_SPEC = pl.BlockSpec(memory_space=pltpu.VMEM)
SMEM_SPEC = pl.BlockSpec(memory_space=pltpu.SMEM)
ANY_SPEC = pl.BlockSpec(memory_space=pl.ANY)


def dot(a, b):
    return jnp.dot(a, b, preferred_element_type=jnp.float32)


def dot_rows(a, b):
    return lax.dot_general(
        a, b, (((1,), (1,)), ((), ())), preferred_element_type=jnp.float32
    )


def call(kernel, out_shape, operands, scratch=(), flops=0, smem=(), anywhere=(), vmem=24):
    specs = [
        SMEM_SPEC if at in smem else ANY_SPEC if at in anywhere else VMEM_SPEC
        for at in range(len(operands))
    ]
    many = isinstance(out_shape, (list, tuple))
    outs = out_shape if many else [out_shape]
    moved = sum(x.size * x.dtype.itemsize for x in [*operands, *outs])
    return pl.pallas_call(
        kernel,
        out_shape=out_shape,
        in_specs=specs,
        out_specs=[VMEM_SPEC] * len(out_shape) if many else VMEM_SPEC,
        scratch_shapes=list(scratch),
        compiler_params=pltpu.CompilerParams(vmem_limit_bytes=vmem * 2**20),
        cost_estimate=pl.CostEstimate(flops=flops, bytes_accessed=moved, transcendentals=0),
    )(*operands)


def weights_kernel(far, owner, wq, wk, wv, *outs):
    depth = wq.shape[0]
    for step, out in enumerate(outs):
        start = pl.multiple_of(far[step] * HEAD_SIZE, HEAD_SIZE)
        width = out.shape[1] - 2 * HEAD_SIZE
        out[:depth, :HEAD_SIZE] = wk[:, pl.ds(start, HEAD_SIZE)]
        out[:depth, HEAD_SIZE : 2 * HEAD_SIZE] = wv[:, pl.ds(start, HEAD_SIZE)]
        start = pl.multiple_of(far[step] * width, width)
        out[:depth, 2 * HEAD_SIZE :] = wq[:, pl.ds(start, width)]
        below = out.shape[0] - depth
        if below:
            row = owner[...].astype(jnp.float32).astype(jnp.bfloat16)
            out[depth:, :] = jnp.zeros((below, out.shape[1]), jnp.bfloat16)
            out[depth:, : row.shape[1]] = jnp.broadcast_to(row, (below, row.shape[1]))


def join_kernel(depth, first, *refs):
    blocks, second, out = refs[:-2], refs[-2], refs[-1]
    tile = out.shape[0] - depth * len(blocks)
    count = LANES
    for step, block in enumerate(blocks):
        out[step * depth : (step + 1) * depth, :] = block[:depth, :]
    row = lax.broadcasted_iota(jnp.int32, (tile, count), 0)

    def spread_row(ref):
        if ref.shape[0] == 1:
            return jnp.broadcast_to(ref[...].astype(jnp.float32), (tile, count))
        return ref[depth:, :count].astype(jnp.float32)

    both = jnp.where(row == 0, spread_row(first), spread_row(second)).astype(out.dtype)
    out[depth * len(blocks) :, :] = jnp.zeros((tile, out.shape[1]), out.dtype)
    out[depth * len(blocks) :, :count] = both


def split_kernel(value, left, right):
    left[...] = value[:, : left.shape[1]]
    right[...] = value[:, left.shape[1] :]


def places_kernel(cap, mine, order, came, mate, twist, doc_starts, freqs, *refs):
    outs, scratch = refs[-11:-6], refs[-6:]
    angles, key_hot, query_bar, slots, columns = outs
    coded, starts, local, owners, landed, semaphore = scratch
    shards, rows = owners.shape
    sources = refs[:-11]
    tile = landed.shape[1]
    copies = []
    for at, source in enumerate(sources):
        bottom = source.at[source.shape[0] - tile :, :rows]
        copies.append(pltpu.make_async_copy(bottom, landed.at[at], semaphore.at[at]))
        copies[-1].start()
    for copy in copies:
        copy.wait()
    each = shards // len(sources)
    for source in range(shards):
        value = landed[source // each].astype(jnp.float32).astype(jnp.int32)
        owners[pl.ds(came[source], 1), :] = value[source % each : source % each + 1, :]
    groups = mine.shape[0]
    team = shards // groups
    span = groups * cap
    owner_at = lax.broadcasted_iota(jnp.int32, (shards, rows), 0)
    upper = jnp.where(
        lax.broadcasted_iota(jnp.int32, (rows, rows), 0)
        < lax.broadcasted_iota(jnp.int32, (rows, rows), 1),
        1.0,
        0.0,
    ).astype(jnp.bfloat16)
    rank_at = lax.broadcasted_iota(jnp.int32, (rows, rows), 0).astype(jnp.float32)
    lane = lax.broadcasted_iota(jnp.int32, (1, rows), 1).astype(jnp.float32)
    before = jnp.zeros((shards, 1), jnp.float32)
    found = jnp.zeros((3 * shards, rows), jnp.float32)
    for shard in range(shards):
        hot = jnp.where(owners[shard : shard + 1, :] == owner_at, 1.0, 0.0)
        within = dot(hot.astype(jnp.bfloat16), upper)
        local[shard : shard + 1, :] = jnp.sum(hot * within, axis=0, keepdims=True)
        rank = jnp.sum(hot * (within + before), axis=0, keepdims=True)
        before = before + jnp.sum(hot, axis=1, keepdims=True)
        rank_hot = jnp.where(rank_at == rank, 1.0, 0.0).astype(jnp.bfloat16)
        codes = jnp.concatenate([hot * float(shard), hot * lane, hot * within], axis=0)
        found = found + dot_rows(codes.astype(jnp.bfloat16), rank_hot)
    shard_of = found[:shards]
    place = shard_of * rows + found[shards : 2 * shards]
    docs = doc_starts.shape[0]
    doc_lane = lax.broadcasted_iota(jnp.int32, (1, LANES), 1)
    doc_row = jnp.full((1, LANES), -1.0, jnp.float32)
    start = jnp.zeros_like(place)
    for doc in range(docs):
        value = doc_starts[doc].astype(jnp.float32)
        start = jnp.maximum(start, jnp.where(value <= place, value, 0.0))
        doc_row = jnp.where(doc_lane == doc, value, doc_row)
    to_shard = shard_of.astype(jnp.int32)
    to_group = jnp.zeros_like(to_shard)
    for group in range(1, groups):
        to_group = jnp.where(to_shard >= group * team, group, to_group)
    to_mate = (to_shard - to_group * team) ^ twist[0]
    inside = found[2 * shards :].astype(jnp.int32)
    coded[...] = (to_mate * groups + to_group) * span + inside
    starts[:shards, :] = start
    starts[shards : 2 * shards, :] = place - start
    flat = jnp.transpose(starts[...])
    which = lax.broadcasted_iota(jnp.int32, flat.shape, 1)
    column = lax.broadcasted_iota(jnp.int32, (rows, 1), 0)
    for group in range(groups):
        own = slice(group * rows, (group + 1) * rows)
        at = mine[group]
        offset = jnp.sum(jnp.where(which == at + shards, flat, 0.0), axis=1, keepdims=True)
        angles[own, :] = offset * freqs[...]
        slots[:, own] = coded[pl.ds(at, 1), :] + group * cap
        shard = group * team + mate[0]
        place = column + shard * rows
        begin = jnp.zeros_like(column)
        for doc in range(docs):
            begin = jnp.where(doc_starts[doc] <= place, doc_starts[doc], begin)
        query_bar[own, :] = jnp.where(begin.astype(jnp.float32) == doc_row, 0.0, OTHER).astype(
            jnp.bfloat16
        )
        owner = owners[pl.ds(shard, 1), :]
        owner_group = jnp.zeros_like(owner)
        for step in range(1, groups):
            owner_group = jnp.where(owner >= step * team, step, owner_group)
        owner_mate = (owner - owner_group * team) ^ twist[0]
        rank = local[pl.ds(shard, 1), :].astype(jnp.int32)
        columns[group : group + 1, :] = owner_mate * span + owner_group * cap + rank
    for block in range(shards):
        own = slice(block * rows, (block + 1) * rows)
        begin = jnp.sum(jnp.where(which == order[block], flat, 0.0), axis=1, keepdims=True)
        key_hot[own, :] = jnp.where(begin == doc_row, 1.0, 0.0).astype(jnp.bfloat16)


def rotate(raw, cosine, sine):
    return raw * cosine + pltpu.roll(raw, HEAD_SIZE // 2, 1) * sine


def project(tokens, weights, cols=slice(None)):
    total = None
    start = 0
    for weight in weights:
        depth = weight.shape[0] // LANES * LANES
        part = dot(tokens[:, start : start + depth], weight[:depth, cols])
        total = part if total is None else total + part
        start += depth
    return total


def tokens_kernel(layout, places, table, *refs):
    row_blocks, col_chunks, blocks = layout
    count = row_blocks * col_chunks
    pieces, weights = refs[:count], refs[count:-4]
    total, later, tokens, loose = refs[-4:]
    rows, width = pieces[0].shape
    for row in range(row_blocks):
        there = pl.ds(pl.multiple_of(places[row] * rows, rows), rows)
        for col in range(col_chunks):
            loose[there, col * width : (col + 1) * width] = pieces[row * col_chunks + col][...]
    width = loose.shape[1] // blocks
    for block in range(blocks):
        source = pl.ds(pl.multiple_of(table[block] * width, width), width)
        tokens[:, block * width : (block + 1) * width] = loose[:, source]
    if later.shape[1] < tokens.shape[1]:
        later[...] = tokens[:, tokens.shape[1] - later.shape[1] :]
    for start in range(0, total.shape[1], 2 * HEAD_SIZE):
        cols = slice(start, start + 2 * HEAD_SIZE)
        total[:, cols] = project(tokens, weights, cols)


def finish_projection(total, later, weights, cols, skip=0):
    if not weights:
        return total[:, cols]
    return total[:, cols] + project(later, weights, slice(cols.start - skip, cols.stop - skip))


def kv_kernel(total, later, *refs):
    weights = refs[:-3]
    cosine, sine, kv = refs[-3:]
    raw = finish_projection(total, later, weights, slice(0, 2 * HEAD_SIZE))
    kv[:, :HEAD_SIZE] = rotate(raw[:, :HEAD_SIZE], cosine[...], sine[...]).astype(kv.dtype)
    kv[:, HEAD_SIZE:] = raw[:, HEAD_SIZE:].astype(kv.dtype)


def query_kernel(layout, total, later, *refs):
    parts, start = layout
    weights = refs[:parts]
    cosine, sine, slots = refs[parts : parts + 3]
    outs, queries = refs[parts + 3 : -1], refs[-1]
    cols = slice(start, start + queries.shape[1])
    raw = finish_projection(total, later, weights, cols, 2 * HEAD_SIZE)
    for head in range(queries.shape[1] // HEAD_SIZE):
        cols = slice(head * HEAD_SIZE, (head + 1) * HEAD_SIZE)
        queries[:, cols] = rotate(raw[:, cols], cosine[...], sine[...]).astype(queries.dtype)
    count = outs[0].shape[0]
    at = lax.broadcasted_iota(jnp.int32, (count, queries.shape[0]), 0)
    for step, out in enumerate(outs):
        hot = jnp.where(at + step * count == slots[...], 1.0, 0.0).astype(jnp.bfloat16)
        out[...] = dot(hot, queries[...]).astype(out.dtype)


def attention_kernel(layout, far, columns, query_bar, key_hot, *refs):
    query_parts, kv_parts, block_rows = layout
    arrived = refs[:query_parts]
    kvs = refs[query_parts : query_parts + kv_parts]
    outs = refs[query_parts + kv_parts : -5]
    keys, values, long, scores, context = refs[-5:]
    groups, rows = columns.shape
    heads = arrived[0].shape[1] // HEAD_SIZE
    start = 0
    for kv in kvs:
        own = slice(start, start + kv.shape[0])
        keys[own, :HEAD_SIZE] = kv[:, :HEAD_SIZE]
        values[own, :] = kv[:, HEAD_SIZE:]
        start += kv.shape[0]
    keys[:, HEAD_SIZE:] = key_hot[...]
    span = arrived[0].shape[0] // groups
    at = lax.broadcasted_iota(jnp.int32, (span * query_parts, rows), 0)
    for group in range(groups):
        hot = jnp.where(at == columns[group : group + 1, :], 1.0, 0.0).astype(jnp.bfloat16)
        there = slice(group * span, (group + 1) * span)
        slab = jnp.concatenate([part[there, :] for part in arrived], axis=0)
        picked = lax.dot_general(
            hot, slab, (((0,), (0,)), ((), ())), preferred_element_type=jnp.float32
        ).astype(jnp.bfloat16)
        own = slice(group * rows, (group + 1) * rows)
        for head in range(heads):
            long[head, own, :HEAD_SIZE] = picked[:, head * HEAD_SIZE : (head + 1) * HEAD_SIZE]
            long[head, own, HEAD_SIZE:] = query_bar[own, :]
    factor = 1.4426950408889634 / HEAD_SIZE**0.5
    blocks = groups * rows // block_rows
    steps = [(block, head) for block in range(blocks) for head in range(heads)]

    def score(step):
        block, head = steps[step]
        own = slice(block * block_rows, (block + 1) * block_rows)
        scores[step % 2] = dot_rows(long[head, own, :], keys[...])

    score(0)
    for step, (block, head) in enumerate(steps):
        if step + 1 < len(steps):
            score(step + 1)
        own = slice(block * block_rows, (block + 1) * block_rows)
        held = scores[step % 2]
        top = jnp.max(held, axis=1, keepdims=True)
        kept = jnp.exp2((held - top) * factor)
        total = jnp.sum(kept, axis=1, keepdims=True)
        mixed = dot(kept.astype(jnp.bfloat16), values[...])
        context[own, head * HEAD_SIZE : (head + 1) * HEAD_SIZE] = (mixed / total).astype(
            context.dtype
        )
    for step, out in enumerate(outs):
        out[...] = context[pl.ds(pl.multiple_of(far[step] * rows, rows), rows), :]


def finish_kernel(far, *refs):
    out = refs[-1]
    groups = far.shape[0]
    parts = (len(refs) - 1) // groups
    width = refs[0].shape[1]
    for part in range(parts):
        for step in range(groups):
            start = pl.multiple_of((far[step] * parts + part) * width, width)
            out[:, pl.ds(start, width)] = refs[part * groups + step][...]


def turn(value, axis, bits):
    count = lax.axis_size(axis)
    return lax.ppermute(value, axis, [(i, i ^ bits) for i in range(count)])


def after(value, *others):
    return lax.optimization_barrier((value, *others))[0]


def spread(value, *others):
    across = turn(value, "team", 2)
    last = turn(after(across, *others), "team", 1)
    return [value, across, turn(value, "team", 1), last]


def body(stored, source_owner, doc_ids, doc_starts, wq, wk, wv):
    groups, team = lax.axis_size("line"), lax.axis_size("team")
    nctx, ntp = groups * team, lax.axis_size("tp")
    group, mate = lax.axis_index("line"), lax.axis_index("team")
    rows = stored.shape[0]
    cap = 2 * rows // nctx
    size = HEAD_SIZE
    depth = wq.shape[0]
    split = groups > 1
    pair = 2 * size
    parts = wq.shape[1] // groups // pair
    total_rows = groups * rows
    width = stored.shape[1] * ntp
    keys = nctx * rows
    far = group ^ jnp.arange(groups, dtype=jnp.int32)

    def flip(value):
        return lax.ppermute(value, "tp", [(0, 1), (1, 0)])

    columns_each = (1 + parts) * pair
    tile = 16
    slabs = call(
        weights_kernel,
        [
            jax.ShapeDtypeStruct((depth + tile * (step % 2), columns_each), jnp.bfloat16)
            for step in range(groups)
        ],
        [far, source_owner[None, :], wq, wk, wv],
        smem=(0,),
    )

    if split:
        def join(first, blocks, second):
            shape = (depth * len(blocks) + tile, columns_each)
            return call(
                functools.partial(join_kernel, depth),
                jax.ShapeDtypeStruct(shape, jnp.bfloat16),
                [first, *blocks, second],
            )

        inner, outer = [(1, 2), (2, 1)], [(1, 0), (2, 3)]
        near = turn(stored, "line", 1)
        over = lax.ppermute(stored, "line", inner)
        flips = [flip(stored)]
        weights_near = turn(slabs[1], "line", 1)
        weights_third = turn(slabs[3], "line", 3)
        over_near = lax.ppermute(after(near, over, flips[0], *slabs), "line", inner)
        end = lax.ppermute(after(over, near, weights_near), "line", outer)
        flips.append(flip(after(near, flips[0], weights_third)))
        held = join(source_owner[None, :], [slabs[0], weights_near], weights_near)
        second_owner = turn(after(source_owner, weights_near), "line", 2)[None, :]
        first = spread(held)
        edge = (group == 0) | (group == groups - 1)
        third = jnp.where(edge, end, over)
        end_near = lax.ppermute(after(over_near, flips[1]), "line", outer)
        flips.append(flip(after(third, flips[1], second_owner)))
        weights_second = turn(after(slabs[2], over_near, end, first[1]), "line", 2)
        fourth = jnp.where(edge, end_near, over_near)
        flips.append(flip(after(fourth, flips[2])))
        third_held = join(weights_third, [weights_third], second_owner)
        second = spread(after(third_held, flips[2], first[1]))
        kv_second, query_second = call(
            split_kernel,
            [
                jax.ShapeDtypeStruct((depth, pair), jnp.bfloat16),
                jax.ShapeDtypeStruct((depth, parts * pair), jnp.bfloat16),
            ],
            [after(weights_second, flips[3], second[1])],
        )
        early = [part for both in zip(first, second) for part in both]
        places = jnp.stack(
            [group, group ^ 1, group ^ jnp.where(edge, 2, 3), group ^ jnp.where(edge, 3, 2)]
        )
        pieces = [
            chunk for both in zip((stored, near, third, fourth), flips) for chunk in both
        ]
        chunks = ntp
        owners = early
    else:
        pieces = [lax.all_gather(stored, "tp", axis=1, tiled=True)]
        places = jnp.zeros((1,), jnp.int32)
        chunks = 1
        early = [lax.all_gather(slabs[0], "team", axis=0, tiled=True)]
        owners = [lax.all_gather(source_owner, "team", axis=0)]

    if split:
        rel = jnp.arange(groups, dtype=jnp.int32)
        turns = mate ^ jnp.array([0, 2, 1, 3], dtype=jnp.int32)
        order = (rel[None, :] * team + turns[:, None]).reshape(-1)
        came = (far[jnp.array([0, 1, 3, 2])][None, :] * team + turns[:, None]).reshape(-1)
        rows_of = jnp.concatenate(
            [came.reshape(team, groups)[:, :3].reshape(-1), came.reshape(team, groups)[:, 3]]
        )
        mine = rel * team + mate
        twist = mate[None]
        share = nctx // ntp
        table = rows_of % share + jnp.where(rows_of // share == lax.axis_index("tp"), 0, share)
    else:
        order = came = jnp.arange(nctx, dtype=jnp.int32)
        mine = mate[None]
        twist = table = jnp.zeros((1,), jnp.int32)

    freqs = ROPE_BASE ** (-np.arange(size // 2) * 2.0 / size)
    freqs = jnp.asarray(np.concatenate([freqs, freqs])[None, :], jnp.float32)
    sign = jnp.asarray(np.repeat([-1.0, 1.0], size // 2)[None, :], jnp.float32)
    angles, key_hot, query_bar, slots, columns = call(
        functools.partial(places_kernel, cap),
        [
            jax.ShapeDtypeStruct((total_rows, size), jnp.float32),
            jax.ShapeDtypeStruct((keys, LANES), jnp.bfloat16),
            jax.ShapeDtypeStruct((total_rows, LANES), jnp.bfloat16),
            jax.ShapeDtypeStruct((1, total_rows), jnp.int32),
            jax.ShapeDtypeStruct((groups, rows), jnp.int32),
        ],
        [mine, order, came, mate[None], twist, doc_starts, freqs, *owners],
        scratch=[
            pltpu.VMEM((nctx, rows), jnp.int32),
            pltpu.VMEM((max(2 * nctx, LANES), rows), jnp.float32),
            pltpu.VMEM((nctx, rows), jnp.float32),
            pltpu.VMEM((nctx, rows), jnp.int32),
            pltpu.VMEM((len(owners), tile if split else nctx, rows), owners[0].dtype),
            pltpu.SemaphoreType.DMA((len(owners),)),
        ],
        flops=10**9,
        smem=(0, 1, 2, 3, 4, 5),
        anywhere=range(7, 7 + len(owners)),
    )
    cosine = jnp.cos(angles)
    sine = jnp.sin(angles) * sign

    rest = width // groups if split else width
    total, later = call(
        functools.partial(tokens_kernel, (groups, chunks, nctx if split else 1)),
        [
            jax.ShapeDtypeStruct((total_rows, columns_each), jnp.float32),
            jax.ShapeDtypeStruct((total_rows, rest if split else LANES), jnp.bfloat16),
        ],
        [places, table, *pieces, *early],
        scratch=[
            pltpu.VMEM((total_rows, width), jnp.bfloat16),
            pltpu.VMEM((total_rows, width), jnp.bfloat16),
        ],
        flops=2 * total_rows * width * columns_each,
        smem=(0, 1),
        vmem=32,
    )
    kv_late = spread(kv_second, total, cosine) if split else []
    kv = call(
        kv_kernel,
        jax.ShapeDtypeStruct((total_rows, pair), jnp.bfloat16),
        [total, later, *kv_late, cosine, sine],
        flops=2 * total_rows * rest * pair,
    )
    late = spread(query_second, kv) if split else []

    block_rows = min(2 * rows, total_rows)
    lanes_out = team if split else 1
    slot_count = nctx * groups * cap

    def project_part(part):
        return call(
            functools.partial(query_kernel, (len(late), (1 + part) * pair)),
            [jax.ShapeDtypeStruct((slot_count // lanes_out, pair), jnp.bfloat16)] * lanes_out,
            [total, later, *late, cosine, sine, slots],
            scratch=[pltpu.VMEM((total_rows, pair), jnp.bfloat16)],
            flops=2 * total_rows * (rest + slot_count) * pair,
        )

    def attend(arrived):
        context = call(
            functools.partial(attention_kernel, (len(arrived), len(kvs), block_rows)),
            [jax.ShapeDtypeStruct((rows, pair), jnp.bfloat16)] * groups,
            [far, columns, query_bar, key_hot, *arrived, *kvs],
            scratch=[
                pltpu.VMEM((keys, size + LANES), jnp.bfloat16),
                pltpu.VMEM((keys, size), jnp.bfloat16),
                pltpu.VMEM((pair // size, total_rows, size + LANES), jnp.bfloat16),
                pltpu.VMEM((2, block_rows, keys), jnp.float32),
                pltpu.VMEM((total_rows, pair), jnp.bfloat16),
            ],
            flops=8 * total_rows * pair * keys,
            smem=(0,),
            vmem=40,
        )
        return [context[0]] + [turn(context[step], "line", step) for step in range(1, groups)]

    def exchange(leaving):
        if split:
            return [leaving[0]] + [turn(leaving[e], "team", e) for e in range(1, team)]
        return [lax.all_to_all(leaving[0], "team", 0, 0, tiled=True)]

    leaving = [project_part(part) for part in range(parts)]
    arrived = [exchange(part) for part in leaving]
    if split:
        across = turn(kv, "team", 2)
        kvs = [kv, across] + [
            turn(after(part, *arrived[-1], leaving[0][0]), "team", 1) for part in (kv, across)
        ]
    else:
        kvs = [lax.all_gather(kv, "team", axis=0, tiled=True)]
    ready = [piece for queries in arrived for piece in attend(queries)]

    return call(
        finish_kernel,
        jax.ShapeDtypeStruct((rows, wq.shape[1]), jnp.bfloat16),
        [far, *ready],
        smem=(0,),
    )


def solution(mesh):
    def program(stored, source_owner, doc_ids, doc_starts, wq, wk, wv):
        ctx, tp = mesh.shape["ctx"], mesh.shape["tp"]
        groups = wk.shape[1] // HEAD_SIZE // tp
        parts = jax.sharding.Mesh(
            mesh.devices.reshape(groups, ctx // groups, tp), ("line", "team", "tp")
        )
        both = ("line", "team")
        return jax.shard_map(
            body,
            mesh=parts,
            in_specs=(
                P(both, "tp"),
                P(both),
                P(both),
                P(),
                P(both, "tp"),
                P(both, "tp"),
                P(both, "tp"),
            ),
            out_specs=P(both, "tp"),
            check_vma=False,
        )(stored, source_owner, doc_ids, doc_starts, wq, wk, wv)

    return program
```

```python
import functools

import jax
import jax.numpy as jnp
import numpy as np
from jax import lax
from jax.experimental import pallas as pl
from jax.experimental.pallas import tpu as pltpu
from jax.sharding import PartitionSpec as P

HEAD_SIZE = 128
LANES = 128
ROPE_BASE = 500000.0
OTHER = -(2.0**100)

VMEM_SPEC = pl.BlockSpec(memory_space=pltpu.VMEM)
SMEM_SPEC = pl.BlockSpec(memory_space=pltpu.SMEM)
ANY_SPEC = pl.BlockSpec(memory_space=pl.ANY)


def dot(a, b):
    return jnp.dot(a, b, preferred_element_type=jnp.float32)


def dot_rows(a, b):
    return lax.dot_general(
        a, b, (((1,), (1,)), ((), ())), preferred_element_type=jnp.float32
    )


def call(kernel, out_shape, operands, scratch=(), flops=0, smem=(), anywhere=(), vmem=24):
    specs = [
        SMEM_SPEC if at in smem else ANY_SPEC if at in anywhere else VMEM_SPEC
        for at in range(len(operands))
    ]
    many = isinstance(out_shape, (list, tuple))
    outs = out_shape if many else [out_shape]
    moved = sum(x.size * x.dtype.itemsize for x in [*operands, *outs])
    return pl.pallas_call(
        kernel,
        out_shape=out_shape,
        in_specs=specs,
        out_specs=[VMEM_SPEC] * len(out_shape) if many else VMEM_SPEC,
        scratch_shapes=list(scratch),
        compiler_params=pltpu.CompilerParams(vmem_limit_bytes=vmem * 2**20),
        cost_estimate=pl.CostEstimate(flops=flops, bytes_accessed=moved, transcendentals=0),
    )(*operands)


def weights_kernel(far, owner, wq, wk, wv, *outs):
    depth = wq.shape[0]
    for step, out in enumerate(outs):
        start = pl.multiple_of(far[step] * HEAD_SIZE, HEAD_SIZE)
        width = out.shape[1] - 2 * HEAD_SIZE
        out[:depth, :HEAD_SIZE] = wk[:, pl.ds(start, HEAD_SIZE)]
        out[:depth, HEAD_SIZE : 2 * HEAD_SIZE] = wv[:, pl.ds(start, HEAD_SIZE)]
        start = pl.multiple_of(far[step] * width, width)
        out[:depth, 2 * HEAD_SIZE :] = wq[:, pl.ds(start, width)]
        below = out.shape[0] - depth
        if below:
            row = owner[...].astype(jnp.float32).astype(jnp.bfloat16)
            out[depth:, :] = jnp.zeros((below, out.shape[1]), jnp.bfloat16)
            out[depth:, : row.shape[1]] = jnp.broadcast_to(row, (below, row.shape[1]))


def join_kernel(depth, first, *refs):
    blocks, second, out = refs[:-2], refs[-2], refs[-1]
    tile = out.shape[0] - depth * len(blocks)
    count = LANES
    for step, block in enumerate(blocks):
        out[step * depth : (step + 1) * depth, :] = block[:depth, :]
    row = lax.broadcasted_iota(jnp.int32, (tile, count), 0)

    def spread_row(ref):
        if ref.shape[0] == 1:
            return jnp.broadcast_to(ref[...].astype(jnp.float32), (tile, count))
        return ref[depth:, :count].astype(jnp.float32)

    both = jnp.where(row == 0, spread_row(first), spread_row(second)).astype(out.dtype)
    out[depth * len(blocks) :, :] = jnp.zeros((tile, out.shape[1]), out.dtype)
    out[depth * len(blocks) :, :count] = both


def split_kernel(value, left, right):
    left[...] = value[:, : left.shape[1]]
    right[...] = value[:, left.shape[1] :]


def places_kernel(cap, mine, order, came, mate, twist, doc_starts, freqs, *refs):
    outs, scratch = refs[-11:-6], refs[-6:]
    angles, key_hot, query_bar, slots, columns = outs
    coded, starts, local, owners, landed, semaphore = scratch
    shards, rows = owners.shape
    sources = refs[:-11]
    tile = landed.shape[1]
    copies = []
    for at, source in enumerate(sources):
        bottom = source.at[source.shape[0] - tile :, :rows]
        copies.append(pltpu.make_async_copy(bottom, landed.at[at], semaphore.at[at]))
        copies[-1].start()
    for copy in copies:
        copy.wait()
    each = shards // len(sources)
    for source in range(shards):
        value = landed[source // each].astype(jnp.float32).astype(jnp.int32)
        owners[pl.ds(came[source], 1), :] = value[source % each : source % each + 1, :]
    groups = mine.shape[0]
    team = shards // groups
    span = groups * cap
    owner_at = lax.broadcasted_iota(jnp.int32, (shards, rows), 0)
    upper = jnp.where(
        lax.broadcasted_iota(jnp.int32, (rows, rows), 0)
        < lax.broadcasted_iota(jnp.int32, (rows, rows), 1),
        1.0,
        0.0,
    ).astype(jnp.bfloat16)
    rank_at = lax.broadcasted_iota(jnp.int32, (rows, rows), 0).astype(jnp.float32)
    lane = lax.broadcasted_iota(jnp.int32, (1, rows), 1).astype(jnp.float32)
    before = jnp.zeros((shards, 1), jnp.float32)
    found = jnp.zeros((3 * shards, rows), jnp.float32)
    for shard in range(shards):
        hot = jnp.where(owners[shard : shard + 1, :] == owner_at, 1.0, 0.0)
        within = dot(hot.astype(jnp.bfloat16), upper)
        local[shard : shard + 1, :] = jnp.sum(hot * within, axis=0, keepdims=True)
        rank = jnp.sum(hot * (within + before), axis=0, keepdims=True)
        before = before + jnp.sum(hot, axis=1, keepdims=True)
        rank_hot = jnp.where(rank_at == rank, 1.0, 0.0).astype(jnp.bfloat16)
        codes = jnp.concatenate([hot * float(shard), hot * lane, hot * within], axis=0)
        found = found + dot_rows(codes.astype(jnp.bfloat16), rank_hot)
    shard_of = found[:shards]
    place = shard_of * rows + found[shards : 2 * shards]
    docs = doc_starts.shape[0]
    doc_lane = lax.broadcasted_iota(jnp.int32, (1, LANES), 1)
    doc_row = jnp.full((1, LANES), -1.0, jnp.float32)
    start = jnp.zeros_like(place)
    for doc in range(docs):
        value = doc_starts[doc].astype(jnp.float32)
        start = jnp.maximum(start, jnp.where(value <= place, value, 0.0))
        doc_row = jnp.where(doc_lane == doc, value, doc_row)
    to_shard = shard_of.astype(jnp.int32)
    to_group = jnp.zeros_like(to_shard)
    for group in range(1, groups):
        to_group = jnp.where(to_shard >= group * team, group, to_group)
    to_mate = (to_shard - to_group * team) ^ twist[0]
    inside = found[2 * shards :].astype(jnp.int32)
    coded[...] = (to_mate * groups + to_group) * span + inside
    starts[:shards, :] = start
    starts[shards : 2 * shards, :] = place - start
    flat = jnp.transpose(starts[...])
    which = lax.broadcasted_iota(jnp.int32, flat.shape, 1)
    column = lax.broadcasted_iota(jnp.int32, (rows, 1), 0)
    for group in range(groups):
        own = slice(group * rows, (group + 1) * rows)
        at = mine[group]
        offset = jnp.sum(jnp.where(which == at + shards, flat, 0.0), axis=1, keepdims=True)
        angles[own, :] = offset * freqs[...]
        slots[:, own] = coded[pl.ds(at, 1), :] + group * cap
        shard = group * team + mate[0]
        place = column + shard * rows
        begin = jnp.zeros_like(column)
        for doc in range(docs):
            begin = jnp.where(doc_starts[doc] <= place, doc_starts[doc], begin)
        query_bar[own, :] = jnp.where(begin.astype(jnp.float32) == doc_row, 0.0, OTHER).astype(
            jnp.bfloat16
        )
        owner = owners[pl.ds(shard, 1), :]
        owner_group = jnp.zeros_like(owner)
        for step in range(1, groups):
            owner_group = jnp.where(owner >= step * team, step, owner_group)
        owner_mate = (owner - owner_group * team) ^ twist[0]
        rank = local[pl.ds(shard, 1), :].astype(jnp.int32)
        columns[group : group + 1, :] = owner_mate * span + owner_group * cap + rank
    for block in range(shards):
        own = slice(block * rows, (block + 1) * rows)
        begin = jnp.sum(jnp.where(which == order[block], flat, 0.0), axis=1, keepdims=True)
        key_hot[own, :] = jnp.where(begin == doc_row, 1.0, 0.0).astype(jnp.bfloat16)


def rotate(raw, cosine, sine):
    return raw * cosine + pltpu.roll(raw, HEAD_SIZE // 2, 1) * sine


def project(tokens, weights, cols=slice(None)):
    total = None
    start = 0
    for weight in weights:
        depth = weight.shape[0] // LANES * LANES
        part = dot(tokens[:, start : start + depth], weight[:depth, cols])
        total = part if total is None else total + part
        start += depth
    return total


def tokens_kernel(layout, places, table, *refs):
    row_blocks, col_chunks, blocks = layout
    count = row_blocks * col_chunks
    pieces, weights = refs[:count], refs[count:-4]
    total, later, tokens, loose = refs[-4:]
    rows, width = pieces[0].shape
    for row in range(row_blocks):
        there = pl.ds(pl.multiple_of(places[row] * rows, rows), rows)
        for col in range(col_chunks):
            loose[there, col * width : (col + 1) * width] = pieces[row * col_chunks + col][...]
    width = loose.shape[1] // blocks
    for block in range(blocks):
        source = pl.ds(pl.multiple_of(table[block] * width, width), width)
        tokens[:, block * width : (block + 1) * width] = loose[:, source]
    if later.shape[1] < tokens.shape[1]:
        later[...] = tokens[:, tokens.shape[1] - later.shape[1] :]
    total[...] = project(tokens, weights, slice(0, total.shape[1]))


def rest_kernel(tokens, *refs):
    weights, total = refs[:-1], refs[-1]
    skip = weights[0].shape[1] - total.shape[1]
    for start in range(0, total.shape[1], 2 * HEAD_SIZE):
        cols = slice(skip + start, skip + start + 2 * HEAD_SIZE)
        total[:, start : start + 2 * HEAD_SIZE] = project(tokens, weights, cols)


def finish_projection(total, later, weights, cols):
    if not weights:
        return total[:, cols]
    return total[:, cols] + project(later, weights, cols)


def kv_kernel(total, later, *refs):
    weights = refs[:-3]
    cosine, sine, kv = refs[-3:]
    raw = finish_projection(total, later, weights, slice(0, 2 * HEAD_SIZE))
    kv[:, :HEAD_SIZE] = rotate(raw[:, :HEAD_SIZE], cosine[...], sine[...]).astype(kv.dtype)
    kv[:, HEAD_SIZE:] = raw[:, HEAD_SIZE:].astype(kv.dtype)


def query_kernel(layout, total, later, *refs):
    parts, start = layout
    weights = refs[:parts]
    cosine, sine, slots = refs[parts : parts + 3]
    outs, queries = refs[parts + 3 : -1], refs[-1]
    raw = finish_projection(total, later, weights, slice(start, start + queries.shape[1]))
    for head in range(queries.shape[1] // HEAD_SIZE):
        cols = slice(head * HEAD_SIZE, (head + 1) * HEAD_SIZE)
        queries[:, cols] = rotate(raw[:, cols], cosine[...], sine[...]).astype(queries.dtype)
    count = outs[0].shape[0]
    at = lax.broadcasted_iota(jnp.int32, (count, queries.shape[0]), 0)
    for step, out in enumerate(outs):
        hot = jnp.where(at + step * count == slots[...], 1.0, 0.0).astype(jnp.bfloat16)
        out[...] = dot(hot, queries[...]).astype(out.dtype)


def attention_kernel(layout, far, columns, query_bar, key_hot, *refs):
    query_parts, kv_parts, block_rows = layout
    arrived = refs[:query_parts]
    kvs = refs[query_parts : query_parts + kv_parts]
    outs = refs[query_parts + kv_parts : -5]
    keys, values, long, scores, context = refs[-5:]
    groups, rows = columns.shape
    heads = arrived[0].shape[1] // HEAD_SIZE
    start = 0
    for kv in kvs:
        own = slice(start, start + kv.shape[0])
        keys[own, :HEAD_SIZE] = kv[:, :HEAD_SIZE]
        values[own, :] = kv[:, HEAD_SIZE:]
        start += kv.shape[0]
    keys[:, HEAD_SIZE:] = key_hot[...]
    span = arrived[0].shape[0] // groups
    at = lax.broadcasted_iota(jnp.int32, (span * query_parts, rows), 0)
    for group in range(groups):
        hot = jnp.where(at == columns[group : group + 1, :], 1.0, 0.0).astype(jnp.bfloat16)
        there = slice(group * span, (group + 1) * span)
        slab = jnp.concatenate([part[there, :] for part in arrived], axis=0)
        picked = lax.dot_general(
            hot, slab, (((0,), (0,)), ((), ())), preferred_element_type=jnp.float32
        ).astype(jnp.bfloat16)
        own = slice(group * rows, (group + 1) * rows)
        for head in range(heads):
            long[head, own, :HEAD_SIZE] = picked[:, head * HEAD_SIZE : (head + 1) * HEAD_SIZE]
            long[head, own, HEAD_SIZE:] = query_bar[own, :]
    factor = 1.4426950408889634 / HEAD_SIZE**0.5
    blocks = groups * rows // block_rows
    steps = [(block, head) for block in range(blocks) for head in range(heads)]

    def score(step):
        block, head = steps[step]
        own = slice(block * block_rows, (block + 1) * block_rows)
        scores[step % 2] = dot_rows(long[head, own, :], keys[...])

    score(0)
    for step, (block, head) in enumerate(steps):
        if step + 1 < len(steps):
            score(step + 1)
        own = slice(block * block_rows, (block + 1) * block_rows)
        held = scores[step % 2]
        top = jnp.max(held, axis=1, keepdims=True)
        kept = jnp.exp2((held - top) * factor)
        total = jnp.sum(kept, axis=1, keepdims=True)
        mixed = dot(kept.astype(jnp.bfloat16), values[...])
        context[own, head * HEAD_SIZE : (head + 1) * HEAD_SIZE] = (mixed / total).astype(
            context.dtype
        )
    for step, out in enumerate(outs):
        out[...] = context[pl.ds(pl.multiple_of(far[step] * rows, rows), rows), :]


def finish_kernel(far, *refs):
    out = refs[-1]
    groups = far.shape[0]
    parts = (len(refs) - 1) // groups
    width = refs[0].shape[1]
    for part in range(parts):
        for step in range(groups):
            start = pl.multiple_of((far[step] * parts + part) * width, width)
            out[:, pl.ds(start, width)] = refs[part * groups + step][...]


def turn(value, axis, bits):
    count = lax.axis_size(axis)
    return lax.ppermute(value, axis, [(i, i ^ bits) for i in range(count)])


def after(value, *others):
    return lax.optimization_barrier((value, *others))[0]


def spread(value, *others):
    across = turn(value, "team", 2)
    last = turn(after(across, *others), "team", 1)
    return [value, across, turn(value, "team", 1), last]


def body(stored, source_owner, doc_ids, doc_starts, wq, wk, wv):
    groups, team = lax.axis_size("line"), lax.axis_size("team")
    nctx, ntp = groups * team, lax.axis_size("tp")
    group, mate = lax.axis_index("line"), lax.axis_index("team")
    rows = stored.shape[0]
    cap = 2 * rows // nctx
    size = HEAD_SIZE
    depth = wq.shape[0]
    split = groups > 1
    pair = 2 * size
    parts = wq.shape[1] // groups // pair
    total_rows = groups * rows
    width = stored.shape[1] * ntp
    keys = nctx * rows
    far = group ^ jnp.arange(groups, dtype=jnp.int32)

    def flip(value):
        return lax.ppermute(value, "tp", [(0, 1), (1, 0)])

    columns_each = (1 + parts) * pair
    tile = 16
    slabs = call(
        weights_kernel,
        [
            jax.ShapeDtypeStruct((depth + tile * (step % 2), columns_each), jnp.bfloat16)
            for step in range(groups)
        ],
        [far, source_owner[None, :], wq, wk, wv],
        smem=(0,),
    )

    if split:
        def join(first, blocks, second):
            shape = (depth * len(blocks) + tile, columns_each)
            return call(
                functools.partial(join_kernel, depth),
                jax.ShapeDtypeStruct(shape, jnp.bfloat16),
                [first, *blocks, second],
            )

        inner, outer = [(1, 2), (2, 1)], [(1, 0), (2, 3)]
        near = turn(stored, "line", 1)
        over = lax.ppermute(stored, "line", inner)
        flips = [flip(stored)]
        weights_near = turn(slabs[1], "line", 1)
        weights_third = turn(slabs[3], "line", 3)
        over_near = lax.ppermute(after(near, over, flips[0], *slabs), "line", inner)
        end = lax.ppermute(after(over, near, weights_near), "line", outer)
        flips.append(flip(after(near, flips[0], weights_third)))
        held = join(source_owner[None, :], [slabs[0], weights_near], weights_near)
        second_owner = turn(after(source_owner, weights_near), "line", 2)[None, :]
        first = spread(held)
        edge = (group == 0) | (group == groups - 1)
        third = jnp.where(edge, end, over)
        end_near = lax.ppermute(after(over_near, flips[1]), "line", outer)
        flips.append(flip(after(third, flips[1], second_owner)))
        weights_second = turn(after(slabs[2], over_near, end, first[1]), "line", 2)
        fourth = jnp.where(edge, end_near, over_near)
        flips.append(flip(after(fourth, flips[2])))
        third_held = join(weights_third, [weights_third], second_owner)
        second = spread(after(third_held, flips[2], first[1]))
        kv_second, query_second = call(
            split_kernel,
            [
                jax.ShapeDtypeStruct((depth, pair), jnp.bfloat16),
                jax.ShapeDtypeStruct((depth, parts * pair), jnp.bfloat16),
            ],
            [after(weights_second, flips[3], second[1])],
        )
        early = [part for both in zip(first, second) for part in both]
        places = jnp.stack(
            [group, group ^ 1, group ^ jnp.where(edge, 2, 3), group ^ jnp.where(edge, 3, 2)]
        )
        pieces = [
            chunk for both in zip((stored, near, third, fourth), flips) for chunk in both
        ]
        chunks = ntp
        owners = early
    else:
        pieces = [lax.all_gather(stored, "tp", axis=1, tiled=True)]
        places = jnp.zeros((1,), jnp.int32)
        chunks = 1
        early = [lax.all_gather(slabs[0], "team", axis=0, tiled=True)]
        owners = [lax.all_gather(source_owner, "team", axis=0)]

    if split:
        rel = jnp.arange(groups, dtype=jnp.int32)
        turns = mate ^ jnp.array([0, 2, 1, 3], dtype=jnp.int32)
        order = (rel[None, :] * team + turns[:, None]).reshape(-1)
        came = (far[jnp.array([0, 1, 3, 2])][None, :] * team + turns[:, None]).reshape(-1)
        rows_of = jnp.concatenate(
            [came.reshape(team, groups)[:, :3].reshape(-1), came.reshape(team, groups)[:, 3]]
        )
        mine = rel * team + mate
        twist = mate[None]
        share = nctx // ntp
        table = rows_of % share + jnp.where(rows_of // share == lax.axis_index("tp"), 0, share)
    else:
        order = came = jnp.arange(nctx, dtype=jnp.int32)
        mine = mate[None]
        twist = table = jnp.zeros((1,), jnp.int32)

    freqs = ROPE_BASE ** (-np.arange(size // 2) * 2.0 / size)
    freqs = jnp.asarray(np.concatenate([freqs, freqs])[None, :], jnp.float32)
    sign = jnp.asarray(np.repeat([-1.0, 1.0], size // 2)[None, :], jnp.float32)
    angles, key_hot, query_bar, slots, columns = call(
        functools.partial(places_kernel, cap),
        [
            jax.ShapeDtypeStruct((total_rows, size), jnp.float32),
            jax.ShapeDtypeStruct((keys, LANES), jnp.bfloat16),
            jax.ShapeDtypeStruct((total_rows, LANES), jnp.bfloat16),
            jax.ShapeDtypeStruct((1, total_rows), jnp.int32),
            jax.ShapeDtypeStruct((groups, rows), jnp.int32),
        ],
        [mine, order, came, mate[None], twist, doc_starts, freqs, *owners],
        scratch=[
            pltpu.VMEM((nctx, rows), jnp.int32),
            pltpu.VMEM((max(2 * nctx, LANES), rows), jnp.float32),
            pltpu.VMEM((nctx, rows), jnp.float32),
            pltpu.VMEM((nctx, rows), jnp.int32),
            pltpu.VMEM((len(owners), tile if split else nctx, rows), owners[0].dtype),
            pltpu.SemaphoreType.DMA((len(owners),)),
        ],
        flops=10**9,
        smem=(0, 1, 2, 3, 4, 5),
        anywhere=range(7, 7 + len(owners)),
    )
    cosine = jnp.cos(angles)
    sine = jnp.sin(angles) * sign

    rest = width // groups if split else width
    kv_total, later, tokens = call(
        functools.partial(tokens_kernel, (groups, chunks, nctx if split else 1)),
        [
            jax.ShapeDtypeStruct((total_rows, pair), jnp.float32),
            jax.ShapeDtypeStruct((total_rows, rest if split else LANES), jnp.bfloat16),
            jax.ShapeDtypeStruct((total_rows, width), jnp.bfloat16),
        ],
        [places, table, *pieces, *early],
        scratch=[pltpu.VMEM((total_rows, width), jnp.bfloat16)],
        flops=2 * total_rows * width * columns_each,
        smem=(0, 1),
        vmem=32,
    )
    kv_late = spread(kv_second, kv_total, cosine) if split else []
    kv = call(
        kv_kernel,
        jax.ShapeDtypeStruct((total_rows, pair), jnp.bfloat16),
        [kv_total, later, *kv_late, cosine, sine],
        flops=2 * total_rows * rest * pair,
    )
    total = call(
        rest_kernel,
        jax.ShapeDtypeStruct((total_rows, parts * pair), jnp.float32),
        [after(tokens, kv), *early],
        flops=2 * total_rows * width * parts * pair,
    )
    late = spread(query_second, kv) if split else []

    block_rows = min(2 * rows, total_rows)
    lanes_out = team if split else 1
    slot_count = nctx * groups * cap

    def project_part(part):
        return call(
            functools.partial(query_kernel, (len(late), part * pair)),
            [jax.ShapeDtypeStruct((slot_count // lanes_out, pair), jnp.bfloat16)] * lanes_out,
            [total, later, *late, cosine, sine, slots],
            scratch=[pltpu.VMEM((total_rows, pair), jnp.bfloat16)],
            flops=2 * total_rows * (rest + slot_count) * pair,
        )

    def attend(arrived):
        context = call(
            functools.partial(attention_kernel, (len(arrived), len(kvs), block_rows)),
            [jax.ShapeDtypeStruct((rows, pair), jnp.bfloat16)] * groups,
            [far, columns, query_bar, key_hot, *arrived, *kvs],
            scratch=[
                pltpu.VMEM((keys, size + LANES), jnp.bfloat16),
                pltpu.VMEM((keys, size), jnp.bfloat16),
                pltpu.VMEM((pair // size, total_rows, size + LANES), jnp.bfloat16),
                pltpu.VMEM((2, block_rows, keys), jnp.float32),
                pltpu.VMEM((total_rows, pair), jnp.bfloat16),
            ],
            flops=8 * total_rows * pair * keys,
            smem=(0,),
            vmem=40,
        )
        return [context[0]] + [turn(context[step], "line", step) for step in range(1, groups)]

    def exchange(leaving):
        if split:
            return [leaving[0]] + [turn(leaving[e], "team", e) for e in range(1, team)]
        return [lax.all_to_all(leaving[0], "team", 0, 0, tiled=True)]

    leaving = [project_part(part) for part in range(parts)]
    arrived = [exchange(part) for part in leaving]
    if split:
        across = turn(kv, "team", 2)
        kvs = [kv, across] + [
            turn(after(part, *arrived[-1], leaving[0][0]), "team", 1) for part in (kv, across)
        ]
    else:
        kvs = [lax.all_gather(kv, "team", axis=0, tiled=True)]
    ready = [piece for queries in arrived for piece in attend(queries)]

    return call(
        finish_kernel,
        jax.ShapeDtypeStruct((rows, wq.shape[1]), jnp.bfloat16),
        [far, *ready],
        smem=(0,),
    )


def solution(mesh):
    def program(stored, source_owner, doc_ids, doc_starts, wq, wk, wv):
        ctx, tp = mesh.shape["ctx"], mesh.shape["tp"]
        groups = wk.shape[1] // HEAD_SIZE // tp
        parts = jax.sharding.Mesh(
            mesh.devices.reshape(groups, ctx // groups, tp), ("line", "team", "tp")
        )
        both = ("line", "team")
        return jax.shard_map(
            body,
            mesh=parts,
            in_specs=(
                P(both, "tp"),
                P(both),
                P(both),
                P(),
                P(both, "tp"),
                P(both, "tp"),
                P(both, "tp"),
            ),
            out_specs=P(both, "tp"),
            check_vma=False,
        )(stored, source_owner, doc_ids, doc_starts, wq, wk, wv)

    return program
```

```python
import functools

import jax
import jax.numpy as jnp
import numpy as np
from jax import lax
from jax.experimental import pallas as pl
from jax.experimental.pallas import tpu as pltpu
from jax.sharding import PartitionSpec as P

HEAD_SIZE = 128
LANES = 128
ROPE_BASE = 500000.0
OTHER = -(2.0**100)

VMEM_SPEC = pl.BlockSpec(memory_space=pltpu.VMEM)
SMEM_SPEC = pl.BlockSpec(memory_space=pltpu.SMEM)
ANY_SPEC = pl.BlockSpec(memory_space=pl.ANY)


def dot(a, b):
    return jnp.dot(a, b, preferred_element_type=jnp.float32)


def dot_rows(a, b):
    return lax.dot_general(
        a, b, (((1,), (1,)), ((), ())), preferred_element_type=jnp.float32
    )


def call(kernel, out_shape, operands, scratch=(), flops=0, smem=(), anywhere=(), vmem=24):
    specs = [
        SMEM_SPEC if at in smem else ANY_SPEC if at in anywhere else VMEM_SPEC
        for at in range(len(operands))
    ]
    many = isinstance(out_shape, (list, tuple))
    outs = out_shape if many else [out_shape]
    moved = sum(x.size * x.dtype.itemsize for x in [*operands, *outs])
    return pl.pallas_call(
        kernel,
        out_shape=out_shape,
        in_specs=specs,
        out_specs=[VMEM_SPEC] * len(out_shape) if many else VMEM_SPEC,
        scratch_shapes=list(scratch),
        compiler_params=pltpu.CompilerParams(vmem_limit_bytes=vmem * 2**20),
        cost_estimate=pl.CostEstimate(flops=flops, bytes_accessed=moved, transcendentals=0),
    )(*operands)


def weights_kernel(far, owner, wq, wk, wv, *outs):
    depth = wq.shape[0]
    for step, out in enumerate(outs):
        start = pl.multiple_of(far[step] * HEAD_SIZE, HEAD_SIZE)
        width = out.shape[1] - 2 * HEAD_SIZE
        out[:depth, :HEAD_SIZE] = wk[:, pl.ds(start, HEAD_SIZE)]
        out[:depth, HEAD_SIZE : 2 * HEAD_SIZE] = wv[:, pl.ds(start, HEAD_SIZE)]
        start = pl.multiple_of(far[step] * width, width)
        out[:depth, 2 * HEAD_SIZE :] = wq[:, pl.ds(start, width)]
        below = out.shape[0] - depth
        if below:
            row = owner[...].astype(jnp.float32).astype(jnp.bfloat16)
            out[depth:, :] = jnp.zeros((below, out.shape[1]), jnp.bfloat16)
            out[depth:, : row.shape[1]] = jnp.broadcast_to(row, (below, row.shape[1]))


def join_kernel(depth, first, *refs):
    blocks, second, out = refs[:-2], refs[-2], refs[-1]
    tile = out.shape[0] - depth * len(blocks)
    count = LANES
    for step, block in enumerate(blocks):
        out[step * depth : (step + 1) * depth, :] = block[:depth, :]
    row = lax.broadcasted_iota(jnp.int32, (tile, count), 0)

    def spread_row(ref):
        if ref.shape[0] == 1:
            return jnp.broadcast_to(ref[...].astype(jnp.float32), (tile, count))
        return ref[depth:, :count].astype(jnp.float32)

    both = jnp.where(row == 0, spread_row(first), spread_row(second)).astype(out.dtype)
    out[depth * len(blocks) :, :] = jnp.zeros((tile, out.shape[1]), out.dtype)
    out[depth * len(blocks) :, :count] = both


def split_kernel(value, left, right):
    left[...] = value[:, : left.shape[1]]
    right[...] = value[:, left.shape[1] :]


def places_kernel(cap, mine, order, came, mate, twist, doc_starts, freqs, *refs):
    outs, scratch = refs[-11:-6], refs[-6:]
    angles, key_hot, query_bar, slots, columns = outs
    coded, starts, local, owners, landed, semaphore = scratch
    shards, rows = owners.shape
    sources = refs[:-11]
    tile = landed.shape[1]
    copies = []
    for at, source in enumerate(sources):
        bottom = source.at[source.shape[0] - tile :, :rows]
        copies.append(pltpu.make_async_copy(bottom, landed.at[at], semaphore.at[at]))
        copies[-1].start()
    for copy in copies:
        copy.wait()
    each = shards // len(sources)
    for source in range(shards):
        value = landed[source // each].astype(jnp.float32).astype(jnp.int32)
        owners[pl.ds(came[source], 1), :] = value[source % each : source % each + 1, :]
    groups = mine.shape[0]
    team = shards // groups
    span = groups * cap
    owner_at = lax.broadcasted_iota(jnp.int32, (shards, rows), 0)
    upper = jnp.where(
        lax.broadcasted_iota(jnp.int32, (rows, rows), 0)
        < lax.broadcasted_iota(jnp.int32, (rows, rows), 1),
        1.0,
        0.0,
    ).astype(jnp.bfloat16)
    rank_at = lax.broadcasted_iota(jnp.int32, (rows, rows), 0).astype(jnp.float32)
    lane = lax.broadcasted_iota(jnp.int32, (1, rows), 1).astype(jnp.float32)
    before = jnp.zeros((shards, 1), jnp.float32)
    found = jnp.zeros((3 * shards, rows), jnp.float32)
    for shard in range(shards):
        hot = jnp.where(owners[shard : shard + 1, :] == owner_at, 1.0, 0.0)
        within = dot(hot.astype(jnp.bfloat16), upper)
        local[shard : shard + 1, :] = jnp.sum(hot * within, axis=0, keepdims=True)
        rank = jnp.sum(hot * (within + before), axis=0, keepdims=True)
        before = before + jnp.sum(hot, axis=1, keepdims=True)
        rank_hot = jnp.where(rank_at == rank, 1.0, 0.0).astype(jnp.bfloat16)
        codes = jnp.concatenate([hot * float(shard), hot * lane, hot * within], axis=0)
        found = found + dot_rows(codes.astype(jnp.bfloat16), rank_hot)
    shard_of = found[:shards]
    place = shard_of * rows + found[shards : 2 * shards]
    docs = doc_starts.shape[0]
    doc_lane = lax.broadcasted_iota(jnp.int32, (1, LANES), 1)
    doc_row = jnp.full((1, LANES), -1.0, jnp.float32)
    start = jnp.zeros_like(place)
    for doc in range(docs):
        value = doc_starts[doc].astype(jnp.float32)
        start = jnp.maximum(start, jnp.where(value <= place, value, 0.0))
        doc_row = jnp.where(doc_lane == doc, value, doc_row)
    to_shard = shard_of.astype(jnp.int32)
    to_group = jnp.zeros_like(to_shard)
    for group in range(1, groups):
        to_group = jnp.where(to_shard >= group * team, group, to_group)
    to_mate = (to_shard - to_group * team) ^ twist[0]
    inside = found[2 * shards :].astype(jnp.int32)
    coded[...] = (to_mate * groups + to_group) * span + inside
    starts[:shards, :] = start
    starts[shards : 2 * shards, :] = place - start
    flat = jnp.transpose(starts[...])
    which = lax.broadcasted_iota(jnp.int32, flat.shape, 1)
    column = lax.broadcasted_iota(jnp.int32, (rows, 1), 0)
    for group in range(groups):
        own = slice(group * rows, (group + 1) * rows)
        at = mine[group]
        offset = jnp.sum(jnp.where(which == at + shards, flat, 0.0), axis=1, keepdims=True)
        angles[own, :] = offset * freqs[...]
        slots[:, own] = coded[pl.ds(at, 1), :] + group * cap
        shard = group * team + mate[0]
        place = column + shard * rows
        begin = jnp.zeros_like(column)
        for doc in range(docs):
            begin = jnp.where(doc_starts[doc] <= place, doc_starts[doc], begin)
        query_bar[own, :] = jnp.where(begin.astype(jnp.float32) == doc_row, 0.0, OTHER).astype(
            jnp.bfloat16
        )
        owner = owners[pl.ds(shard, 1), :]
        owner_group = jnp.zeros_like(owner)
        for step in range(1, groups):
            owner_group = jnp.where(owner >= step * team, step, owner_group)
        owner_mate = (owner - owner_group * team) ^ twist[0]
        rank = local[pl.ds(shard, 1), :].astype(jnp.int32)
        columns[group : group + 1, :] = owner_mate * span + owner_group * cap + rank
    for block in range(shards):
        own = slice(block * rows, (block + 1) * rows)
        begin = jnp.sum(jnp.where(which == order[block], flat, 0.0), axis=1, keepdims=True)
        key_hot[own, :] = jnp.where(begin == doc_row, 1.0, 0.0).astype(jnp.bfloat16)


def rotate(raw, cosine, sine):
    return raw * cosine + pltpu.roll(raw, HEAD_SIZE // 2, 1) * sine


def project(tokens, weights, cols=slice(None)):
    total = None
    start = 0
    for weight in weights:
        depth = weight.shape[0] // LANES * LANES
        part = dot(tokens[:, start : start + depth], weight[:depth, cols])
        total = part if total is None else total + part
        start += depth
    return total


def tokens_kernel(layout, places, table, *refs):
    row_blocks, col_chunks, blocks = layout
    count = row_blocks * col_chunks
    pieces, weights = refs[:count], refs[count:-4]
    total, later, tokens, loose = refs[-4:]
    rows, width = pieces[0].shape
    for row in range(row_blocks):
        there = pl.ds(pl.multiple_of(places[row] * rows, rows), rows)
        for col in range(col_chunks):
            loose[there, col * width : (col + 1) * width] = pieces[row * col_chunks + col][...]
    width = loose.shape[1] // blocks
    for block in range(blocks):
        source = pl.ds(pl.multiple_of(table[block] * width, width), width)
        tokens[:, block * width : (block + 1) * width] = loose[:, source]
    if later.shape[1] < tokens.shape[1]:
        later[...] = tokens[:, tokens.shape[1] - later.shape[1] :]
    for start in range(0, total.shape[1], 2 * HEAD_SIZE):
        cols = slice(start, start + 2 * HEAD_SIZE)
        total[:, cols] = project(tokens, weights, cols)


def finish_projection(total, later, weights, cols, skip=0):
    if not weights:
        return total[:, cols]
    return total[:, cols] + project(later, weights, slice(cols.start - skip, cols.stop - skip))


def kv_kernel(total, later, *refs):
    weights = refs[:-3]
    cosine, sine, kv = refs[-3:]
    raw = finish_projection(total, later, weights, slice(0, 2 * HEAD_SIZE))
    kv[:, :HEAD_SIZE] = rotate(raw[:, :HEAD_SIZE], cosine[...], sine[...]).astype(kv.dtype)
    kv[:, HEAD_SIZE:] = raw[:, HEAD_SIZE:].astype(kv.dtype)


def query_kernel(layout, total, later, *refs):
    parts, start = layout
    weights = refs[:parts]
    cosine, sine, slots = refs[parts : parts + 3]
    outs, queries = refs[parts + 3 : -1], refs[-1]
    cols = slice(start, start + queries.shape[1])
    raw = finish_projection(total, later, weights, cols, 2 * HEAD_SIZE)
    for head in range(queries.shape[1] // HEAD_SIZE):
        cols = slice(head * HEAD_SIZE, (head + 1) * HEAD_SIZE)
        queries[:, cols] = rotate(raw[:, cols], cosine[...], sine[...]).astype(queries.dtype)
    count = outs[0].shape[0]
    at = lax.broadcasted_iota(jnp.int32, (count, queries.shape[0]), 0)
    for step, out in enumerate(outs):
        hot = jnp.where(at + step * count == slots[...], 1.0, 0.0).astype(jnp.bfloat16)
        out[...] = dot(hot, queries[...]).astype(out.dtype)


def attention_kernel(layout, far, columns, query_bar, key_hot, *refs):
    query_parts, kv_parts, block_rows = layout
    arrived = refs[:query_parts]
    kvs = refs[query_parts : query_parts + kv_parts]
    outs = refs[query_parts + kv_parts : -5]
    keys, values, long, scores, context = refs[-5:]
    groups, rows = columns.shape
    heads = arrived[0].shape[1] // HEAD_SIZE
    start = 0
    for kv in kvs:
        own = slice(start, start + kv.shape[0])
        keys[own, :HEAD_SIZE] = kv[:, :HEAD_SIZE]
        values[own, :HEAD_SIZE] = kv[:, HEAD_SIZE:]
        start += kv.shape[0]
    keys[:, HEAD_SIZE:] = key_hot[...]
    values[:, HEAD_SIZE:] = jnp.ones_like(key_hot)
    span = arrived[0].shape[0] // groups
    at = lax.broadcasted_iota(jnp.int32, (span * query_parts, rows), 0)
    for group in range(groups):
        hot = jnp.where(at == columns[group : group + 1, :], 1.0, 0.0).astype(jnp.bfloat16)
        there = slice(group * span, (group + 1) * span)
        slab = jnp.concatenate([part[there, :] for part in arrived], axis=0)
        picked = lax.dot_general(
            hot, slab, (((0,), (0,)), ((), ())), preferred_element_type=jnp.float32
        ).astype(jnp.bfloat16)
        own = slice(group * rows, (group + 1) * rows)
        for head in range(heads):
            long[head, own, :HEAD_SIZE] = picked[:, head * HEAD_SIZE : (head + 1) * HEAD_SIZE]
            long[head, own, HEAD_SIZE:] = query_bar[own, :]
    factor = 1.4426950408889634 / HEAD_SIZE**0.5
    blocks = groups * rows // block_rows
    steps = [(block, head) for block in range(blocks) for head in range(heads)]

    def score(step):
        block, head = steps[step]
        own = slice(block * block_rows, (block + 1) * block_rows)
        scores[step % 2] = dot_rows(long[head, own, :], keys[...])

    score(0)
    for step, (block, head) in enumerate(steps):
        if step + 1 < len(steps):
            score(step + 1)
        own = slice(block * block_rows, (block + 1) * block_rows)
        held = scores[step % 2]
        top = jnp.max(held, axis=1, keepdims=True)
        kept = jnp.exp2((held - top) * factor)
        both = dot(kept.astype(jnp.bfloat16), values[...])
        mixed, total = both[:, :HEAD_SIZE], both[:, HEAD_SIZE : HEAD_SIZE + 1]
        context[own, head * HEAD_SIZE : (head + 1) * HEAD_SIZE] = (mixed / total).astype(
            context.dtype
        )
    for step, out in enumerate(outs):
        out[...] = context[pl.ds(pl.multiple_of(far[step] * rows, rows), rows), :]


def finish_kernel(far, *refs):
    out = refs[-1]
    groups = far.shape[0]
    parts = (len(refs) - 1) // groups
    width = refs[0].shape[1]
    for part in range(parts):
        for step in range(groups):
            start = pl.multiple_of((far[step] * parts + part) * width, width)
            out[:, pl.ds(start, width)] = refs[part * groups + step][...]


def turn(value, axis, bits):
    count = lax.axis_size(axis)
    return lax.ppermute(value, axis, [(i, i ^ bits) for i in range(count)])


def after(value, *others):
    return lax.optimization_barrier((value, *others))[0]


def spread(value, *others):
    across = turn(value, "team", 2)
    last = turn(after(across, *others), "team", 1)
    return [value, across, turn(value, "team", 1), last]


def body(stored, source_owner, doc_ids, doc_starts, wq, wk, wv):
    groups, team = lax.axis_size("line"), lax.axis_size("team")
    nctx, ntp = groups * team, lax.axis_size("tp")
    group, mate = lax.axis_index("line"), lax.axis_index("team")
    rows = stored.shape[0]
    cap = 2 * rows // nctx
    size = HEAD_SIZE
    depth = wq.shape[0]
    split = groups > 1
    pair = 2 * size
    parts = wq.shape[1] // groups // pair
    total_rows = groups * rows
    width = stored.shape[1] * ntp
    keys = nctx * rows
    far = group ^ jnp.arange(groups, dtype=jnp.int32)

    def flip(value):
        return lax.ppermute(value, "tp", [(0, 1), (1, 0)])

    columns_each = (1 + parts) * pair
    tile = 16
    slabs = call(
        weights_kernel,
        [
            jax.ShapeDtypeStruct((depth + tile * (step % 2), columns_each), jnp.bfloat16)
            for step in range(groups)
        ],
        [far, source_owner[None, :], wq, wk, wv],
        smem=(0,),
    )

    if split:
        def join(first, blocks, second):
            shape = (depth * len(blocks) + tile, columns_each)
            return call(
                functools.partial(join_kernel, depth),
                jax.ShapeDtypeStruct(shape, jnp.bfloat16),
                [first, *blocks, second],
            )

        inner, outer = [(1, 2), (2, 1)], [(1, 0), (2, 3)]
        near = turn(stored, "line", 1)
        over = lax.ppermute(stored, "line", inner)
        flips = [flip(stored)]
        weights_near = turn(slabs[1], "line", 1)
        weights_third = turn(slabs[3], "line", 3)
        over_near = lax.ppermute(after(near, over, flips[0], *slabs), "line", inner)
        end = lax.ppermute(after(over, near, weights_near), "line", outer)
        flips.append(flip(after(near, flips[0], weights_third)))
        held = join(source_owner[None, :], [slabs[0], weights_near], weights_near)
        second_owner = turn(after(source_owner, weights_near), "line", 2)[None, :]
        first = spread(held)
        edge = (group == 0) | (group == groups - 1)
        third = jnp.where(edge, end, over)
        end_near = lax.ppermute(after(over_near, flips[1]), "line", outer)
        flips.append(flip(after(third, flips[1], second_owner)))
        weights_second = turn(after(slabs[2], over_near, end, first[1]), "line", 2)
        fourth = jnp.where(edge, end_near, over_near)
        flips.append(flip(after(fourth, flips[2])))
        third_held = join(weights_third, [weights_third], second_owner)
        second = spread(after(third_held, flips[2], first[1]))
        kv_second, query_second = call(
            split_kernel,
            [
                jax.ShapeDtypeStruct((depth, pair), jnp.bfloat16),
                jax.ShapeDtypeStruct((depth, parts * pair), jnp.bfloat16),
            ],
            [after(weights_second, flips[3], second[1])],
        )
        early = [part for both in zip(first, second) for part in both]
        places = jnp.stack(
            [group, group ^ 1, group ^ jnp.where(edge, 2, 3), group ^ jnp.where(edge, 3, 2)]
        )
        pieces = [
            chunk for both in zip((stored, near, third, fourth), flips) for chunk in both
        ]
        chunks = ntp
        owners = early
    else:
        pieces = [lax.all_gather(stored, "tp", axis=1, tiled=True)]
        places = jnp.zeros((1,), jnp.int32)
        chunks = 1
        early = [lax.all_gather(slabs[0], "team", axis=0, tiled=True)]
        owners = [lax.all_gather(source_owner, "team", axis=0)]

    if split:
        rel = jnp.arange(groups, dtype=jnp.int32)
        turns = mate ^ jnp.array([0, 2, 1, 3], dtype=jnp.int32)
        order = (rel[None, :] * team + turns[:, None]).reshape(-1)
        came = (far[jnp.array([0, 1, 3, 2])][None, :] * team + turns[:, None]).reshape(-1)
        rows_of = jnp.concatenate(
            [came.reshape(team, groups)[:, :3].reshape(-1), came.reshape(team, groups)[:, 3]]
        )
        mine = rel * team + mate
        twist = mate[None]
        share = nctx // ntp
        table = rows_of % share + jnp.where(rows_of // share == lax.axis_index("tp"), 0, share)
    else:
        order = came = jnp.arange(nctx, dtype=jnp.int32)
        mine = mate[None]
        twist = table = jnp.zeros((1,), jnp.int32)

    freqs = ROPE_BASE ** (-np.arange(size // 2) * 2.0 / size)
    freqs = jnp.asarray(np.concatenate([freqs, freqs])[None, :], jnp.float32)
    sign = jnp.asarray(np.repeat([-1.0, 1.0], size // 2)[None, :], jnp.float32)
    angles, key_hot, query_bar, slots, columns = call(
        functools.partial(places_kernel, cap),
        [
            jax.ShapeDtypeStruct((total_rows, size), jnp.float32),
            jax.ShapeDtypeStruct((keys, LANES), jnp.bfloat16),
            jax.ShapeDtypeStruct((total_rows, LANES), jnp.bfloat16),
            jax.ShapeDtypeStruct((1, total_rows), jnp.int32),
            jax.ShapeDtypeStruct((groups, rows), jnp.int32),
        ],
        [mine, order, came, mate[None], twist, doc_starts, freqs, *owners],
        scratch=[
            pltpu.VMEM((nctx, rows), jnp.int32),
            pltpu.VMEM((max(2 * nctx, LANES), rows), jnp.float32),
            pltpu.VMEM((nctx, rows), jnp.float32),
            pltpu.VMEM((nctx, rows), jnp.int32),
            pltpu.VMEM((len(owners), tile if split else nctx, rows), owners[0].dtype),
            pltpu.SemaphoreType.DMA((len(owners),)),
        ],
        flops=10**9,
        smem=(0, 1, 2, 3, 4, 5),
        anywhere=range(7, 7 + len(owners)),
    )
    cosine = jnp.cos(angles)
    sine = jnp.sin(angles) * sign

    rest = width // groups if split else width
    total, later = call(
        functools.partial(tokens_kernel, (groups, chunks, nctx if split else 1)),
        [
            jax.ShapeDtypeStruct((total_rows, columns_each), jnp.float32),
            jax.ShapeDtypeStruct((total_rows, rest if split else LANES), jnp.bfloat16),
        ],
        [places, table, *pieces, *early],
        scratch=[
            pltpu.VMEM((total_rows, width), jnp.bfloat16),
            pltpu.VMEM((total_rows, width), jnp.bfloat16),
        ],
        flops=2 * total_rows * width * columns_each,
        smem=(0, 1),
        vmem=32,
    )
    kv_late = spread(kv_second, total, cosine) if split else []
    kv = call(
        kv_kernel,
        jax.ShapeDtypeStruct((total_rows, pair), jnp.bfloat16),
        [total, later, *kv_late, cosine, sine],
        flops=2 * total_rows * rest * pair,
    )
    late = spread(query_second, kv) if split else []

    block_rows = min(2 * rows, total_rows)
    lanes_out = team if split else 1
    slot_count = nctx * groups * cap

    def project_part(part):
        return call(
            functools.partial(query_kernel, (len(late), (1 + part) * pair)),
            [jax.ShapeDtypeStruct((slot_count // lanes_out, pair), jnp.bfloat16)] * lanes_out,
            [total, later, *late, cosine, sine, slots],
            scratch=[pltpu.VMEM((total_rows, pair), jnp.bfloat16)],
            flops=2 * total_rows * (rest + slot_count) * pair,
        )

    def attend(arrived):
        context = call(
            functools.partial(attention_kernel, (len(arrived), len(kvs), block_rows)),
            [jax.ShapeDtypeStruct((rows, pair), jnp.bfloat16)] * groups,
            [far, columns, query_bar, key_hot, *arrived, *kvs],
            scratch=[
                pltpu.VMEM((keys, size + LANES), jnp.bfloat16),
                pltpu.VMEM((keys, size + LANES), jnp.bfloat16),
                pltpu.VMEM((pair // size, total_rows, size + LANES), jnp.bfloat16),
                pltpu.VMEM((2, block_rows, keys), jnp.float32),
                pltpu.VMEM((total_rows, pair), jnp.bfloat16),
            ],
            flops=8 * total_rows * pair * keys,
            smem=(0,),
            vmem=40,
        )
        return [context[0]] + [turn(context[step], "line", step) for step in range(1, groups)]

    def exchange(leaving):
        if split:
            return [leaving[0]] + [turn(leaving[e], "team", e) for e in range(1, team)]
        return [lax.all_to_all(leaving[0], "team", 0, 0, tiled=True)]

    leaving = [project_part(part) for part in range(parts)]
    arrived = [exchange(part) for part in leaving]
    if split:
        across = turn(kv, "team", 2)
        kvs = [kv, across] + [
            turn(after(part, *arrived[-1], leaving[0][0]), "team", 1) for part in (kv, across)
        ]
    else:
        kvs = [lax.all_gather(kv, "team", axis=0, tiled=True)]
    ready = [piece for queries in arrived for piece in attend(queries)]

    return call(
        finish_kernel,
        jax.ShapeDtypeStruct((rows, wq.shape[1]), jnp.bfloat16),
        [far, *ready],
        smem=(0,),
    )


def solution(mesh):
    def program(stored, source_owner, doc_ids, doc_starts, wq, wk, wv):
        ctx, tp = mesh.shape["ctx"], mesh.shape["tp"]
        groups = wk.shape[1] // HEAD_SIZE // tp
        parts = jax.sharding.Mesh(
            mesh.devices.reshape(groups, ctx // groups, tp), ("line", "team", "tp")
        )
        both = ("line", "team")
        return jax.shard_map(
            body,
            mesh=parts,
            in_specs=(
                P(both, "tp"),
                P(both),
                P(both),
                P(),
                P(both, "tp"),
                P(both, "tp"),
                P(both, "tp"),
            ),
            out_specs=P(both, "tp"),
            check_vma=False,
        )(stored, source_owner, doc_ids, doc_starts, wq, wk, wv)

    return program
```
